256 devices in a mesh: gy: 16 (over y, z_lo), gz: 16 (over z_hi, x, core).
Axes of the slice: x: 4, y: 4, z: 8 (z_hi: 2, z_lo: 4; z = z_hi * 4 + z_lo), core: 2. Of those that a mesh axis runs over, the one named last changes fastest.
Arguments:
- velocity: float32 [3, 128, 32, 256], P(None, 'gy', 'gz'), may hold values from -6 to 6
- hidden: bfloat16 [32, 128, 32, 256], P(None, 'gy', 'gz'), may hold values from -3 to 3
- cell: float32 [32, 128, 32, 256], P(None, 'gy', 'gz'), may hold values from -6 to 6
- gate_weight: bfloat16 [128, 945], replicated, may hold values from -0.1875 to 0.1875
- gate_bias: float32 [128], replicated, may hold values from -1 to 1
- decoder: bfloat16 [3, 32], replicated, may hold values from -1 to 1
Outputs:
- hidden_next: bfloat16 [32, 128, 32, 256], P(None, 'gy', 'gz')
- cell_next: float32 [32, 128, 32, 256], P(None, 'gy', 'gz')
- velocity_next: float32 [3, 128, 32, 256], P(None, 'gy', 'gz')
The draws below stay inside these ranges and needn't reach their ends.
All inputs are finite; a program needn't handle non-finite values.
Results may differ from the reference program's by a relative error of at most 0.0025.
Values may be sent and summed in bfloat16 or wider, within the bound.
A program may use at most 64 MiB of HBM per device.

```python
import jax
import jax.numpy as jnp
from jax import lax

NX = 256
HID = 32
CIN = 3
GATES = 128
NY = 128
NZ = 32


def level_of(key, shape, cuts, smallest, largest):
    loudness, own = 1.0, jax.random.fold_in(key, 6)
    for dim, blocks in cuts:
        draws = jnp.exp(jax.random.uniform(jax.random.fold_in(own, dim), (blocks,), jnp.float32, smallest / len(cuts), largest / len(cuts)))
        loudness = loudness * jnp.repeat(draws, shape[dim] // blocks).reshape([-1 if axis == dim else 1 for axis in range(len(shape))])
    return loudness


def scatter_about(rng, extent, spread, reach, shards=(), kind=jnp.bfloat16):
    result = spread * jax.random.normal(rng, extent, jnp.float32)
    if shards:
        result = result * level_of(rng, extent, shards, -0.22, 0.18)
    return jnp.clip(result, -reach, reach).astype(kind)


def setup_inputs(seed: int = 0) -> dict:
    seeds = jax.random.split(jax.random.key(seed), 7)
    return {
        "velocity": scatter_about(seeds[0], (CIN, NY, NZ, NX), 1.0, 6.0, ((1, 16), (2, 16)), jnp.float32),
        "hidden": scatter_about(seeds[1], (HID, NY, NZ, NX), 0.5, 3.0, ((1, 16), (2, 16))),
        "cell": scatter_about(seeds[2], (HID, NY, NZ, NX), 1.0, 6.0, ((1, 16), (2, 16)), jnp.float32),
        "gate_weight": scatter_about(seeds[3], (GATES, 27 * (CIN + HID)), (27 * (CIN + HID)) ** -0.5, 0.1875),
        "gate_bias": jnp.clip(jax.random.uniform(seeds[4], (GATES,), jnp.float32, -1.0, 1.0), -1.0, 1.0),
        "decoder": scatter_about(seeds[5], (CIN, HID), HID ** -0.5, 1.0),
    }


def lstm_update(gate_values, previous):
    hidden_units = previous.shape[0]
    input_gate = jax.nn.sigmoid(gate_values[:hidden_units])
    forget_gate = jax.nn.sigmoid(gate_values[hidden_units:2 * hidden_units])
    candidate = jnp.tanh(gate_values[2 * hidden_units:3 * hidden_units])
    output_gate = jax.nn.sigmoid(gate_values[3 * hidden_units:])
    cell_next = forget_gate * previous + input_gate * candidate
    hidden_next = (output_gate * jnp.tanh(cell_next)).astype(jnp.bfloat16)
    return hidden_next, cell_next


def gather_columns(slab_rows, depth_cells, width_cells):
    pieces = [slab_rows[:, shift_y, shift_z:shift_z + depth_cells, shift_x:shift_x + width_cells]
              for shift_y in range(3) for shift_z in range(3) for shift_x in range(3)]
    return jnp.concatenate(pieces, 0)


def wavenumbers(count, start, total):
    positions = start + jnp.arange(count, dtype=jnp.int32)
    signed = jnp.where(positions < total // 2, positions, positions - total)
    signed = jnp.where(positions == total // 2, 0, signed)
    return signed.astype(jnp.float32)


def reference(velocity, hidden, cell, gate_weight, gate_bias, decoder):
    stacked = jnp.concatenate([velocity.astype(jnp.bfloat16), hidden], 0)
    padded = jnp.pad(stacked, ((0, 0), (1, 1), (1, 1), (1, 1)), mode="wrap")
    depth_cells = cell.shape[2]
    width_cells = cell.shape[3]

    def one_row(row_index):
        slab_rows = lax.dynamic_slice_in_dim(padded, row_index, 3, 1)
        columns = gather_columns(slab_rows, depth_cells, width_cells)
        gate_values = jnp.dot(gate_weight, columns.reshape(columns.shape[0], depth_cells * width_cells),
                              preferred_element_type=jnp.float32)
        gate_values = gate_values.reshape(-1, depth_cells, width_cells) + gate_bias[:, None, None]
        previous = lax.dynamic_index_in_dim(cell, row_index, 1, keepdims=False)
        return lstm_update(gate_values, previous)

    hidden_rows, cell_rows = lax.map(one_row, jnp.arange(cell.shape[1], dtype=jnp.int32))
    hidden_next = jnp.moveaxis(hidden_rows, 0, 1)
    cell_next = jnp.moveaxis(cell_rows, 0, 1)
    hidden_units = hidden.shape[0]
    increment = jnp.dot(decoder, hidden_next.reshape(hidden_units, -1), preferred_element_type=jnp.float32)
    advanced = velocity + increment.reshape(velocity.shape)
    spectrum = jnp.fft.fftn(advanced, axes=(1, 2, 3))
    total_y, total_z, total_x = advanced.shape[1], advanced.shape[2], advanced.shape[3]
    wave_y = wavenumbers(total_y, 0, total_y)[:, None, None]
    wave_z = wavenumbers(total_z, 0, total_z)[None, :, None]
    wave_x = wavenumbers(total_x, 0, total_x)[None, None, :]
    magnitude = jnp.maximum(wave_x * wave_x + wave_y * wave_y + wave_z * wave_z, 1.0)
    scaled = (wave_x * spectrum[0] + wave_y * spectrum[1] + wave_z * spectrum[2]) / magnitude
    projected = jnp.stack([spectrum[0] - wave_x * scaled, spectrum[1] - wave_y * scaled,
                           spectrum[2] - wave_z * scaled])
    velocity_next = jnp.real(jnp.fft.ifftn(projected, axes=(1, 2, 3))).astype(jnp.float32)
    return hidden_next, cell_next, velocity_next
```

```python
import functools

import jax
import jax.numpy as jnp
import numpy as np
from jax import lax
from jax.experimental import pallas as pl
from jax.experimental.pallas import tpu as pltpu
from jax.sharding import PartitionSpec as P

F32 = jnp.float32
BF16 = jnp.bfloat16
MESH = pl.DeviceIdType.MESH
NX, NY, NZ = 256, 128, 32
RANKS = 16
SLAB = 128
HALO = [(sy, sz) for sz in (-1, 1) for sy in (0, -1, 1)] + [(-1, 0), (1, 0)]


def halves(table):
    high = table.astype(np.float32).astype(jnp.bfloat16)
    low = (table - high.astype(np.float64)).astype(np.float32).astype(jnp.bfloat16)
    return np.stack([np.asarray(high), np.asarray(low)])


def signed_waves(total):
    index = np.arange(total)
    wave = np.where(index < total // 2, index, index - total)
    return np.where(index == total // 2, 0, wave).astype(np.float64)


def x_tables():
    lane = np.arange(128)
    mode = (lane % 16) * 8 + lane // 16
    n = np.arange(NX)
    angle = 2 * np.pi / NX * ((n[:, None] * mode[None, :]) % NX)
    sign = np.where(n % 2 == 0, 1.0, -1.0)
    imag = np.where(mode[None, :] == 0, sign[:, None], -np.sin(angle))
    forward = np.concatenate([np.cos(angle), imag], 1)
    weight = np.where(mode == 0, 1.0, 2.0)
    inverse = forward.T * np.concatenate([weight, weight])[:, None]
    return forward, inverse


def y_tables():
    lane = np.arange(128)
    mode = (lane % 16) * 8 + lane // 16
    y = np.arange(NY)
    angle = 2 * np.pi / NY * ((y[:, None] * mode[None, :]) % NY)
    forward = np.concatenate([np.cos(angle), np.sin(angle)], 0)
    inverse = np.concatenate([np.cos(angle).T, np.sin(angle).T], 0)
    return forward, inverse


def z_tables():
    kz = np.arange(NZ)
    z = np.arange(NZ)
    wave = signed_waves(NZ)[:, None]
    angle = 2 * np.pi / NZ * ((kz[:, None] * z[None, :]) % NZ)
    cosine, sine = np.cos(angle), np.sin(angle)
    forward = np.zeros((2, NZ, RANKS, 2, 2, 2))
    inverse = np.zeros((RANKS, 2, 2, 2, 2, NZ))
    for own in range(2):
        c, s = cosine[:, own::2], sine[:, own::2]
        for field, scale in ((0, np.ones_like(wave)), (1, wave)):
            forward[0, :, :, field, own, 0] = scale * c
            forward[0, :, :, field, own, 1] = scale * s
            forward[1, :, :, field, own, 1] = scale * c
            forward[1, :, :, field, own, 0] = -scale * s
            inverse[:, field, own, 0, 0, :] = (scale * c).T
            inverse[:, field, own, 0, 1, :] = -(scale * s).T
            inverse[:, field, own, 1, 1, :] = (scale * c).T
            inverse[:, field, own, 1, 0, :] = (scale * s).T
    return forward.reshape(64, 128), inverse.reshape(128, 64)


def split(value):
    high = value.astype(BF16)
    return high, (value - high.astype(F32)).astype(BF16)


def dot(a, b):
    return jnp.dot(a, b, preferred_element_type=F32)


def data_by_table(value, table):
    high, low = split(value)
    return dot(high, table[0]) + (dot(low, table[0]) + dot(high, table[1]))


def table_by_data(table, value):
    high, low = split(value)
    return dot(table[0], high) + (dot(table[0], low) + dot(table[1], high))


def roll_lanes(value, shift):
    return value if shift % 128 == 0 else pltpu.roll(value, shift % 128, 1)


def roll_rows(value, shift):
    return pltpu.roll(value, shift % value.shape[0], 0)


def lane_ids():
    return lax.broadcasted_iota(jnp.int32, (8, 128), 1)


def lane_mix(values, count):
    low = lane_ids() % 16
    masks = [low == q for q in range(16)]
    rolled = [roll_lanes(v, r) for r, v in enumerate(values)]
    outs = []
    for j in range(count):
        acc = jnp.zeros((8, 128), F32)
        for r, v in enumerate(rolled):
            acc = jnp.where(masks[(j + r) % 16], v, acc)
        outs.append(roll_lanes(acc, -j))
    return outs


def wave_of(index, total):
    wave = jnp.where(index < total // 2, index, index - total)
    return jnp.where(index == total // 2, 0, wave).astype(F32)


def mode_waves(total):
    lane = lane_ids()
    return wave_of((lane % 16) * 8 + lane // 16, total)


def x_forward(rows, table):
    spectrum = data_by_table(rows, table)
    kx = mode_waves(2 * NX)

    def part(c, z, p):
        start = (2 * c + z) * 8
        return spectrum[start : start + 8, 128 * p : 128 * p + 128]

    values = []
    for c in (0, 2, 1):
        for z in range(2):
            for p in range(2):
                values.append(part(c, z, p) * kx if c == 0 else part(c, z, p))
    return lane_mix(values, RANKS)


def swapped(value, sign):
    even = lax.broadcasted_iota(jnp.int32, value.shape, 0) % 2 == 0
    return jnp.where(even, sign * roll_rows(value, -1), -sign * roll_rows(value, 1))


def y_forward(tiles, table):
    rows = tiles.T
    out = data_by_table(jnp.concatenate([rows, swapped(rows, 1.0)], 1), table)
    ky = mode_waves(NY)
    values = [out[16 * k : 16 * k + 8] + ky * out[16 * k + 8 : 16 * k + 16] for k in range(8)]
    return lane_mix(values, RANKS)


def z_both(tiles, forward, inverse, me_gy, me_gz):
    numer = table_by_data(forward, tiles)
    lane = lax.broadcasted_iota(jnp.int32, (NZ, 128), 1)
    kx = (me_gy * 8 + lane % 8).astype(F32)
    ky = wave_of(me_gz * 8 + lane // 16, NY)
    kz = wave_of(lax.broadcasted_iota(jnp.int32, (NZ, 128), 0), NZ)
    factor = (1.0 / (NX * NY * NZ)) / jnp.maximum(kx * kx + ky * ky + kz * kz, 1.0)
    return table_by_data(inverse, numer * jnp.concatenate([factor, factor], 0))


def y_inverse(tiles, table):
    values = lane_mix(tiles, 8)
    ky = mode_waves(NY)
    rows = []
    for v in values:
        rows += [v, v * ky]
    rows = jnp.concatenate(rows, 0)
    out = data_by_table(jnp.concatenate([rows, swapped(rows, -1.0)], 1), table)
    return out.T


def x_inverse(tiles, table):
    values = lane_mix(tiles, 12)
    kx = mode_waves(2 * NX)
    rows = []
    for c, base in ((0, 0), (1, 8), (2, 4)):
        for z in range(2):
            pair = [values[base + 2 * z + p] for p in range(2)]
            if c == 0:
                pair = [v * kx for v in pair]
            rows.append(jnp.concatenate(pair, 1))
    return data_by_table(jnp.concatenate(rows, 0), table)


def around(index, step):
    return lax.rem(index + step + RANKS, RANKS)


def spectral_kernel(
    u_ref, xf_ref, xi_ref, yf_ref, yi_ref, zf_ref, zi_ref, out_ref, send, recv, send_sem, recv_sem
):
    gy, gz = lax.axis_index("gy"), lax.axis_index("gz")
    barrier = pltpu.get_barrier_semaphore()

    def greet(d, carry):
        pl.semaphore_signal(barrier, inc=1, device_id=(around(gy, d), gz), device_id_type=MESH)
        pl.semaphore_signal(barrier, inc=1, device_id=(gy, around(gz, d)), device_id_type=MESH)
        return carry

    lax.fori_loop(1, RANKS, greet, 0)

    def exchange(step, along_y):
        me = gy if along_y else gz

        def start(d, carry):
            to = around(me, d)
            target = (to, gz) if along_y else (gy, to)
            pltpu.make_async_remote_copy(
                src_ref=send.at[step, to],
                dst_ref=recv.at[step, me],
                send_sem=send_sem.at[step],
                recv_sem=recv_sem.at[step],
                device_id=target,
                device_id_type=MESH,
            ).start()
            return carry

        lax.fori_loop(1, RANKS, start, 0)
        recv[step, pl.ds(me, 1)] = send[step, pl.ds(me, 1)]
        some = recv.at[step, pl.ds(0, RANKS - 1)]
        pltpu.make_async_copy(some, some, recv_sem.at[step]).wait()

    tiles = x_forward(u_ref[...], xf_ref)
    for j in range(RANKS):
        send[0, j] = tiles[j]
    pl.semaphore_wait(barrier, 2 * (RANKS - 1))
    exchange(0, True)
    tiles = y_forward(recv[0].reshape(128, 128), yf_ref)
    for j in range(RANKS):
        send[1, j] = tiles[j]
    exchange(1, False)
    send[2] = z_both(recv[1].reshape(128, 128), zf_ref, zi_ref, gy, gz).reshape(RANKS, 8, 128)
    exchange(2, False)
    send[3] = y_inverse([recv[2, j] for j in range(RANKS)], yi_ref).reshape(RANKS, 8, 128)
    exchange(3, True)
    gradient = x_inverse([recv[3, j] for j in range(RANKS)], xi_ref)
    result = u_ref[...] - gradient
    for c in range(3):
        for z in range(2):
            start = (2 * c + z) * 8
            for t in range(2):
                out_ref[pl.ds(c * 32 + 2 * t + z, 8, stride=4), :] = result[
                    start : start + 8, 128 * t : 128 * t + 128
                ]
    for step in range(4):
        some = send.at[step, pl.ds(0, RANKS - 1)]
        pltpu.make_async_copy(some, some, send_sem.at[step]).wait()


def conv_kernel(
    vel_hbm, hid_hbm, cell_hbm, weight_hbm, bias_ref, dec_ref, hid_out, cell_out, u_ref,
    hid_in, hid_f, vel_f, cell_v, weight_v, weight_f, block_f, wide, side, slabs, vels, vel_t,
    vz_s, vz_r, vy_s, vy_r, vc_s, vc_r, acc, moved, load_sem, send_sem, recv_sem, store_sem,
):
    gy, gz = lax.axis_index("gy"), lax.axis_index("gz")
    loads = [
        pltpu.make_async_copy(src, dst, load_sem.at[i])
        for i, (src, dst) in enumerate(
            [(hid_hbm, hid_in), (vel_hbm, vel_f), (weight_hbm, weight_v), (cell_hbm, cell_v)]
        )
    ]
    for load in loads:
        load.start()
    barrier = pltpu.get_barrier_semaphore()
    targets = [(around(gy, sy), around(gz, sz)) for sy, sz in HALO]
    for target in targets:
        pl.semaphore_signal(barrier, inc=1, device_id=target, device_id_type=MESH)
    vels[...] = jnp.zeros_like(vels)

    loads[0].wait()
    hid_f[...] = hid_in[...].astype(F32)
    loads[1].wait()

    def centre(y, carry):
        for z in range(2):
            for t in range(2):
                lanes = slice(128 * t, 128 * t + 128)
                rows = hid_f[pl.ds(y * 4 + 2 * t + z, 32, stride=32), :]
                slabs[y + 1, z + 1, 32:64, lanes] = rows.astype(BF16)
                vels[y + 1, z + 1, 0:3, lanes] = vel_f[pl.ds(y * 4 + 2 * t + z, 3, stride=32), :]
        return carry

    lax.fori_loop(0, 8, centre, 0)
    for z in range(2):
        for t in range(2):
            rows = vel_f[pl.ds(2 * t + z, 24, stride=4), :]
            rows = jnp.concatenate([rows, jnp.zeros((8, 128), F32)], 0)
            vz_s[z, :, 128 * t : 128 * t + 128] = rows.astype(BF16)
    for k in range(2):
        y = 1 + 7 * k
        vy_s[k] = jnp.concatenate([vels[y, 1], vels[y, 2]], 0).astype(BF16)
        for z in range(2):
            rows = jnp.concatenate([vels[y, z + 1], jnp.zeros((8, NX), F32)], 0)
            vc_s[2 * k + z] = rows.astype(BF16)

    pl.semaphore_wait(barrier, len(HALO))
    copies = []
    for i, (sy, sz) in enumerate(HALO):
        k, z = (1 + sy) // 2, (1 + sz) // 2
        src_y, dst_y = (pl.ds(1, 8), pl.ds(1, 8)) if sy == 0 else (pl.ds(1 + 7 * k, 1), pl.ds(9 - 9 * k, 1))
        src_z, dst_z = (pl.ds(1, 2), pl.ds(1, 2)) if sz == 0 else (pl.ds(1 + z, 1), pl.ds(3 - 3 * z, 1))
        if sy == 0:
            extra = (vz_s.at[z], vz_r.at[z])
        elif sz == 0:
            extra = (vy_s.at[k], vy_r.at[k])
        else:
            extra = (vc_s.at[2 * k + z], vc_r.at[2 * k + z])
        mids = pl.ds(32, 32)
        pair = []
        for n, (src, dst) in enumerate(
            [(slabs.at[src_y, src_z, mids], slabs.at[dst_y, dst_z, mids]), extra]
        ):
            pair.append(
                pltpu.make_async_remote_copy(
                    src_ref=src,
                    dst_ref=dst,
                    send_sem=send_sem.at[i, n],
                    recv_sem=recv_sem.at[i, n],
                    device_id=targets[i],
                    device_id_type=MESH,
                )
            )
            pair[-1].start()
        copies.append(pair)

    def fill(y, z):
        mid = slabs[y, z, 32:64, :].astype(F32)
        slabs[y, z, 0:32, :] = pltpu.roll(mid, 1, 1).astype(BF16)
        slabs[y, z, 64:96, :] = pltpu.roll(mid, NX - 1, 1).astype(BF16)
        v = vels[y, z]
        first = v + pltpu.roll(pltpu.roll(v, 1, 1), 3, 0)
        tile = jnp.concatenate([first, pltpu.roll(v, NX - 1, 1), jnp.ones((16, NX), F32)], 0)
        slabs[y, z, 96:128, :] = tile.astype(BF16)

    def fill_own(y, carry):
        fill(y, 1)
        fill(y, 2)
        return carry

    lax.fori_loop(1, 9, fill_own, 0)

    loads[2].wait()
    weight_f[0:945, :] = weight_v[...].astype(F32)
    block_f[96:128, :] = jnp.zeros((32, 128), F32)
    for dy in range(3):
        for dz in range(3):
            first = (9 * dy + 3 * dz) * 35
            for dx in range(3):
                at = first + 35 * dx
                block_f[32 * dx : 32 * dx + 32, :] = weight_f[at + 3 : at + 35, :]
                row = 96 + (3, 0, 8)[dx]
                block_f[row : row + 3, :] = weight_f[at : at + 3, :]
            if dy == 1 and dz == 1:
                rest = bias_ref[...]
                for part in range(3):
                    high = rest.astype(BF16).astype(F32)
                    block_f[112 + part : 113 + part, :] = high
                    rest = rest - high
            turned = block_f[...].T.astype(BF16)
            if dy == 1 and dz == 1:
                block_f[112:120, :] = jnp.zeros((8, 128), F32)
            if dz == 0:
                side[0, :, 128 * dy : 128 * dy + 128] = turned
            if dz == 2:
                side[1, :, 128 * dy : 128 * dy + 128] = turned
            for z in range(2):
                own = z + dz - 1
                if 0 <= own < 2:
                    at = (2 * dy + own) * 128
                    wide[128 * z : 128 * z + 128, at : at + 128] = turned

    def inner(y):
        acc[y] = dot(wide[...], slabs[pl.ds(y, 3), 1:3].reshape(6 * SLAB, NX))

    def inner_step(y, carry):
        inner(y)
        return carry

    lax.fori_loop(1, 7, inner_step, 0)

    for i in (6, 7):
        for copy in copies[i]:
            copy.wait_recv()
        k = (1 + HALO[i][0]) // 2
        rows = vy_r[k].astype(F32)
        y = 9 - 9 * k
        vels[y, 1] = rows[0:8]
        vels[y, 2] = rows[8:16]
        fill(y, 1)
        fill(y, 2)
    inner(0)
    inner(7)

    for i in range(6):
        for copy in copies[i]:
            copy.wait_recv()
    for z in range(2):
        to = 3 - 3 * z
        rows = vz_r[z].astype(F32)
        for t in range(2):
            vel_t[t] = rows[:, 128 * t : 128 * t + 128]
            for y in range(8):
                vels[y + 1, to, 0:3, 128 * t : 128 * t + 128] = vel_t[t, pl.ds(y, 3, stride=8), :]
        for k in range(2):
            vels[9 - 9 * k, to] = vc_r[2 * k + z].astype(F32)[0:8]

    def fill_outer(y, carry):
        fill(y, 0)
        fill(y, 3)
        return carry

    lax.fori_loop(0, 10, fill_outer, 0)

    loads[3].wait()

    def sigmoid(value):
        return 0.5 * jnp.tanh(0.5 * value) + 0.5

    def update(y, carry):
        for z in range(2):
            outer = slabs[pl.ds(y, 3), 3 * z].reshape(3 * SLAB, NX)
            gates = acc[y, 128 * z : 128 * z + 128, :] + dot(side[z], outer)
            hidden_parts = []
            for t in range(2):
                lanes = slice(128 * t, 128 * t + 128)
                rows = pl.ds(y * 4 + 2 * t + z, 32, stride=32)
                part = gates[:, lanes]
                cell = sigmoid(part[32:64]) * cell_v[rows, :] + sigmoid(part[0:32]) * jnp.tanh(part[64:96])
                hidden = sigmoid(part[96:128]) * jnp.tanh(cell)
                cell_v[rows, :] = cell
                hid_f[rows, :] = hidden
                hidden_parts.append(hidden.astype(BF16))
            increment = dot(dec_ref[...], jnp.concatenate(hidden_parts, 1))
            advanced = vels[y + 1, z + 1, 0:3, :] + increment
            for t in range(2):
                rows = pl.ds(pl.multiple_of(16 * y + 8 * z, 8), 3)
                moved[t, rows, :] = advanced[:, 128 * t : 128 * t + 128]
        return carry

    lax.fori_loop(0, 8, update, 0)
    for c in range(3):
        for z in range(2):
            for t in range(2):
                start = 16 * c + 8 * z
                u_ref[start : start + 8, 128 * t : 128 * t + 128] = moved[
                    t, pl.ds(8 * z + c, 8, stride=16), :
                ]
    cell_store = pltpu.make_async_copy(cell_v, cell_out, store_sem.at[0])
    cell_store.start()
    hid_in[...] = hid_f[...].astype(BF16)
    hid_store = pltpu.make_async_copy(hid_in, hid_out, store_sem.at[1])
    hid_store.start()
    for pair in copies:
        for copy in pair:
            copy.wait_send()
    cell_store.wait()
    hid_store.wait()


def to_rows(array):
    c = array.shape[0]
    return array.reshape(c, 8, 2, 2, 128).transpose(0, 1, 3, 2, 4).reshape(c * 32, 128)


def from_rows(array):
    c = array.shape[0] // 32
    return array.reshape(c, 8, 2, 2, 128).transpose(0, 1, 3, 2, 4).reshape(c, 8, 2, 256)


def per_device(velocity, hidden, cell, gate_weight, gate_bias, decoder):
    vmem = pl.BlockSpec(memory_space=pltpu.VMEM)
    anywhere = pl.BlockSpec(memory_space=pl.ANY)
    hid_next, cell_next, advanced = pl.pallas_call(
        conv_kernel,
        out_shape=(
            jax.ShapeDtypeStruct((1024, 128), BF16),
            jax.ShapeDtypeStruct((1024, 128), F32),
            jax.ShapeDtypeStruct((48, 256), F32),
        ),
        in_specs=[anywhere] * 4 + [vmem] * 2,
        out_specs=(anywhere, anywhere, vmem),
        scratch_shapes=[
            pltpu.VMEM((1024, 128), BF16),
            pltpu.VMEM((1024, 128), F32),
            pltpu.VMEM((96, 128), F32),
            pltpu.VMEM((1024, 128), F32),
            pltpu.VMEM((945, 128), BF16),
            pltpu.VMEM((952, 128), F32),
            pltpu.VMEM((128, 128), F32),
            pltpu.VMEM((256, 768), BF16),
            pltpu.VMEM((2, 128, 384), BF16),
            pltpu.VMEM((10, 4, SLAB, NX), BF16),
            pltpu.VMEM((10, 4, 8, NX), F32),
            pltpu.VMEM((2, 32, 128), F32),
            pltpu.VMEM((2, 32, NX), BF16),
            pltpu.VMEM((2, 32, NX), BF16),
            pltpu.VMEM((2, 16, NX), BF16),
            pltpu.VMEM((2, 16, NX), BF16),
            pltpu.VMEM((4, 16, NX), BF16),
            pltpu.VMEM((4, 16, NX), BF16),
            pltpu.VMEM((8, 256, 256), F32),
            pltpu.VMEM((2, 128, 128), F32),
            pltpu.SemaphoreType.DMA((4,)),
            pltpu.SemaphoreType.DMA((8, 2)),
            pltpu.SemaphoreType.DMA((8, 2)),
            pltpu.SemaphoreType.DMA((2,)),
        ],
        compiler_params=pltpu.CompilerParams(
            collective_id=0, has_side_effects=True, vmem_limit_bytes=24 * 1024 * 1024
        ),
    )(
        to_rows(velocity),
        to_rows(hidden),
        to_rows(cell),
        gate_weight.T,
        gate_bias.reshape(1, 128),
        decoder,
    )
    tables = [jnp.asarray(halves(t)) for t in (*x_tables(), *y_tables(), *z_tables())]
    velocity_next = pl.pallas_call(
        spectral_kernel,
        out_shape=jax.ShapeDtypeStruct((96, 128), F32),
        in_specs=[vmem] * 7,
        out_specs=vmem,
        scratch_shapes=[
            pltpu.VMEM((4, RANKS, 8, 128), F32),
            pltpu.VMEM((4, RANKS, 8, 128), F32),
            pltpu.SemaphoreType.DMA((4,)),
            pltpu.SemaphoreType.DMA((4,)),
        ],
        compiler_params=pltpu.CompilerParams(
            collective_id=1, has_side_effects=True, vmem_limit_bytes=16 * 1024 * 1024
        ),
    )(advanced, *tables)
    return from_rows(hid_next), from_rows(cell_next), from_rows(velocity_next)


def solution(mesh):
    field = P(None, "gy", "gz", None)
    return jax.shard_map(
        per_device,
        mesh=mesh,
        in_specs=(field, field, field, P(), P(), P()),
        out_specs=(field, field, field),
        check_vma=False,
    )
```

```python
import functools

import jax
import jax.numpy as jnp
import numpy as np
from jax import lax
from jax.experimental import pallas as pl
from jax.experimental.pallas import tpu as pltpu
from jax.sharding import PartitionSpec as P

F32 = jnp.float32
BF16 = jnp.bfloat16
MESH = pl.DeviceIdType.MESH
NX, NY, NZ = 256, 128, 32
RANKS = 16
SLAB = 128
HALO = [(sy, sz) for sz in (-1, 1) for sy in (0, -1, 1)] + [(-1, 0), (1, 0)]


def halves(table):
    high = table.astype(np.float32).astype(jnp.bfloat16)
    low = (table - high.astype(np.float64)).astype(np.float32).astype(jnp.bfloat16)
    pair = np.stack([np.asarray(high), np.asarray(low)])
    if table.shape[1] == 256:
        pair = pair.reshape(2, -1, 2, 128).transpose(0, 2, 1, 3)
    return np.ascontiguousarray(pair)


def signed_waves(total):
    index = np.arange(total)
    wave = np.where(index < total // 2, index, index - total)
    return np.where(index == total // 2, 0, wave).astype(np.float64)


def x_tables():
    lane = np.arange(128)
    mode = (lane % 16) * 8 + lane // 16
    n = np.arange(NX)
    angle = 2 * np.pi / NX * ((n[:, None] * mode[None, :]) % NX)
    sign = np.where(n % 2 == 0, 1.0, -1.0)
    imag = np.where(mode[None, :] == 0, sign[:, None], -np.sin(angle))
    forward = np.concatenate([np.cos(angle), imag], 1)
    weight = np.where(mode == 0, 1.0, 2.0)
    inverse = forward.T * np.concatenate([weight, weight])[:, None]
    return forward, inverse


def y_tables():
    lane = np.arange(128)
    mode = (lane % 16) * 8 + lane // 16
    y = np.arange(NY)
    angle = 2 * np.pi / NY * ((y[:, None] * mode[None, :]) % NY)
    forward = np.concatenate([np.cos(angle), np.sin(angle)], 0)
    inverse = np.concatenate([np.cos(angle).T, np.sin(angle).T], 0)
    return forward, inverse


def z_tables():
    kz = np.arange(NZ)
    z = np.arange(NZ)
    wave = signed_waves(NZ)[:, None]
    angle = 2 * np.pi / NZ * ((kz[:, None] * z[None, :]) % NZ)
    cosine, sine = np.cos(angle), np.sin(angle)
    forward = np.zeros((2, NZ, RANKS, 2, 2, 2))
    inverse = np.zeros((RANKS, 2, 2, 2, 2, NZ))
    for own in range(2):
        c, s = cosine[:, own::2], sine[:, own::2]
        for field, scale in ((0, np.ones_like(wave)), (1, wave)):
            forward[0, :, :, field, own, 0] = scale * c
            forward[0, :, :, field, own, 1] = scale * s
            forward[1, :, :, field, own, 1] = scale * c
            forward[1, :, :, field, own, 0] = -scale * s
            inverse[:, field, own, 0, 0, :] = (scale * c).T
            inverse[:, field, own, 0, 1, :] = -(scale * s).T
            inverse[:, field, own, 1, 1, :] = (scale * c).T
            inverse[:, field, own, 1, 0, :] = (scale * s).T
    return forward.reshape(64, 128), inverse.reshape(128, 64)


def split(value):
    high = value.astype(BF16)
    return high, (value - high.astype(F32)).astype(BF16)


def dot(a, b):
    return jnp.dot(a, b, preferred_element_type=F32)


def whole(table):
    if len(table.shape) == 3:
        return [table[0], table[1]]
    return [jnp.concatenate([table[part, 0], table[part, 1]], 1) for part in range(2)]


def data_by_table(value, table):
    table = whole(table)
    high, low = split(value)
    return dot(high, table[0]) + (dot(low, table[0]) + dot(high, table[1]))


def table_by_data(table, value):
    high, low = split(value)
    return dot(table[0], high) + (dot(table[0], low) + dot(table[1], high))


def roll_lanes(value, shift):
    return value if shift % 128 == 0 else pltpu.roll(value, shift % 128, 1)


def roll_rows(value, shift):
    return pltpu.roll(value, shift % value.shape[0], 0)


def lane_ids():
    return lax.broadcasted_iota(jnp.int32, (8, 128), 1)


def lane_mix(values, count):
    low = lane_ids() % 16
    masks = [low == q for q in range(16)]
    rolled = [roll_lanes(v, r) for r, v in enumerate(values)]
    outs = []
    for j in range(count):
        acc = jnp.zeros((8, 128), F32)
        for r, v in enumerate(rolled):
            acc = jnp.where(masks[(j + r) % 16], v, acc)
        outs.append(roll_lanes(acc, -j))
    return outs


def wave_of(index, total):
    wave = jnp.where(index < total // 2, index, index - total)
    return jnp.where(index == total // 2, 0, wave).astype(F32)


def mode_waves(total):
    lane = lane_ids()
    return wave_of((lane % 16) * 8 + lane // 16, total)


def x_forward(rows, table):
    spectrum = data_by_table(rows, table)
    kx = mode_waves(2 * NX)

    def part(c, z, p):
        start = (2 * c + z) * 8
        return spectrum[start : start + 8, 128 * p : 128 * p + 128]

    values = []
    for c in (0, 2, 1):
        for z in range(2):
            for p in range(2):
                values.append(part(c, z, p) * kx if c == 0 else part(c, z, p))
    return lane_mix(values, RANKS)


def swapped(value, sign):
    even = lax.broadcasted_iota(jnp.int32, value.shape, 0) % 2 == 0
    return jnp.where(even, sign * roll_rows(value, -1), -sign * roll_rows(value, 1))


def y_forward(tiles, table):
    rows = tiles.T
    out = data_by_table(jnp.concatenate([rows, swapped(rows, 1.0)], 1), table)
    ky = mode_waves(NY)
    values = [out[16 * k : 16 * k + 8] + ky * out[16 * k + 8 : 16 * k + 16] for k in range(8)]
    return lane_mix(values, RANKS)


def z_both(tiles, forward, inverse, me_gy, me_gz):
    numer = table_by_data(forward, tiles)
    lane = lax.broadcasted_iota(jnp.int32, (NZ, 128), 1)
    kx = (me_gy * 8 + lane % 8).astype(F32)
    ky = wave_of(me_gz * 8 + lane // 16, NY)
    kz = wave_of(lax.broadcasted_iota(jnp.int32, (NZ, 128), 0), NZ)
    factor = (1.0 / (NX * NY * NZ)) / jnp.maximum(kx * kx + ky * ky + kz * kz, 1.0)
    return table_by_data(inverse, numer * jnp.concatenate([factor, factor], 0))


def y_inverse(tiles, table):
    values = lane_mix(tiles, 8)
    ky = mode_waves(NY)
    rows = []
    for v in values:
        rows += [v, v * ky]
    rows = jnp.concatenate(rows, 0)
    out = data_by_table(jnp.concatenate([rows, swapped(rows, -1.0)], 1), table)
    return out.T


def x_inverse(tiles, table):
    values = lane_mix(tiles, 12)
    kx = mode_waves(2 * NX)
    rows = []
    for c, base in ((0, 0), (1, 8), (2, 4)):
        for z in range(2):
            pair = [values[base + 2 * z + p] for p in range(2)]
            if c == 0:
                pair = [v * kx for v in pair]
            rows.append(jnp.concatenate(pair, 1))
    return data_by_table(jnp.concatenate(rows, 0), table)


def around(index, step):
    return lax.rem(index + step + RANKS, RANKS)


def project(u_ref, tables, out_ref, send, recv, send_sem, recv_sem):
    gy, gz = lax.axis_index("gy"), lax.axis_index("gz")
    xf_ref, xi_ref, yf_ref, yi_ref, zf_ref, zi_ref = tables

    def exchange(step, along_y):
        me = gy if along_y else gz

        def start(d, carry):
            to = around(me, d)
            target = (to, gz) if along_y else (gy, to)
            pltpu.make_async_remote_copy(
                src_ref=send.at[step, to],
                dst_ref=recv.at[step, me],
                send_sem=send_sem.at[step],
                recv_sem=recv_sem.at[step],
                device_id=target,
                device_id_type=MESH,
            ).start()
            return carry

        lax.fori_loop(1, RANKS, start, 0)
        recv[step, pl.ds(me, 1)] = send[step, pl.ds(me, 1)]
        some = recv.at[step, pl.ds(0, RANKS - 1)]
        pltpu.make_async_copy(some, some, recv_sem.at[step]).wait()

    tiles = x_forward(u_ref[...], xf_ref)
    for j in range(RANKS):
        send[0, j] = tiles[j]
    exchange(0, True)
    tiles = y_forward(recv[0].reshape(128, 128), yf_ref)
    for j in range(RANKS):
        send[1, j] = tiles[j]
    exchange(1, False)
    send[2] = z_both(recv[1].reshape(128, 128), zf_ref, zi_ref, gy, gz).reshape(RANKS, 8, 128)
    exchange(2, False)
    send[3] = y_inverse([recv[2, j] for j in range(RANKS)], yi_ref).reshape(RANKS, 8, 128)
    exchange(3, True)
    gradient = x_inverse([recv[3, j] for j in range(RANKS)], xi_ref)
    result = u_ref[...] - gradient
    for c in range(3):
        for z in range(2):
            start = (2 * c + z) * 8
            for t in range(2):
                out_ref[pl.ds(c * 32 + 2 * t + z, 8, stride=4), :] = result[
                    start : start + 8, 128 * t : 128 * t + 128
                ]
    for step in range(4):
        some = send.at[step, pl.ds(0, RANKS - 1)]
        pltpu.make_async_copy(some, some, send_sem.at[step]).wait()


def step_kernel(
    vel_hbm, hid_hbm, cell_hbm, weight_hbm, bias_hbm, dec_hbm, *refs,
):
    tables_hbm, (hid_out, cell_out, vel_out) = refs[:6], refs[6:9]
    tables, refs = refs[9:15], refs[15:]
    (
        bias_ref, dec_ref, u_ref, vel_next,
        hid_in, hid_f, vel_f, cell_v, weight_v, weight_f, block_f, wide, side, slabs, vels, vel_t,
        vz_s, vz_r, vy_s, vy_r, vc_s, vc_r, acc, moved, send, recv,
        load_sem, send_sem, recv_sem, store_sem, tile_send_sem, tile_recv_sem,
    ) = refs
    gy, gz = lax.axis_index("gy"), lax.axis_index("gz")
    loads = [
        pltpu.make_async_copy(src, dst, load_sem.at[i])
        for i, (src, dst) in enumerate(
            [
                (hid_hbm, hid_in),
                (vel_hbm, vel_f),
                (weight_hbm, weight_v),
                (cell_hbm, cell_v),
                (bias_hbm, bias_ref),
                (dec_hbm, dec_ref),
                *zip(tables_hbm, tables),
            ]
        )
    ]
    for load in loads:
        load.start()
    barrier = pltpu.get_barrier_semaphore()
    targets = [(around(gy, sy), around(gz, sz)) for sy, sz in HALO]
    for target in targets:
        pl.semaphore_signal(barrier, inc=1, device_id=target, device_id_type=MESH)

    def greet(d, carry):
        pl.semaphore_signal(barrier, inc=1, device_id=(around(gy, d), gz), device_id_type=MESH)
        pl.semaphore_signal(barrier, inc=1, device_id=(gy, around(gz, d)), device_id_type=MESH)
        return carry

    lax.fori_loop(2, RANKS - 1, greet, 0)
    vels[...] = jnp.zeros_like(vels)

    loads[0].wait()
    hid_f[...] = hid_in[...].astype(F32)
    loads[1].wait()

    def centre(y, carry):
        for z in range(2):
            for t in range(2):
                lanes = slice(128 * t, 128 * t + 128)
                rows = hid_f[pl.ds(y * 4 + 2 * t + z, 32, stride=32), :]
                slabs[y + 1, z + 1, 32:64, lanes] = rows.astype(BF16)
                vels[y + 1, z + 1, 0:3, lanes] = vel_f[pl.ds(y * 4 + 2 * t + z, 3, stride=32), :]
        return carry

    lax.fori_loop(0, 8, centre, 0)
    for z in range(2):
        for t in range(2):
            rows = vel_f[pl.ds(2 * t + z, 24, stride=4), :]
            rows = jnp.concatenate([rows, jnp.zeros((8, 128), F32)], 0)
            vz_s[z, :, 128 * t : 128 * t + 128] = rows.astype(BF16)
    for k in range(2):
        y = 1 + 7 * k
        vy_s[k] = jnp.concatenate([vels[y, 1], vels[y, 2]], 0).astype(BF16)
        for z in range(2):
            rows = jnp.concatenate([vels[y, z + 1], jnp.zeros((8, NX), F32)], 0)
            vc_s[2 * k + z] = rows.astype(BF16)

    pl.semaphore_wait(barrier, len(HALO) + 2 * (RANKS - 3))
    copies = []
    for i, (sy, sz) in enumerate(HALO):
        k, z = (1 + sy) // 2, (1 + sz) // 2
        src_y, dst_y = (pl.ds(1, 8), pl.ds(1, 8)) if sy == 0 else (pl.ds(1 + 7 * k, 1), pl.ds(9 - 9 * k, 1))
        src_z, dst_z = (pl.ds(1, 2), pl.ds(1, 2)) if sz == 0 else (pl.ds(1 + z, 1), pl.ds(3 - 3 * z, 1))
        if sy == 0:
            extra = (vz_s.at[z], vz_r.at[z])
        elif sz == 0:
            extra = (vy_s.at[k], vy_r.at[k])
        else:
            extra = (vc_s.at[2 * k + z], vc_r.at[2 * k + z])
        mids = pl.ds(32, 32)
        pair = []
        for n, (src, dst) in enumerate(
            [(slabs.at[src_y, src_z, mids], slabs.at[dst_y, dst_z, mids]), extra]
        ):
            pair.append(
                pltpu.make_async_remote_copy(
                    src_ref=src,
                    dst_ref=dst,
                    send_sem=send_sem.at[i, n],
                    recv_sem=recv_sem.at[i, n],
                    device_id=targets[i],
                    device_id_type=MESH,
                )
            )
            pair[-1].start()
        copies.append(pair)

    def fill(y, z):
        mid = slabs[y, z, 32:64, :].astype(F32)
        slabs[y, z, 0:32, :] = pltpu.roll(mid, 1, 1).astype(BF16)
        slabs[y, z, 64:96, :] = pltpu.roll(mid, NX - 1, 1).astype(BF16)
        v = vels[y, z]
        first = v + pltpu.roll(pltpu.roll(v, 1, 1), 3, 0)
        tile = jnp.concatenate([first, pltpu.roll(v, NX - 1, 1), jnp.ones((16, NX), F32)], 0)
        slabs[y, z, 96:128, :] = tile.astype(BF16)

    def fill_own(y, carry):
        fill(y, 1)
        fill(y, 2)
        return carry

    lax.fori_loop(1, 9, fill_own, 0)

    loads[2].wait()
    loads[4].wait()
    weight_f[0:945, :] = weight_v[...].astype(F32)
    block_f[96:128, :] = jnp.zeros((32, 128), F32)
    for dy in range(3):
        for dz in range(3):
            first = (9 * dy + 3 * dz) * 35
            for dx in range(3):
                at = first + 35 * dx
                block_f[32 * dx : 32 * dx + 32, :] = weight_f[at + 3 : at + 35, :]
                row = 96 + (3, 0, 8)[dx]
                block_f[row : row + 3, :] = weight_f[at : at + 3, :]
            if dy == 1 and dz == 1:
                rest = bias_ref[...]
                for part in range(3):
                    high = rest.astype(BF16).astype(F32)
                    block_f[112 + part : 113 + part, :] = high
                    rest = rest - high
            turned = block_f[...].T.astype(BF16)
            if dy == 1 and dz == 1:
                block_f[112:120, :] = jnp.zeros((8, 128), F32)
            if dz == 0:
                side[0, :, 128 * dy : 128 * dy + 128] = turned
            if dz == 2:
                side[1, :, 128 * dy : 128 * dy + 128] = turned
            for z in range(2):
                own = z + dz - 1
                if 0 <= own < 2:
                    at = (2 * dy + own) * 128
                    wide[128 * z : 128 * z + 128, at : at + 128] = turned

    def inner(y):
        acc[y] = dot(wide[...], slabs[pl.ds(y, 3), 1:3].reshape(6 * SLAB, NX))

    def inner_step(y, carry):
        inner(y)
        return carry

    lax.fori_loop(1, 7, inner_step, 0)

    for i in (6, 7):
        for copy in copies[i]:
            copy.wait_recv()
        k = (1 + HALO[i][0]) // 2
        rows = vy_r[k].astype(F32)
        y = 9 - 9 * k
        vels[y, 1] = rows[0:8]
        vels[y, 2] = rows[8:16]
        fill(y, 1)
        fill(y, 2)
    inner(0)
    inner(7)

    for i in range(6):
        for copy in copies[i]:
            copy.wait_recv()
    for z in range(2):
        to = 3 - 3 * z
        rows = vz_r[z].astype(F32)
        for t in range(2):
            vel_t[t] = rows[:, 128 * t : 128 * t + 128]
            for y in range(8):
                vels[y + 1, to, 0:3, 128 * t : 128 * t + 128] = vel_t[t, pl.ds(y, 3, stride=8), :]
        for k in range(2):
            vels[9 - 9 * k, to] = vc_r[2 * k + z].astype(F32)[0:8]

    def fill_outer(y, carry):
        fill(y, 0)
        fill(y, 3)
        return carry

    lax.fori_loop(0, 10, fill_outer, 0)

    loads[3].wait()
    loads[5].wait()

    def sigmoid(value):
        return 0.5 * jnp.tanh(0.5 * value) + 0.5

    def update(y, carry):
        for z in range(2):
            outer = slabs[pl.ds(y, 3), 3 * z].reshape(3 * SLAB, NX)
            gates = acc[y, 128 * z : 128 * z + 128, :] + dot(side[z], outer)
            hidden_parts = []
            for t in range(2):
                lanes = slice(128 * t, 128 * t + 128)
                rows = pl.ds(y * 4 + 2 * t + z, 32, stride=32)
                part = gates[:, lanes]
                cell = sigmoid(part[32:64]) * cell_v[rows, :] + sigmoid(part[0:32]) * jnp.tanh(part[64:96])
                hidden = sigmoid(part[96:128]) * jnp.tanh(cell)
                cell_v[rows, :] = cell
                hid_f[rows, :] = hidden
                hidden_parts.append(hidden.astype(BF16))
            increment = dot(dec_ref[...], jnp.concatenate(hidden_parts, 1))
            advanced = vels[y + 1, z + 1, 0:3, :] + increment
            for t in range(2):
                rows = pl.ds(pl.multiple_of(16 * y + 8 * z, 8), 3)
                moved[t, rows, :] = advanced[:, 128 * t : 128 * t + 128]
        return carry

    lax.fori_loop(0, 8, update, 0)
    for c in range(3):
        for z in range(2):
            for t in range(2):
                start = 16 * c + 8 * z
                u_ref[start : start + 8, 128 * t : 128 * t + 128] = moved[
                    t, pl.ds(8 * z + c, 8, stride=16), :
                ]
    cell_store = pltpu.make_async_copy(cell_v, cell_out, store_sem.at[0])
    cell_store.start()
    hid_in[...] = hid_f[...].astype(BF16)
    hid_store = pltpu.make_async_copy(hid_in, hid_out, store_sem.at[1])
    hid_store.start()
    for load in loads[6:]:
        load.wait()
    project(u_ref, tables, vel_next, send, recv, tile_send_sem, tile_recv_sem)
    vel_store = pltpu.make_async_copy(vel_next, vel_out, store_sem.at[2])
    vel_store.start()
    for pair in copies:
        for copy in pair:
            copy.wait_send()
    cell_store.wait()
    hid_store.wait()
    vel_store.wait()


def hand_on_kernel(*refs):
    sources, results, sem = refs[:3], refs[3:6], refs[6]
    copies = [pltpu.make_async_copy(a, b, sem.at[i]) for i, (a, b) in enumerate(zip(sources, results))]
    for copy in copies:
        copy.start()
    for copy in copies:
        copy.wait()


def to_rows(array):
    c = array.shape[0]
    return array.reshape(c, 8, 2, 2, 128).transpose(0, 1, 3, 2, 4).reshape(c * 32, 128)


def from_rows(array):
    c = array.shape[0] // 32
    return array.reshape(c, 8, 2, 2, 128).transpose(0, 1, 3, 2, 4).reshape(c, 8, 2, 256)


def per_device(velocity, hidden, cell, gate_weight, gate_bias, decoder):
    anywhere = pl.BlockSpec(memory_space=pl.ANY)
    tables = [halves(t) for t in (*x_tables(), *y_tables(), *z_tables())]
    results = (
        jax.ShapeDtypeStruct((1024, 128), BF16),
        jax.ShapeDtypeStruct((1024, 128), F32),
        jax.ShapeDtypeStruct((96, 128), F32),
    )
    outs = pl.pallas_call(
        step_kernel,
        out_shape=results,
        in_specs=[anywhere] * 12,
        out_specs=(anywhere,) * 3,
        scratch_shapes=[
            *(pltpu.VMEM(t.shape, BF16) for t in tables),
            pltpu.VMEM((1, 128), F32),
            pltpu.VMEM((3, 32), BF16),
            pltpu.VMEM((48, 256), F32),
            pltpu.VMEM((96, 128), F32),
            pltpu.VMEM((1024, 128), BF16),
            pltpu.VMEM((1024, 128), F32),
            pltpu.VMEM((96, 128), F32),
            pltpu.VMEM((1024, 128), F32),
            pltpu.VMEM((945, 128), BF16),
            pltpu.VMEM((952, 128), F32),
            pltpu.VMEM((128, 128), F32),
            pltpu.VMEM((256, 768), BF16),
            pltpu.VMEM((2, 128, 384), BF16),
            pltpu.VMEM((10, 4, SLAB, NX), BF16),
            pltpu.VMEM((10, 4, 8, NX), F32),
            pltpu.VMEM((2, 32, 128), F32),
            pltpu.VMEM((2, 32, NX), BF16),
            pltpu.VMEM((2, 32, NX), BF16),
            pltpu.VMEM((2, 16, NX), BF16),
            pltpu.VMEM((2, 16, NX), BF16),
            pltpu.VMEM((4, 16, NX), BF16),
            pltpu.VMEM((4, 16, NX), BF16),
            pltpu.VMEM((8, 256, 256), F32),
            pltpu.VMEM((2, 128, 128), F32),
            pltpu.VMEM((4, RANKS, 8, 128), F32),
            pltpu.VMEM((4, RANKS, 8, 128), F32),
            pltpu.SemaphoreType.DMA((12,)),
            pltpu.SemaphoreType.DMA((8, 2)),
            pltpu.SemaphoreType.DMA((8, 2)),
            pltpu.SemaphoreType.DMA((3,)),
            pltpu.SemaphoreType.DMA((4,)),
            pltpu.SemaphoreType.DMA((4,)),
        ],
        compiler_params=pltpu.CompilerParams(
            collective_id=0, has_side_effects=True, vmem_limit_bytes=56 * 1024 * 1024
        ),
    )(
        to_rows(velocity),
        to_rows(hidden),
        to_rows(cell),
        gate_weight.T,
        gate_bias.reshape(1, 128),
        decoder,
        *(jnp.asarray(t) for t in tables),
    )
    outs = pl.pallas_call(
        hand_on_kernel,
        out_shape=results,
        in_specs=[anywhere] * 3,
        out_specs=(anywhere,) * 3,
        scratch_shapes=[pltpu.SemaphoreType.DMA((3,))],
        compiler_params=pltpu.CompilerParams(vmem_limit_bytes=56 * 1024 * 1024),
    )(*outs)
    return tuple(from_rows(out) for out in outs)


def solution(mesh):
    field = P(None, "gy", "gz", None)
    return jax.shard_map(
        per_device,
        mesh=mesh,
        in_specs=(field, field, field, P(), P(), P()),
        out_specs=(field, field, field),
        check_vma=False,
    )
```

```python
import functools

import jax
import jax.numpy as jnp
import numpy as np
from jax import lax
from jax.experimental import pallas as pl
from jax.experimental.pallas import tpu as pltpu
from jax.sharding import PartitionSpec as P

F32 = jnp.float32
BF16 = jnp.bfloat16
MESH = pl.DeviceIdType.MESH
NX, NY, NZ = 256, 128, 32
RANKS = 16
SLAB = 128
HALO = [(sy, sz) for sz in (-1, 1) for sy in (0, -1, 1)] + [(-1, 0), (1, 0)]


def halves(table):
    high = table.astype(np.float32).astype(jnp.bfloat16)
    low = (table - high.astype(np.float64)).astype(np.float32).astype(jnp.bfloat16)
    pair = np.stack([np.asarray(high), np.asarray(low)])
    if table.shape[1] == 256:
        pair = pair.reshape(2, -1, 2, 128).transpose(0, 2, 1, 3)
    return np.ascontiguousarray(pair)


def signed_waves(total):
    index = np.arange(total)
    wave = np.where(index < total // 2, index, index - total)
    return np.where(index == total // 2, 0, wave).astype(np.float64)


def x_tables():
    lane = np.arange(128)
    mode = (lane % 16) * 8 + lane // 16
    n = np.arange(NX)
    angle = 2 * np.pi / NX * ((n[:, None] * mode[None, :]) % NX)
    sign = np.where(n % 2 == 0, 1.0, -1.0)
    imag = np.where(mode[None, :] == 0, sign[:, None], -np.sin(angle))
    forward = np.concatenate([np.cos(angle), imag], 1)
    weight = np.where(mode == 0, 1.0, 2.0)
    inverse = forward.T * np.concatenate([weight, weight])[:, None]
    return forward, inverse


def y_tables():
    lane = np.arange(128)
    mode = (lane % 16) * 8 + lane // 16
    y = np.arange(NY)
    angle = 2 * np.pi / NY * ((y[:, None] * mode[None, :]) % NY)
    forward = np.concatenate([np.cos(angle), np.sin(angle)], 0)
    inverse = np.concatenate([np.cos(angle).T, np.sin(angle).T], 0)
    return forward, inverse


def z_tables():
    kz = np.arange(NZ)
    z = np.arange(NZ)
    wave = signed_waves(NZ)[:, None]
    angle = 2 * np.pi / NZ * ((kz[:, None] * z[None, :]) % NZ)
    cosine, sine = np.cos(angle), np.sin(angle)
    forward = np.zeros((2, NZ, RANKS, 2, 2, 2))
    inverse = np.zeros((RANKS, 2, 2, 2, 2, NZ))
    for own in range(2):
        c, s = cosine[:, own::2], sine[:, own::2]
        for field, scale in ((0, np.ones_like(wave)), (1, wave)):
            forward[0, :, :, field, own, 0] = scale * c
            forward[0, :, :, field, own, 1] = scale * s
            forward[1, :, :, field, own, 1] = scale * c
            forward[1, :, :, field, own, 0] = -scale * s
            inverse[:, field, own, 0, 0, :] = (scale * c).T
            inverse[:, field, own, 0, 1, :] = -(scale * s).T
            inverse[:, field, own, 1, 1, :] = (scale * c).T
            inverse[:, field, own, 1, 0, :] = (scale * s).T
    return forward.reshape(64, 128), inverse.reshape(128, 64)


def split(value):
    high = value.astype(BF16)
    return high, (value - high.astype(F32)).astype(BF16)


def dot(a, b):
    return jnp.dot(a, b, preferred_element_type=F32)


def whole(table):
    if len(table.shape) == 3:
        return [table[0], table[1]]
    return [jnp.concatenate([table[part, 0], table[part, 1]], 1) for part in range(2)]


def data_by_table(value, table):
    table = whole(table)
    high, low = split(value)
    return dot(high, table[0]) + (dot(low, table[0]) + dot(high, table[1]))


def table_by_data(table, value):
    high, low = split(value)
    return dot(table[0], high) + (dot(table[0], low) + dot(table[1], high))


def roll_lanes(value, shift):
    return value if shift % 128 == 0 else pltpu.roll(value, shift % 128, 1)


def roll_rows(value, shift):
    return pltpu.roll(value, shift % value.shape[0], 0)


def lane_ids():
    return lax.broadcasted_iota(jnp.int32, (8, 128), 1)


def lane_mix(values, count):
    low = lane_ids() % 16
    masks = [low == q for q in range(16)]
    rolled = [roll_lanes(v, r) for r, v in enumerate(values)]
    outs = []
    for j in range(count):
        acc = jnp.zeros((8, 128), F32)
        for r, v in enumerate(rolled):
            acc = jnp.where(masks[(j + r) % 16], v, acc)
        outs.append(roll_lanes(acc, -j))
    return outs


def wave_of(index, total):
    wave = jnp.where(index < total // 2, index, index - total)
    return jnp.where(index == total // 2, 0, wave).astype(F32)


def mode_waves(total):
    lane = lane_ids()
    return wave_of((lane % 16) * 8 + lane // 16, total)


def x_forward(rows, table):
    spectrum = data_by_table(rows, table)
    kx = mode_waves(2 * NX)

    def part(c, z, p):
        start = (2 * c + z) * 8
        return spectrum[start : start + 8, 128 * p : 128 * p + 128]

    values = []
    for c in (0, 2, 1):
        for z in range(2):
            for p in range(2):
                values.append(part(c, z, p) * kx if c == 0 else part(c, z, p))
    return lane_mix(values, RANKS)


def swapped(value, sign):
    even = lax.broadcasted_iota(jnp.int32, value.shape, 0) % 2 == 0
    return jnp.where(even, sign * roll_rows(value, -1), -sign * roll_rows(value, 1))


def y_forward(tiles, table):
    rows = tiles.T
    out = data_by_table(jnp.concatenate([rows, swapped(rows, 1.0)], 1), table)
    ky = mode_waves(NY)
    values = [out[16 * k : 16 * k + 8] + ky * out[16 * k + 8 : 16 * k + 16] for k in range(8)]
    return lane_mix(values, RANKS)


def z_both(tiles, forward, inverse, me_gy, me_gz):
    numer = table_by_data(forward, tiles)
    lane = lax.broadcasted_iota(jnp.int32, (NZ, 128), 1)
    kx = (me_gy * 8 + lane % 8).astype(F32)
    ky = wave_of(me_gz * 8 + lane // 16, NY)
    kz = wave_of(lax.broadcasted_iota(jnp.int32, (NZ, 128), 0), NZ)
    factor = (1.0 / (NX * NY * NZ)) / jnp.maximum(kx * kx + ky * ky + kz * kz, 1.0)
    return table_by_data(inverse, numer * jnp.concatenate([factor, factor], 0))


def y_inverse(tiles, table):
    values = lane_mix(tiles, 8)
    ky = mode_waves(NY)
    rows = []
    for v in values:
        rows += [v, v * ky]
    rows = jnp.concatenate(rows, 0)
    out = data_by_table(jnp.concatenate([rows, swapped(rows, -1.0)], 1), table)
    return out.T


def x_inverse(tiles, table):
    values = lane_mix(tiles, 12)
    kx = mode_waves(2 * NX)
    rows = []
    for c, base in ((0, 0), (1, 8), (2, 4)):
        for z in range(2):
            pair = [values[base + 2 * z + p] for p in range(2)]
            if c == 0:
                pair = [v * kx for v in pair]
            rows.append(jnp.concatenate(pair, 1))
    return data_by_table(jnp.concatenate(rows, 0), table)


def around(index, step):
    return lax.rem(index + step + RANKS, RANKS)


def project(u_ref, tables, out_ref, send, recv, send_sem, recv_sem):
    gy, gz = lax.axis_index("gy"), lax.axis_index("gz")
    xf_ref, xi_ref, yf_ref, yi_ref, zf_ref, zi_ref = tables

    def exchange(step, along_y):
        me = gy if along_y else gz

        def start(d, carry):
            to = around(me, d)
            target = (to, gz) if along_y else (gy, to)
            pltpu.make_async_remote_copy(
                src_ref=send.at[step, to],
                dst_ref=recv.at[step, me],
                send_sem=send_sem.at[step],
                recv_sem=recv_sem.at[step],
                device_id=target,
                device_id_type=MESH,
            ).start()
            return carry

        lax.fori_loop(1, RANKS, start, 0)
        recv[step, pl.ds(me, 1)] = send[step, pl.ds(me, 1)]
        some = recv.at[step, pl.ds(0, RANKS - 1)]
        pltpu.make_async_copy(some, some, recv_sem.at[step]).wait()

    tiles = x_forward(u_ref[...], xf_ref)
    for j in range(RANKS):
        send[0, j] = tiles[j]
    exchange(0, True)
    tiles = y_forward(recv[0].reshape(128, 128), yf_ref)
    for j in range(RANKS):
        send[1, j] = tiles[j]
    exchange(1, False)
    send[2] = z_both(recv[1].reshape(128, 128), zf_ref, zi_ref, gy, gz).reshape(RANKS, 8, 128)
    exchange(2, False)
    send[3] = y_inverse([recv[2, j] for j in range(RANKS)], yi_ref).reshape(RANKS, 8, 128)
    exchange(3, True)
    gradient = x_inverse([recv[3, j] for j in range(RANKS)], xi_ref)
    result = u_ref[...] - gradient
    for c in range(3):
        for z in range(2):
            start = (2 * c + z) * 8
            for t in range(2):
                out_ref[pl.ds(c * 32 + 2 * t + z, 8, stride=4), :] = result[
                    start : start + 8, 128 * t : 128 * t + 128
                ]
    for step in range(4):
        some = send.at[step, pl.ds(0, RANKS - 1)]
        pltpu.make_async_copy(some, some, send_sem.at[step]).wait()


def step_kernel(
    vel_hbm, hid_hbm, cell_hbm, weight_hbm, bias_hbm, dec_hbm, *refs,
):
    tables_hbm, (hid_out, cell_out, vel_out) = refs[:6], refs[6:9]
    tables, refs = refs[9:15], refs[15:]
    (
        bias_ref, dec_ref, u_ref, vel_next,
        hid_in, hid_f, vel_f, cell_v, weight_v, weight_f, block_f, wide, side, slabs, vels, vel_t,
        vz_s, vz_r, vy_s, vy_r, vc_s, vc_r, acc, moved, send, recv,
        load_sem, send_sem, recv_sem, store_sem, tile_send_sem, tile_recv_sem,
    ) = refs
    gy, gz = lax.axis_index("gy"), lax.axis_index("gz")
    loads = [
        pltpu.make_async_copy(src, dst, load_sem.at[i])
        for i, (src, dst) in enumerate(
            [
                (hid_hbm, hid_in),
                (vel_hbm, vel_f),
                (weight_hbm, weight_v),
                (cell_hbm, cell_v),
                (bias_hbm, bias_ref),
                (dec_hbm, dec_ref),
                *zip(tables_hbm, tables),
            ]
        )
    ]
    for load in loads:
        load.start()
    barrier = pltpu.get_barrier_semaphore()
    targets = [(around(gy, sy), around(gz, sz)) for sy, sz in HALO]
    for target in targets:
        pl.semaphore_signal(barrier, inc=1, device_id=target, device_id_type=MESH)

    def greet(d, carry):
        pl.semaphore_signal(barrier, inc=1, device_id=(around(gy, d), gz), device_id_type=MESH)
        pl.semaphore_signal(barrier, inc=1, device_id=(gy, around(gz, d)), device_id_type=MESH)
        return carry

    lax.fori_loop(2, RANKS - 1, greet, 0)
    vels[...] = jnp.zeros_like(vels)

    loads[0].wait()
    hid_f[...] = hid_in[...].astype(F32)
    loads[1].wait()

    def centre(y, carry):
        for z in range(2):
            for t in range(2):
                lanes = slice(128 * t, 128 * t + 128)
                rows = hid_f[pl.ds(y * 4 + 2 * t + z, 32, stride=32), :]
                slabs[y + 1, z + 1, 32:64, lanes] = rows.astype(BF16)
                vels[y + 1, z + 1, 0:3, lanes] = vel_f[pl.ds(y * 4 + 2 * t + z, 3, stride=32), :]
        return carry

    lax.fori_loop(0, 8, centre, 0)
    for z in range(2):
        for t in range(2):
            rows = vel_f[pl.ds(2 * t + z, 24, stride=4), :]
            rows = jnp.concatenate([rows, jnp.zeros((8, 128), F32)], 0)
            vz_s[z, :, 128 * t : 128 * t + 128] = rows.astype(BF16)
    for k in range(2):
        y = 1 + 7 * k
        vy_s[k] = jnp.concatenate([vels[y, 1], vels[y, 2]], 0).astype(BF16)
        for z in range(2):
            rows = jnp.concatenate([vels[y, z + 1], jnp.zeros((8, NX), F32)], 0)
            vc_s[2 * k + z] = rows.astype(BF16)

    pl.semaphore_wait(barrier, len(HALO) + 2 * (RANKS - 3))
    copies = []
    for i, (sy, sz) in enumerate(HALO):
        k, z = (1 + sy) // 2, (1 + sz) // 2
        src_y, dst_y = (pl.ds(1, 8), pl.ds(1, 8)) if sy == 0 else (pl.ds(1 + 7 * k, 1), pl.ds(9 - 9 * k, 1))
        src_z, dst_z = (pl.ds(1, 2), pl.ds(1, 2)) if sz == 0 else (pl.ds(1 + z, 1), pl.ds(3 - 3 * z, 1))
        if sy == 0:
            extra = (vz_s.at[z], vz_r.at[z])
        elif sz == 0:
            extra = (vy_s.at[k], vy_r.at[k])
        else:
            extra = (vc_s.at[2 * k + z], vc_r.at[2 * k + z])
        mids = pl.ds(32, 32)
        pair = []
        for n, (src, dst) in enumerate(
            [(slabs.at[src_y, src_z, mids], slabs.at[dst_y, dst_z, mids]), extra]
        ):
            pair.append(
                pltpu.make_async_remote_copy(
                    src_ref=src,
                    dst_ref=dst,
                    send_sem=send_sem.at[i, n],
                    recv_sem=recv_sem.at[i, n],
                    device_id=targets[i],
                    device_id_type=MESH,
                )
            )
            pair[-1].start()
        copies.append(pair)

    def fill(y, z):
        mid = slabs[y, z, 32:64, :].astype(F32)
        slabs[y, z, 0:32, :] = pltpu.roll(mid, 1, 1).astype(BF16)
        slabs[y, z, 64:96, :] = pltpu.roll(mid, NX - 1, 1).astype(BF16)
        v = vels[y, z]
        first = v + pltpu.roll(pltpu.roll(v, 1, 1), 3, 0)
        tile = jnp.concatenate([first, pltpu.roll(v, NX - 1, 1), jnp.ones((16, NX), F32)], 0)
        slabs[y, z, 96:128, :] = tile.astype(BF16)

    def fill_own(y, carry):
        fill(y, 1)
        fill(y, 2)
        return carry

    lax.fori_loop(1, 9, fill_own, 0)

    loads[2].wait()
    loads[4].wait()
    weight_f[0:945, :] = weight_v[...].astype(F32)
    block_f[96:128, :] = jnp.zeros((32, 128), F32)
    for dy in range(3):
        for dz in range(3):
            first = (9 * dy + 3 * dz) * 35
            for dx in range(3):
                at = first + 35 * dx
                block_f[32 * dx : 32 * dx + 32, :] = weight_f[at + 3 : at + 35, :]
                row = 96 + (3, 0, 8)[dx]
                block_f[row : row + 3, :] = weight_f[at : at + 3, :]
            if dy == 1 and dz == 1:
                rest = bias_ref[...]
                for part in range(3):
                    high = rest.astype(BF16).astype(F32)
                    block_f[112 + part : 113 + part, :] = high
                    rest = rest - high
            turned = block_f[...].T.astype(BF16)
            if dy == 1 and dz == 1:
                block_f[112:120, :] = jnp.zeros((8, 128), F32)
            if dz == 0:
                side[0, :, 128 * dy : 128 * dy + 128] = turned
            if dz == 2:
                side[1, :, 128 * dy : 128 * dy + 128] = turned
            for z in range(2):
                own = z + dz - 1
                if 0 <= own < 2:
                    at = (2 * dy + own) * 128
                    wide[128 * z : 128 * z + 128, at : at + 128] = turned

    def inner(y):
        acc[y] = dot(wide[...], slabs[pl.ds(y, 3), 1:3].reshape(6 * SLAB, NX))

    def inner_step(y, carry):
        inner(y)
        return carry

    lax.fori_loop(1, 7, inner_step, 0)

    for i in (6, 7):
        for copy in copies[i]:
            copy.wait_recv()
        k = (1 + HALO[i][0]) // 2
        rows = vy_r[k].astype(F32)
        y = 9 - 9 * k
        vels[y, 1] = rows[0:8]
        vels[y, 2] = rows[8:16]
        fill(y, 1)
        fill(y, 2)
    inner(0)
    inner(7)

    for i in range(6):
        for copy in copies[i]:
            copy.wait_recv()
    for z in range(2):
        to = 3 - 3 * z
        rows = vz_r[z].astype(F32)
        for t in range(2):
            vel_t[t] = rows[:, 128 * t : 128 * t + 128]
            for y in range(8):
                vels[y + 1, to, 0:3, 128 * t : 128 * t + 128] = vel_t[t, pl.ds(y, 3, stride=8), :]
        for k in range(2):
            vels[9 - 9 * k, to] = vc_r[2 * k + z].astype(F32)[0:8]

    def fill_outer(y, carry):
        fill(y, 0)
        fill(y, 3)
        return carry

    lax.fori_loop(0, 10, fill_outer, 0)

    loads[3].wait()
    loads[5].wait()

    def sigmoid(value):
        return 0.5 * jnp.tanh(0.5 * value) + 0.5

    def update(y, carry):
        for z in range(2):
            outer = slabs[pl.ds(y, 3), 3 * z].reshape(3 * SLAB, NX)
            gates = acc[y, 128 * z : 128 * z + 128, :] + dot(side[z], outer)
            hidden_parts = []
            for t in range(2):
                lanes = slice(128 * t, 128 * t + 128)
                rows = pl.ds(y * 4 + 2 * t + z, 32, stride=32)
                part = gates[:, lanes]
                cell = sigmoid(part[32:64]) * cell_v[rows, :] + sigmoid(part[0:32]) * jnp.tanh(part[64:96])
                hidden = sigmoid(part[96:128]) * jnp.tanh(cell)
                cell_v[rows, :] = cell
                hid_f[rows, :] = hidden
                hidden_parts.append(hidden.astype(BF16))
            increment = dot(dec_ref[...], jnp.concatenate(hidden_parts, 1))
            advanced = vels[y + 1, z + 1, 0:3, :] + increment
            for t in range(2):
                rows = pl.ds(pl.multiple_of(16 * y + 8 * z, 8), 3)
                moved[t, rows, :] = advanced[:, 128 * t : 128 * t + 128]
        return carry

    lax.fori_loop(0, 8, update, 0)
    for c in range(3):
        for z in range(2):
            for t in range(2):
                start = 16 * c + 8 * z
                u_ref[start : start + 8, 128 * t : 128 * t + 128] = moved[
                    t, pl.ds(8 * z + c, 8, stride=16), :
                ]
    cell_store = pltpu.make_async_copy(cell_v, cell_out, store_sem.at[0])
    cell_store.start()
    hid_in[...] = hid_f[...].astype(BF16)
    hid_store = pltpu.make_async_copy(hid_in, hid_out, store_sem.at[1])
    hid_store.start()
    for load in loads[6:]:
        load.wait()
    project(u_ref, tables, vel_next, send, recv, tile_send_sem, tile_recv_sem)
    vel_store = pltpu.make_async_copy(vel_next, vel_out, store_sem.at[2])
    vel_store.start()
    for pair in copies:
        for copy in pair:
            copy.wait_send()
    cell_store.wait()
    hid_store.wait()
    vel_store.wait()


def hand_on_kernel(*refs):
    sources, results, held, sem = refs[:3], refs[3:6], refs[6:9], refs[9]
    arrive = [pltpu.make_async_copy(a, b, sem.at[0, i]) for i, (a, b) in enumerate(zip(sources, held))]
    leave = [pltpu.make_async_copy(a, b, sem.at[1, i]) for i, (a, b) in enumerate(zip(held, results))]
    for copy in arrive:
        copy.start()
    for i in (2, 0, 1):
        arrive[i].wait()
        leave[i].start()
    for copy in leave:
        copy.wait()


def to_rows(array):
    c = array.shape[0]
    return array.reshape(c, 8, 2, 2, 128).transpose(0, 1, 3, 2, 4).reshape(c * 32, 128)


def from_rows(array):
    c = array.shape[0] // 32
    return array.reshape(c, 8, 2, 2, 128).transpose(0, 1, 3, 2, 4).reshape(c, 8, 2, 256)


def per_device(velocity, hidden, cell, gate_weight, gate_bias, decoder):
    anywhere = pl.BlockSpec(memory_space=pl.ANY)
    tables = [halves(t) for t in (*x_tables(), *y_tables(), *z_tables())]
    results = (
        jax.ShapeDtypeStruct((1024, 128), BF16),
        jax.ShapeDtypeStruct((1024, 128), F32),
        jax.ShapeDtypeStruct((96, 128), F32),
    )
    outs = pl.pallas_call(
        step_kernel,
        out_shape=results,
        in_specs=[anywhere] * 12,
        out_specs=(anywhere,) * 3,
        scratch_shapes=[
            *(pltpu.VMEM(t.shape, BF16) for t in tables),
            pltpu.VMEM((1, 128), F32),
            pltpu.VMEM((3, 32), BF16),
            pltpu.VMEM((48, 256), F32),
            pltpu.VMEM((96, 128), F32),
            pltpu.VMEM((1024, 128), BF16),
            pltpu.VMEM((1024, 128), F32),
            pltpu.VMEM((96, 128), F32),
            pltpu.VMEM((1024, 128), F32),
            pltpu.VMEM((945, 128), BF16),
            pltpu.VMEM((952, 128), F32),
            pltpu.VMEM((128, 128), F32),
            pltpu.VMEM((256, 768), BF16),
            pltpu.VMEM((2, 128, 384), BF16),
            pltpu.VMEM((10, 4, SLAB, NX), BF16),
            pltpu.VMEM((10, 4, 8, NX), F32),
            pltpu.VMEM((2, 32, 128), F32),
            pltpu.VMEM((2, 32, NX), BF16),
            pltpu.VMEM((2, 32, NX), BF16),
            pltpu.VMEM((2, 16, NX), BF16),
            pltpu.VMEM((2, 16, NX), BF16),
            pltpu.VMEM((4, 16, NX), BF16),
            pltpu.VMEM((4, 16, NX), BF16),
            pltpu.VMEM((8, 256, 256), F32),
            pltpu.VMEM((2, 128, 128), F32),
            pltpu.VMEM((4, RANKS, 8, 128), F32),
            pltpu.VMEM((4, RANKS, 8, 128), F32),
            pltpu.SemaphoreType.DMA((12,)),
            pltpu.SemaphoreType.DMA((8, 2)),
            pltpu.SemaphoreType.DMA((8, 2)),
            pltpu.SemaphoreType.DMA((3,)),
            pltpu.SemaphoreType.DMA((4,)),
            pltpu.SemaphoreType.DMA((4,)),
        ],
        compiler_params=pltpu.CompilerParams(
            collective_id=0, has_side_effects=True, vmem_limit_bytes=56 * 1024 * 1024
        ),
    )(
        to_rows(velocity),
        to_rows(hidden),
        to_rows(cell),
        gate_weight.T,
        gate_bias.reshape(1, 128),
        decoder,
        *(jnp.asarray(t) for t in tables),
    )
    outs = pl.pallas_call(
        hand_on_kernel,
        out_shape=results,
        in_specs=[anywhere] * 3,
        out_specs=(anywhere,) * 3,
        scratch_shapes=[*(pltpu.VMEM(r.shape, r.dtype) for r in results), pltpu.SemaphoreType.DMA((2, 3))],
        compiler_params=pltpu.CompilerParams(vmem_limit_bytes=56 * 1024 * 1024),
    )(*outs)
    return tuple(from_rows(out) for out in outs)


def solution(mesh):
    field = P(None, "gy", "gz", None)
    return jax.shard_map(
        per_device,
        mesh=mesh,
        in_specs=(field, field, field, P(), P(), P()),
        out_specs=(field, field, field),
        check_vma=False,
    )
```

```python
import functools

import jax
import jax.numpy as jnp
import numpy as np
from jax import lax
from jax.experimental import pallas as pl
from jax.experimental.pallas import tpu as pltpu
from jax.sharding import PartitionSpec as P

F32 = jnp.float32
BF16 = jnp.bfloat16
MESH = pl.DeviceIdType.MESH
NX, NY, NZ = 256, 128, 32
RANKS = 16
SLAB = 128
HALO = [(sy, sz) for sz in (-1, 1) for sy in (0, -1, 1)] + [(-1, 0), (1, 0)]


def halves(table):
    high = table.astype(np.float32).astype(jnp.bfloat16)
    low = (table - high.astype(np.float64)).astype(np.float32).astype(jnp.bfloat16)
    pair = np.stack([np.asarray(high), np.asarray(low)])
    if table.shape[1] == 256:
        pair = pair.reshape(2, -1, 2, 128).transpose(0, 2, 1, 3)
    return np.ascontiguousarray(pair)


def signed_waves(total):
    index = np.arange(total)
    wave = np.where(index < total // 2, index, index - total)
    return np.where(index == total // 2, 0, wave).astype(np.float64)


def x_tables():
    lane = np.arange(128)
    mode = (lane % 16) * 8 + lane // 16
    n = np.arange(NX)
    angle = 2 * np.pi / NX * ((n[:, None] * mode[None, :]) % NX)
    sign = np.where(n % 2 == 0, 1.0, -1.0)
    imag = np.where(mode[None, :] == 0, sign[:, None], -np.sin(angle))
    forward = np.concatenate([np.cos(angle), imag], 1)
    weight = np.where(mode == 0, 1.0, 2.0)
    inverse = forward.T * np.concatenate([weight, weight])[:, None]
    return forward, inverse


def y_tables():
    lane = np.arange(128)
    mode = (lane % 16) * 8 + lane // 16
    y = np.arange(NY)
    angle = 2 * np.pi / NY * ((y[:, None] * mode[None, :]) % NY)
    forward = np.concatenate([np.cos(angle), np.sin(angle)], 0)
    inverse = np.concatenate([np.cos(angle).T, np.sin(angle).T], 0)
    return forward, inverse


def z_tables():
    kz = np.arange(NZ)
    z = np.arange(NZ)
    wave = signed_waves(NZ)[:, None]
    angle = 2 * np.pi / NZ * ((kz[:, None] * z[None, :]) % NZ)
    cosine, sine = np.cos(angle), np.sin(angle)
    forward = np.zeros((2, NZ, RANKS, 2, 2, 2))
    inverse = np.zeros((RANKS, 2, 2, 2, 2, NZ))
    for own in range(2):
        c, s = cosine[:, own::2], sine[:, own::2]
        for field, scale in ((0, np.ones_like(wave)), (1, wave)):
            forward[0, :, :, field, own, 0] = scale * c
            forward[0, :, :, field, own, 1] = scale * s
            forward[1, :, :, field, own, 1] = scale * c
            forward[1, :, :, field, own, 0] = -scale * s
            inverse[:, field, own, 0, 0, :] = (scale * c).T
            inverse[:, field, own, 0, 1, :] = -(scale * s).T
            inverse[:, field, own, 1, 1, :] = (scale * c).T
            inverse[:, field, own, 1, 0, :] = (scale * s).T
    return forward.reshape(64, 128), inverse.reshape(128, 64)


def split(value):
    high = value.astype(BF16)
    return high, (value - high.astype(F32)).astype(BF16)


def dot(a, b):
    return jnp.dot(a, b, preferred_element_type=F32)


def whole(table):
    if len(table.shape) == 3:
        return [table[0], table[1]]
    return [jnp.concatenate([table[part, 0], table[part, 1]], 1) for part in range(2)]


def data_by_table(value, table):
    table = whole(table)
    high, low = split(value)
    return dot(high, table[0]) + (dot(low, table[0]) + dot(high, table[1]))


def table_by_data(table, value):
    high, low = split(value)
    return dot(table[0], high) + (dot(table[0], low) + dot(table[1], high))


def roll_lanes(value, shift):
    return value if shift % 128 == 0 else pltpu.roll(value, shift % 128, 1)


def roll_rows(value, shift):
    return pltpu.roll(value, shift % value.shape[0], 0)


def lane_ids():
    return lax.broadcasted_iota(jnp.int32, (8, 128), 1)


def lane_mix(values, count):
    low = lane_ids() % 16
    masks = [low == q for q in range(16)]
    rolled = [roll_lanes(v, r) for r, v in enumerate(values)]
    outs = []
    for j in range(count):
        acc = jnp.zeros((8, 128), F32)
        for r, v in enumerate(rolled):
            acc = jnp.where(masks[(j + r) % 16], v, acc)
        outs.append(roll_lanes(acc, -j))
    return outs


def wave_of(index, total):
    wave = jnp.where(index < total // 2, index, index - total)
    return jnp.where(index == total // 2, 0, wave).astype(F32)


def mode_waves(total):
    lane = lane_ids()
    return wave_of((lane % 16) * 8 + lane // 16, total)


def x_forward(rows, table):
    spectrum = data_by_table(rows, table)
    kx = mode_waves(2 * NX)

    def part(c, z, p):
        start = (2 * c + z) * 8
        return spectrum[start : start + 8, 128 * p : 128 * p + 128]

    values = []
    for c in (0, 2, 1):
        for z in range(2):
            for p in range(2):
                values.append(part(c, z, p) * kx if c == 0 else part(c, z, p))
    return lane_mix(values, RANKS)


def swapped(value, sign):
    even = lax.broadcasted_iota(jnp.int32, value.shape, 0) % 2 == 0
    return jnp.where(even, sign * roll_rows(value, -1), -sign * roll_rows(value, 1))


def y_forward(tiles, table):
    rows = tiles.T
    out = data_by_table(jnp.concatenate([rows, swapped(rows, 1.0)], 1), table)
    ky = mode_waves(NY)
    values = [out[16 * k : 16 * k + 8] + ky * out[16 * k + 8 : 16 * k + 16] for k in range(8)]
    return lane_mix(values, RANKS)


def z_both(tiles, forward, inverse, me_gy, me_gz):
    numer = table_by_data(forward, tiles)
    lane = lax.broadcasted_iota(jnp.int32, (NZ, 128), 1)
    kx = (me_gy * 8 + lane % 8).astype(F32)
    ky = wave_of(me_gz * 8 + lane // 16, NY)
    kz = wave_of(lax.broadcasted_iota(jnp.int32, (NZ, 128), 0), NZ)
    factor = (1.0 / (NX * NY * NZ)) / jnp.maximum(kx * kx + ky * ky + kz * kz, 1.0)
    return table_by_data(inverse, numer * jnp.concatenate([factor, factor], 0))


def y_inverse(tiles, table):
    values = lane_mix(tiles, 8)
    ky = mode_waves(NY)
    rows = []
    for v in values:
        rows += [v, v * ky]
    rows = jnp.concatenate(rows, 0)
    out = data_by_table(jnp.concatenate([rows, swapped(rows, -1.0)], 1), table)
    return out.T


def x_inverse(tiles, table):
    values = lane_mix(tiles, 12)
    kx = mode_waves(2 * NX)
    rows = []
    for c, base in ((0, 0), (1, 8), (2, 4)):
        for z in range(2):
            pair = [values[base + 2 * z + p] for p in range(2)]
            if c == 0:
                pair = [v * kx for v in pair]
            rows.append(jnp.concatenate(pair, 1))
    return data_by_table(jnp.concatenate(rows, 0), table)


def around(index, step):
    return lax.rem(index + step + RANKS, RANKS)


def project(u_ref, tables, out_ref, send, recv, send_sem, recv_sem, meanwhile):
    gy, gz = lax.axis_index("gy"), lax.axis_index("gz")
    xf_ref, xi_ref, yf_ref, yi_ref, zf_ref, zi_ref = tables

    def exchange(step, along_y, meanwhile=None):
        me = gy if along_y else gz

        def start(d, carry):
            to = around(me, d)
            target = (to, gz) if along_y else (gy, to)
            pltpu.make_async_remote_copy(
                src_ref=send.at[step, to],
                dst_ref=recv.at[step, me],
                send_sem=send_sem.at[step],
                recv_sem=recv_sem.at[step],
                device_id=target,
                device_id_type=MESH,
            ).start()
            return carry

        lax.fori_loop(1, RANKS, start, 0)
        recv[step, pl.ds(me, 1)] = send[step, pl.ds(me, 1)]
        if meanwhile is not None:
            meanwhile()
        some = recv.at[step, pl.ds(0, RANKS - 1)]
        pltpu.make_async_copy(some, some, recv_sem.at[step]).wait()

    tiles = x_forward(u_ref[...], xf_ref)
    for j in range(RANKS):
        send[0, j] = tiles[j]
    exchange(0, True, meanwhile)
    tiles = y_forward(recv[0].reshape(128, 128), yf_ref)
    for j in range(RANKS):
        send[1, j] = tiles[j]
    exchange(1, False)
    send[2] = z_both(recv[1].reshape(128, 128), zf_ref, zi_ref, gy, gz).reshape(RANKS, 8, 128)
    exchange(2, False)
    send[3] = y_inverse([recv[2, j] for j in range(RANKS)], yi_ref).reshape(RANKS, 8, 128)
    exchange(3, True)
    gradient = x_inverse([recv[3, j] for j in range(RANKS)], xi_ref)
    result = u_ref[...] - gradient
    for c in range(3):
        for z in range(2):
            start = (2 * c + z) * 8
            for t in range(2):
                out_ref[pl.ds(c * 32 + 2 * t + z, 8, stride=4), :] = result[
                    start : start + 8, 128 * t : 128 * t + 128
                ]
    for step in range(4):
        some = send.at[step, pl.ds(0, RANKS - 1)]
        pltpu.make_async_copy(some, some, send_sem.at[step]).wait()


def step_kernel(
    vel_hbm, hid_hbm, cell_hbm, weight_hbm, bias_hbm, dec_hbm, *refs,
):
    tables_hbm, (hid_out, cell_out, vel_out) = refs[:6], refs[6:9]
    tables, refs = refs[9:15], refs[15:]
    (
        bias_ref, dec_ref, u_ref, vel_next,
        hid_in, hid_f, vel_f, cell_v, weight_v, weight_f, block_f, wide, side, slabs, vels, vel_t,
        vz_s, vz_r, vy_s, vy_r, vc_s, vc_r, acc, cells, hids, moved, send, recv,
        load_sem, send_sem, recv_sem, store_sem, tile_send_sem, tile_recv_sem,
    ) = refs
    gy, gz = lax.axis_index("gy"), lax.axis_index("gz")
    loads = [
        pltpu.make_async_copy(src, dst, load_sem.at[i])
        for i, (src, dst) in enumerate(
            [
                (hid_hbm, hid_in),
                (vel_hbm, vel_f),
                (weight_hbm, weight_v),
                (cell_hbm, cell_v),
                (bias_hbm, bias_ref),
                (dec_hbm, dec_ref),
                *zip(tables_hbm, tables),
            ]
        )
    ]
    for load in loads:
        load.start()
    barrier = pltpu.get_barrier_semaphore()
    targets = [(around(gy, sy), around(gz, sz)) for sy, sz in HALO]
    for target in targets:
        pl.semaphore_signal(barrier, inc=1, device_id=target, device_id_type=MESH)

    def greet(d, carry):
        pl.semaphore_signal(barrier, inc=1, device_id=(around(gy, d), gz), device_id_type=MESH)
        pl.semaphore_signal(barrier, inc=1, device_id=(gy, around(gz, d)), device_id_type=MESH)
        return carry

    lax.fori_loop(2, RANKS - 1, greet, 0)
    vels[...] = jnp.zeros_like(vels)

    loads[0].wait()
    hid_f[...] = hid_in[...].astype(F32)
    loads[1].wait()

    def centre(y, carry):
        for z in range(2):
            for t in range(2):
                lanes = slice(128 * t, 128 * t + 128)
                rows = hid_f[pl.ds(y * 4 + 2 * t + z, 32, stride=32), :]
                slabs[y + 1, z + 1, 32:64, lanes] = rows.astype(BF16)
                vels[y + 1, z + 1, 0:3, lanes] = vel_f[pl.ds(y * 4 + 2 * t + z, 3, stride=32), :]
        return carry

    lax.fori_loop(0, 8, centre, 0)
    for z in range(2):
        for t in range(2):
            rows = vel_f[pl.ds(2 * t + z, 24, stride=4), :]
            rows = jnp.concatenate([rows, jnp.zeros((8, 128), F32)], 0)
            vz_s[z, :, 128 * t : 128 * t + 128] = rows.astype(BF16)
    for k in range(2):
        y = 1 + 7 * k
        vy_s[k] = jnp.concatenate([vels[y, 1], vels[y, 2]], 0).astype(BF16)
        for z in range(2):
            rows = jnp.concatenate([vels[y, z + 1], jnp.zeros((8, NX), F32)], 0)
            vc_s[2 * k + z] = rows.astype(BF16)

    pl.semaphore_wait(barrier, len(HALO) + 2 * (RANKS - 3))
    copies = {}

    def start_halo(name, i, n, src, dst):
        copies[name] = pltpu.make_async_remote_copy(
            src_ref=src,
            dst_ref=dst,
            send_sem=send_sem.at[i, n],
            recv_sem=recv_sem.at[i, n],
            device_id=targets[i],
            device_id_type=MESH,
        )
        copies[name].start()

    mids = pl.ds(32, 32)

    def send_plane(part):
        for i, (sy, sz) in enumerate(HALO):
            if sy == 0:
                z = (1 + sz) // 2
                ys = pl.ds(1 + 4 * part, 4)
                src, dst = slabs.at[ys, z + 1, mids], slabs.at[ys, 3 - 3 * z, mids]
                start_halo(("plane", z, part), i, part, src, dst)

    def send_edge(i):
        sy, sz = HALO[i]
        k, z = (1 + sy) // 2, (1 + sz) // 2
        if sz == 0:
            src, dst = slabs.at[1 + 7 * k, pl.ds(1, 2), mids], slabs.at[9 - 9 * k, pl.ds(1, 2), mids]
            start_halo(("edge", k, 0), i, 0, src, dst)
            start_halo(("edge", k, 1), i, 1, vy_s.at[k], vy_r.at[k])
        else:
            src, dst = slabs.at[1 + 7 * k, 1 + z, mids], slabs.at[9 - 9 * k, 3 - 3 * z, mids]
            start_halo(("corner", k, z, 0), i, 0, src, dst)
            start_halo(("corner", k, z, 1), i, 1, vc_s.at[2 * k + z], vc_r.at[2 * k + z])

    send_plane(0)
    for i, (sy, sz) in enumerate(HALO):
        if sy == 0:
            z = (1 + sz) // 2
            start_halo(("side", z), i, 2, vz_s.at[z], vz_r.at[z])
    for wanted in ((1, True), (-1, False), (1, False)):
        for i, (sy, sz) in enumerate(HALO):
            if (sy, sz != 0) == wanted:
                send_edge(i)
    send_plane(1)
    for i, (sy, sz) in enumerate(HALO):
        if sy == -1 and sz != 0:
            send_edge(i)

    def fill(y, z):
        mid = slabs[y, z, 32:64, :].astype(F32)
        slabs[y, z, 0:32, :] = pltpu.roll(mid, 1, 1).astype(BF16)
        slabs[y, z, 64:96, :] = pltpu.roll(mid, NX - 1, 1).astype(BF16)
        v = vels[y, z]
        first = v + pltpu.roll(pltpu.roll(v, 1, 1), 3, 0)
        tile = jnp.concatenate([first, pltpu.roll(v, NX - 1, 1), jnp.ones((16, NX), F32)], 0)
        slabs[y, z, 96:128, :] = tile.astype(BF16)

    def fill_own(y, carry):
        fill(y, 1)
        fill(y, 2)
        return carry

    lax.fori_loop(1, 9, fill_own, 0)

    loads[2].wait()
    loads[4].wait()
    weight_f[0:945, :] = weight_v[...].astype(F32)
    block_f[96:128, :] = jnp.zeros((32, 128), F32)
    gate = lax.broadcasted_iota(jnp.int32, (128, 128), 0)
    gate_scale = jnp.where((gate >= 64) & (gate < 96), 1.0, 0.5)
    for dy in range(3):
        for dz in range(3):
            first = (9 * dy + 3 * dz) * 35
            for dx in range(3):
                at = first + 35 * dx
                block_f[32 * dx : 32 * dx + 32, :] = weight_f[at + 3 : at + 35, :]
                row = 96 + (3, 0, 8)[dx]
                block_f[row : row + 3, :] = weight_f[at : at + 3, :]
            if dy == 1 and dz == 1:
                rest = bias_ref[...]
                for part in range(3):
                    high = rest.astype(BF16).astype(F32)
                    block_f[112 + part : 113 + part, :] = high
                    rest = rest - high
            turned = (block_f[...].T * gate_scale).astype(BF16)
            if dy == 1 and dz == 1:
                block_f[112:120, :] = jnp.zeros((8, 128), F32)
            if dz == 0:
                side[0, :, 128 * dy : 128 * dy + 128] = turned
            if dz == 2:
                side[1, :, 128 * dy : 128 * dy + 128] = turned
            for z in range(2):
                own = z + dz - 1
                if 0 <= own < 2:
                    at = (2 * dy + own) * 128
                    wide[128 * z : 128 * z + 128, at : at + 128] = turned

    def inner(y):
        acc[y] = dot(wide[...], slabs[pl.ds(y, 3), 1:3].reshape(6 * SLAB, NX))

    def inner_step(y, carry):
        inner(y)
        return carry

    lax.fori_loop(1, 7, inner_step, 0)

    loads[3].wait()
    loads[5].wait()

    def own_cells(y, carry):
        for z in range(2):
            for t in range(2):
                cells[y, z, :, 128 * t : 128 * t + 128] = cell_v[
                    pl.ds(y * 4 + 2 * t + z, 32, stride=32), :
                ]
        return carry

    lax.fori_loop(0, 8, own_cells, 0)

    for k in range(2):
        copies["edge", k, 0].wait_recv()
        copies["edge", k, 1].wait_recv()
        rows = vy_r[k].astype(F32)
        y = 9 - 9 * k
        vels[y, 1] = rows[0:8]
        vels[y, 2] = rows[8:16]
        fill(y, 1)
        fill(y, 2)
    inner(0)
    inner(7)

    def update(y, carry):
        for z in range(2):
            outer = slabs[pl.ds(y, 3), 3 * z].reshape(3 * SLAB, NX)
            gates = acc[y, 128 * z : 128 * z + 128, :] + dot(side[z], outer)
            turned = jnp.tanh(gates)
            new = 0.5 * (
                (turned[32:64] + 1.0) * cells[y, z] + (turned[0:32] + 1.0) * turned[64:96]
            )
            cells[y, z] = new
            hids[y, z] = (0.5 * (turned[96:128] + 1.0) * jnp.tanh(new)).astype(BF16)
        return carry

    def fill_outer(y, carry):
        fill(y, 0)
        fill(y, 3)
        return carry

    for z in range(2):
        copies["side", z].wait_recv()
        to = 3 - 3 * z
        rows = vz_r[z].astype(F32)
        for t in range(2):
            vel_t[t] = rows[:, 128 * t : 128 * t + 128]
            for y in range(8):
                vels[y + 1, to, 0:3, 128 * t : 128 * t + 128] = vel_t[t, pl.ds(y, 3, stride=8), :]
    for part, ys, rows in ((0, (0, 5), (0, 3)), (1, (5, 10), (3, 8))):
        k = 1 - part
        for z in range(2):
            copies["plane", z, part].wait_recv()
            copies["corner", k, z, 0].wait_recv()
            copies["corner", k, z, 1].wait_recv()
            vels[9 - 9 * k, 3 - 3 * z] = vc_r[2 * k + z].astype(F32)[0:8]
        lax.fori_loop(*ys, fill_outer, 0)
        lax.fori_loop(*rows, update, 0)

    for y in range(8):
        for z in range(2):
            advanced = vels[y + 1, z + 1, 0:3, :] + dot(dec_ref[...], hids[y, z])
            for t in range(2):
                at = 16 * y + 8 * z
                moved[t, at : at + 3, :] = advanced[:, 128 * t : 128 * t + 128]
    for c in range(3):
        for z in range(2):
            for t in range(2):
                start = 16 * c + 8 * z
                u_ref[start : start + 8, 128 * t : 128 * t + 128] = moved[
                    t, pl.ds(8 * z + c, 8, stride=16), :
                ]

    cell_store = pltpu.make_async_copy(cell_v, cell_out, store_sem.at[0])
    hid_store = pltpu.make_async_copy(hid_in, hid_out, store_sem.at[1])

    def store_states():
        def turn(y, carry):
            for z in range(2):
                for t in range(2):
                    rows = pl.ds(y * 4 + 2 * t + z, 32, stride=32)
                    lanes = slice(128 * t, 128 * t + 128)
                    cell_v[rows, :] = cells[y, z, :, lanes]
                    hid_f[rows, :] = hids[y, z, :, lanes].astype(F32)
            return carry

        lax.fori_loop(0, 8, turn, 0)
        cell_store.start()
        hid_in[...] = hid_f[...].astype(BF16)
        hid_store.start()

    for load in loads[6:]:
        load.wait()
    project(u_ref, tables, vel_next, send, recv, tile_send_sem, tile_recv_sem, store_states)
    vel_store = pltpu.make_async_copy(vel_next, vel_out, store_sem.at[2])
    vel_store.start()
    for copy in copies.values():
        copy.wait_send()
    cell_store.wait()
    hid_store.wait()
    vel_store.wait()


def hand_on_kernel(*refs):
    sources, results, held, sem = refs[:3], refs[3:6], refs[6:9], refs[9]
    arrive = [pltpu.make_async_copy(a, b, sem.at[0, i]) for i, (a, b) in enumerate(zip(sources, held))]
    leave = [pltpu.make_async_copy(a, b, sem.at[1, i]) for i, (a, b) in enumerate(zip(held, results))]
    for copy in arrive:
        copy.start()
    for i in (2, 0, 1):
        arrive[i].wait()
        leave[i].start()
    for copy in leave:
        copy.wait()


def to_rows(array):
    c = array.shape[0]
    return array.reshape(c, 8, 2, 2, 128).transpose(0, 1, 3, 2, 4).reshape(c * 32, 128)


def from_rows(array):
    c = array.shape[0] // 32
    return array.reshape(c, 8, 2, 2, 128).transpose(0, 1, 3, 2, 4).reshape(c, 8, 2, 256)


def per_device(velocity, hidden, cell, gate_weight, gate_bias, decoder):
    anywhere = pl.BlockSpec(memory_space=pl.ANY)
    tables = [halves(t) for t in (*x_tables(), *y_tables(), *z_tables())]
    results = (
        jax.ShapeDtypeStruct((1024, 128), BF16),
        jax.ShapeDtypeStruct((1024, 128), F32),
        jax.ShapeDtypeStruct((96, 128), F32),
    )
    outs = pl.pallas_call(
        step_kernel,
        out_shape=results,
        in_specs=[anywhere] * 12,
        out_specs=(anywhere,) * 3,
        scratch_shapes=[
            *(pltpu.VMEM(t.shape, BF16) for t in tables),
            pltpu.VMEM((1, 128), F32),
            pltpu.VMEM((3, 32), BF16),
            pltpu.VMEM((48, 256), F32),
            pltpu.VMEM((96, 128), F32),
            pltpu.VMEM((1024, 128), BF16),
            pltpu.VMEM((1024, 128), F32),
            pltpu.VMEM((96, 128), F32),
            pltpu.VMEM((1024, 128), F32),
            pltpu.VMEM((945, 128), BF16),
            pltpu.VMEM((952, 128), F32),
            pltpu.VMEM((128, 128), F32),
            pltpu.VMEM((256, 768), BF16),
            pltpu.VMEM((2, 128, 384), BF16),
            pltpu.VMEM((10, 4, SLAB, NX), BF16),
            pltpu.VMEM((10, 4, 8, NX), F32),
            pltpu.VMEM((2, 32, 128), F32),
            pltpu.VMEM((2, 32, NX), BF16),
            pltpu.VMEM((2, 32, NX), BF16),
            pltpu.VMEM((2, 16, NX), BF16),
            pltpu.VMEM((2, 16, NX), BF16),
            pltpu.VMEM((4, 16, NX), BF16),
            pltpu.VMEM((4, 16, NX), BF16),
            pltpu.VMEM((8, 256, 256), F32),
            pltpu.VMEM((8, 2, 32, NX), F32),
            pltpu.VMEM((8, 2, 32, NX), BF16),
            pltpu.VMEM((2, 128, 128), F32),
            pltpu.VMEM((4, RANKS, 8, 128), F32),
            pltpu.VMEM((4, RANKS, 8, 128), F32),
            pltpu.SemaphoreType.DMA((12,)),
            pltpu.SemaphoreType.DMA((8, 3)),
            pltpu.SemaphoreType.DMA((8, 3)),
            pltpu.SemaphoreType.DMA((3,)),
            pltpu.SemaphoreType.DMA((4,)),
            pltpu.SemaphoreType.DMA((4,)),
        ],
        compiler_params=pltpu.CompilerParams(
            collective_id=0, has_side_effects=True, vmem_limit_bytes=56 * 1024 * 1024
        ),
    )(
        to_rows(velocity),
        to_rows(hidden),
        to_rows(cell),
        gate_weight.T,
        gate_bias.reshape(1, 128),
        decoder,
        *(jnp.asarray(t) for t in tables),
    )
    outs = pl.pallas_call(
        hand_on_kernel,
        out_shape=results,
        in_specs=[anywhere] * 3,
        out_specs=(anywhere,) * 3,
        scratch_shapes=[*(pltpu.VMEM(r.shape, r.dtype) for r in results), pltpu.SemaphoreType.DMA((2, 3))],
        compiler_params=pltpu.CompilerParams(vmem_limit_bytes=56 * 1024 * 1024),
    )(*outs)
    return tuple(from_rows(out) for out in outs)


def solution(mesh):
    field = P(None, "gy", "gz", None)
    return jax.shard_map(
        per_device,
        mesh=mesh,
        in_specs=(field, field, field, P(), P(), P()),
        out_specs=(field, field, field),
        check_vma=False,
    )
```

```python
import functools

import jax
import jax.numpy as jnp
import numpy as np
from jax import lax
from jax.experimental import pallas as pl
from jax.experimental.pallas import tpu as pltpu
from jax.sharding import PartitionSpec as P

F32 = jnp.float32
BF16 = jnp.bfloat16
MESH = pl.DeviceIdType.MESH
NX, NY, NZ = 256, 128, 32
RANKS = 16
SLAB = 128
HALO = [(sy, sz) for sz in (-1, 1) for sy in (0, -1, 1)] + [(-1, 0), (1, 0)]


def halves(table):
    high = table.astype(np.float32).astype(jnp.bfloat16)
    low = (table - high.astype(np.float64)).astype(np.float32).astype(jnp.bfloat16)
    pair = np.stack([np.asarray(high), np.asarray(low)])
    if table.shape[1] == 256:
        pair = pair.reshape(2, -1, 2, 128).transpose(0, 2, 1, 3)
    return np.ascontiguousarray(pair)


def x_tables():
    mode = np.arange(128)
    n = np.arange(NX)
    angle = 2 * np.pi / NX * ((n[:, None] * mode[None, :]) % NX)
    sign = np.where(n % 2 == 0, 1.0, -1.0)
    imag = np.where(mode[None, :] == 0, sign[:, None], -np.sin(angle))
    forward = np.concatenate([np.cos(angle), imag], 1)
    weight = np.where(mode == 0, 1.0, 2.0) / NX
    inverse = forward.T * np.concatenate([weight, weight])[:, None]
    return forward, inverse


def real_waves(total):
    half = total // 2
    index = np.arange(total)
    return np.where(index < half, index, index - half).astype(np.float64)


def real_tables(total):
    half = total // 2
    cosines, sines = np.arange(half + 1), np.arange(1, half)
    place = np.arange(total)
    angle = 2 * np.pi / total * ((np.concatenate([cosines, sines])[:, None] * place[None, :]) % total)
    is_sine = np.arange(total)[:, None] > half
    analysis = np.where(is_sine, np.sin(angle), np.cos(angle))
    weight = np.full(total, 2.0 / total)
    weight[0] = weight[half] = 1.0 / total
    synthesis = analysis.T * weight[None, :]
    derivative = np.zeros((total, total))
    for k in range(1, half):
        derivative[k, half + k] = k
        derivative[half + k, k] = -k
    return analysis, synthesis, derivative


def y_tables():
    analysis, synthesis, derivative = real_tables(NY)
    forward = np.concatenate([analysis, derivative @ analysis], 0)
    inverse = np.concatenate([synthesis, -(synthesis @ derivative)], 0)
    return forward, inverse


def z_tables():
    analysis, synthesis, derivative = real_tables(NZ)
    lane = np.arange(NZ)
    z = (lane // 8 % 2) * 16 + (lane % 4) * 4 + (lane // 4 % 2) * 2 + lane // 16
    forward, inverse = np.zeros((128, 128)), np.zeros((128, 128))
    for c in range(3):
        lanes = slice(32 * c, 32 * c + 32)
        forward[lanes, :32] = (derivative @ analysis if c == 2 else analysis)[:, z].T
        inverse[:32, lanes] = (-(synthesis @ derivative) if c == 2 else synthesis)[z, :].T
    return forward, inverse


def split(value):
    high = value.astype(BF16)
    return high, (value - high.astype(F32)).astype(BF16)


def dot(a, b):
    return jnp.dot(a, b, preferred_element_type=F32)


def whole(table):
    if len(table.shape) == 3:
        return [table[0], table[1]]
    return [jnp.concatenate([table[part, 0], table[part, 1]], 1) for part in range(2)]


def data_by_table(value, table):
    table = whole(table)
    high, low = split(value)
    return dot(high, table[0]) + (dot(low, table[0]) + dot(high, table[1]))


def table_by_data(table, value):
    high, low = split(value)
    return dot(table[0], high) + (dot(table[0], low) + dot(table[1], high))


def roll_lanes(value, shift):
    return value if shift % 128 == 0 else pltpu.roll(value, shift % 128, 1)


def lane_mix(values, count, stride, base):
    digit = lax.broadcasted_iota(jnp.int32, (8, 128), 1) // stride % base
    masks = [digit == q for q in range(base)]
    rolled = [roll_lanes(v, r * stride) for r, v in enumerate(values)]
    outs = []
    for j in range(count):
        acc = rolled[0] if len(values) == base else jnp.zeros((8, 128), F32)
        for r, v in enumerate(rolled):
            if r or len(values) < base:
                acc = jnp.where(masks[(j + r) % base], v, acc)
        outs.append(roll_lanes(acc, -j * stride))
    return outs


def x_forward(rows, table):
    spectrum = data_by_table(rows, table)
    values = []
    for cz in range(6):
        part = [spectrum[8 * cz : 8 * cz + 8, 128 * p : 128 * p + 128] for p in range(2)]
        values += [-part[1], part[0]] if cz < 2 else part
    return lane_mix(values, RANKS, 8, 16)


def solve(tiles, yf_ref, yi_ref, zf_ref, zi_ref, wave_x):
    def swap(blocks, first_of, second_of):
        out = [None] * 16
        for low in range(4):
            mixed = lane_mix([blocks[first_of(low, i)] for i in range(4)], 4, 4, 4)
            for i in range(4):
                out[second_of(low, i)] = mixed[i]
        return out

    def by_source(low, i):
        return (i // 2) * 8 + low * 2 + i % 2

    def by_y(low, i):
        return i * 4 + low

    lane = lax.broadcasted_iota(jnp.int32, (NY, 128), 1)
    is_y = (lane >= 32) & (lane < 64)
    scale = jnp.where(lane < 32, wave_x, 1.0)
    rows = jnp.concatenate(swap(tiles, by_source, by_y), 0)
    out = table_by_data(yf_ref, rows)
    terms = jnp.where(is_y, out[NY:], out[:NY]) * scale
    divergence = data_by_table(terms, zf_ref)
    row = lax.broadcasted_iota(jnp.int32, (NY, 128), 0)
    wave_y = jnp.where(row < NY // 2, row, row - NY // 2).astype(F32)
    wave_z = jnp.where(lane < NZ // 2, lane, lane - NZ // 2).astype(F32)
    square = wave_x * wave_x + wave_y * wave_y + wave_z * wave_z
    potential = divergence / jnp.maximum(square, 1.0)
    out = table_by_data(yi_ref, data_by_table(potential, zi_ref))
    rows = jnp.where(is_y, out[NY:], out[:NY]) * scale
    return swap([rows[8 * i : 8 * i + 8] for i in range(16)], by_y, by_source)


def x_inverse(tiles, table):
    values = lane_mix(tiles, 12, 8, 16)
    rows = []
    for cz in range(6):
        pair = values[2 * cz : 2 * cz + 2]
        rows.append(jnp.concatenate([pair[1], -pair[0]] if cz < 2 else pair, 1))
    return data_by_table(jnp.concatenate(rows, 0), table)


def around(index, step):
    return lax.rem(index + step + RANKS, RANKS)


def positions():
    gy, gz = lax.axis_index("gy"), lax.axis_index("gz")
    y, z_low, z_high, x, core = gy // 4, gy % 4, gz // 8, gz // 2 % 4, gz % 2

    def first(index):
        return (index // 4 * 4 + z_low, z_high * 8 + index % 4 * 2 + core)

    def second(index):
        return (y * 4 + index // 2 % 4, index // 8 * 8 + x * 2 + index % 2)

    return (y * 4 + x, first), (z_high * 8 + z_low * 2 + core, second)


def project(u_ref, tables, out_ref, send, recv, send_sem, recv_sem, meanwhile):
    xf_ref, xi_ref, yf_ref, yi_ref, zf_ref, zi_ref = tables
    group_1, group_2 = positions()

    def exchange(step, group, tiles, meanwhile=None):
        me, place = group
        for j in range(RANKS):
            send[step, j] = tiles[j]

        def start(d, carry):
            to = around(me, d)
            pltpu.make_async_remote_copy(
                src_ref=send.at[step, to],
                dst_ref=recv.at[step, me],
                send_sem=send_sem.at[step],
                recv_sem=recv_sem.at[step],
                device_id=place(to),
                device_id_type=MESH,
            ).start()
            return carry

        lax.fori_loop(1, RANKS, start, 0)
        recv[step, pl.ds(me, 1)] = send[step, pl.ds(me, 1)]
        if meanwhile is not None:
            meanwhile()
        some = recv.at[step, pl.ds(0, RANKS - 1)]
        pltpu.make_async_copy(some, some, recv_sem.at[step]).wait()
        return [recv[step, j] for j in range(RANKS)]

    tiles = exchange(0, group_1, x_forward(u_ref[...], xf_ref), meanwhile)
    tiles = exchange(1, group_2, lane_mix(tiles, RANKS, 1, 16))
    wave_x = (group_1[0] * 8 + group_2[0] % 8).astype(F32)
    tiles = exchange(2, group_2, solve(tiles, yf_ref, yi_ref, zf_ref, zi_ref, wave_x))
    tiles = exchange(3, group_1, lane_mix(tiles, RANKS, 1, 16))
    gradient = x_inverse(tiles, xi_ref)
    result = u_ref[...] - gradient
    for c in range(3):
        for z in range(2):
            start = (2 * c + z) * 8
            for t in range(2):
                out_ref[pl.ds(c * 32 + 2 * t + z, 8, stride=4), :] = result[
                    start : start + 8, 128 * t : 128 * t + 128
                ]
    for step in range(4):
        some = send.at[step, pl.ds(0, RANKS - 1)]
        pltpu.make_async_copy(some, some, send_sem.at[step]).wait()


def step_kernel(
    vel_hbm, hid_hbm, cell_hbm, weight_hbm, bias_hbm, dec_hbm, *refs,
):
    tables_hbm, (hid_out, cell_out, vel_out) = refs[:6], refs[6:9]
    tables, refs = refs[9:15], refs[15:]
    (
        bias_ref, dec_ref, u_ref, vel_next,
        hid_in, hid_f, vel_f, cell_v, weight_v, weight_f, block_f, wide, side, slabs, vels, vel_t,
        vz_s, vz_r, vy_s, vy_r, vc_s, vc_r, acc, cells, hids, moved, send, recv,
        load_sem, send_sem, recv_sem, store_sem, tile_send_sem, tile_recv_sem,
    ) = refs
    gy, gz = lax.axis_index("gy"), lax.axis_index("gz")
    loads = [
        pltpu.make_async_copy(src, dst, load_sem.at[i])
        for i, (src, dst) in enumerate(
            [
                (hid_hbm, hid_in),
                (vel_hbm, vel_f),
                (weight_hbm, weight_v),
                (cell_hbm, cell_v),
                (bias_hbm, bias_ref),
                (dec_hbm, dec_ref),
                *zip(tables_hbm, tables),
            ]
        )
    ]
    for load in loads:
        load.start()
    barrier = pltpu.get_barrier_semaphore()
    targets = [(around(gy, sy), around(gz, sz)) for sy, sz in HALO]
    for target in targets:
        pl.semaphore_signal(barrier, inc=1, device_id=target, device_id_type=MESH)

    groups = positions()

    def greet(d, carry):
        for me, place in groups:
            pl.semaphore_signal(barrier, inc=1, device_id=place(around(me, d)), device_id_type=MESH)
        return carry

    lax.fori_loop(1, RANKS, greet, 0)
    vels[...] = jnp.zeros_like(vels)

    loads[0].wait()
    hid_f[...] = hid_in[...].astype(F32)
    loads[1].wait()

    def centre(y, carry):
        for z in range(2):
            for t in range(2):
                lanes = slice(128 * t, 128 * t + 128)
                rows = hid_f[pl.ds(y * 4 + 2 * t + z, 32, stride=32), :]
                slabs[y + 1, z + 1, 32:64, lanes] = rows.astype(BF16)
                vels[y + 1, z + 1, 0:3, lanes] = vel_f[pl.ds(y * 4 + 2 * t + z, 3, stride=32), :]
        return carry

    lax.fori_loop(0, 8, centre, 0)
    for z in range(2):
        for t in range(2):
            rows = vel_f[pl.ds(2 * t + z, 24, stride=4), :]
            rows = jnp.concatenate([rows, jnp.zeros((8, 128), F32)], 0)
            vz_s[z, :, 128 * t : 128 * t + 128] = rows.astype(BF16)
    for k in range(2):
        y = 1 + 7 * k
        vy_s[k] = jnp.concatenate([vels[y, 1], vels[y, 2]], 0).astype(BF16)
        for z in range(2):
            rows = jnp.concatenate([vels[y, z + 1], jnp.zeros((8, NX), F32)], 0)
            vc_s[2 * k + z] = rows.astype(BF16)

    pl.semaphore_wait(barrier, len(HALO) + 2 * (RANKS - 1))
    copies = {}

    def start_halo(name, i, n, src, dst):
        copies[name] = pltpu.make_async_remote_copy(
            src_ref=src,
            dst_ref=dst,
            send_sem=send_sem.at[i, n],
            recv_sem=recv_sem.at[i, n],
            device_id=targets[i],
            device_id_type=MESH,
        )
        copies[name].start()

    mids = pl.ds(32, 32)

    def send_plane(part):
        for i, (sy, sz) in enumerate(HALO):
            if sy == 0:
                z = (1 + sz) // 2
                ys = pl.ds(1 + 4 * part, 4)
                src, dst = slabs.at[ys, z + 1, mids], slabs.at[ys, 3 - 3 * z, mids]
                start_halo(("plane", z, part), i, part, src, dst)

    def send_edge(i):
        sy, sz = HALO[i]
        k, z = (1 + sy) // 2, (1 + sz) // 2
        if sz == 0:
            src, dst = slabs.at[1 + 7 * k, pl.ds(1, 2), mids], slabs.at[9 - 9 * k, pl.ds(1, 2), mids]
            start_halo(("edge", k, 0), i, 0, src, dst)
            start_halo(("edge", k, 1), i, 1, vy_s.at[k], vy_r.at[k])
        else:
            src, dst = slabs.at[1 + 7 * k, 1 + z, mids], slabs.at[9 - 9 * k, 3 - 3 * z, mids]
            start_halo(("corner", k, z, 0), i, 0, src, dst)
            start_halo(("corner", k, z, 1), i, 1, vc_s.at[2 * k + z], vc_r.at[2 * k + z])

    send_plane(0)
    for i, (sy, sz) in enumerate(HALO):
        if sy == 0:
            z = (1 + sz) // 2
            start_halo(("side", z), i, 2, vz_s.at[z], vz_r.at[z])
    for wanted in ((1, True), (-1, False), (1, False)):
        for i, (sy, sz) in enumerate(HALO):
            if (sy, sz != 0) == wanted:
                send_edge(i)
    send_plane(1)
    for i, (sy, sz) in enumerate(HALO):
        if sy == -1 and sz != 0:
            send_edge(i)

    def fill(y, z):
        mid = slabs[y, z, 32:64, :].astype(F32)
        slabs[y, z, 0:32, :] = pltpu.roll(mid, 1, 1).astype(BF16)
        slabs[y, z, 64:96, :] = pltpu.roll(mid, NX - 1, 1).astype(BF16)
        v = vels[y, z]
        first = v + pltpu.roll(pltpu.roll(v, 1, 1), 3, 0)
        tile = jnp.concatenate([first, pltpu.roll(v, NX - 1, 1), jnp.ones((16, NX), F32)], 0)
        slabs[y, z, 96:128, :] = tile.astype(BF16)

    def fill_own(y, carry):
        fill(y, 1)
        fill(y, 2)
        return carry

    lax.fori_loop(1, 9, fill_own, 0)

    loads[2].wait()
    loads[4].wait()
    weight_f[0:945, :] = weight_v[...].astype(F32)
    block_f[96:128, :] = jnp.zeros((32, 128), F32)
    gate = lax.broadcasted_iota(jnp.int32, (128, 128), 0)
    gate_scale = jnp.where((gate >= 64) & (gate < 96), 1.0, 0.5)
    for dy in range(3):
        for dz in range(3):
            first = (9 * dy + 3 * dz) * 35
            for dx in range(3):
                at = first + 35 * dx
                block_f[32 * dx : 32 * dx + 32, :] = weight_f[at + 3 : at + 35, :]
                row = 96 + (3, 0, 8)[dx]
                block_f[row : row + 3, :] = weight_f[at : at + 3, :]
            if dy == 1 and dz == 1:
                rest = bias_ref[...]
                for part in range(3):
                    high = rest.astype(BF16).astype(F32)
                    block_f[112 + part : 113 + part, :] = high
                    rest = rest - high
            turned = (block_f[...].T * gate_scale).astype(BF16)
            if dy == 1 and dz == 1:
                block_f[112:120, :] = jnp.zeros((8, 128), F32)
            if dz == 0:
                side[0, :, 128 * dy : 128 * dy + 128] = turned
            if dz == 2:
                side[1, :, 128 * dy : 128 * dy + 128] = turned
            for z in range(2):
                own = z + dz - 1
                if 0 <= own < 2:
                    at = (2 * dy + own) * 128
                    wide[128 * z : 128 * z + 128, at : at + 128] = turned

    def inner(y):
        acc[y] = dot(wide[...], slabs[pl.ds(y, 3), 1:3].reshape(6 * SLAB, NX))

    def inner_step(y, carry):
        inner(y)
        return carry

    lax.fori_loop(1, 7, inner_step, 0)

    loads[3].wait()
    loads[5].wait()

    def own_cells(y, carry):
        for z in range(2):
            for t in range(2):
                cells[y, z, :, 128 * t : 128 * t + 128] = cell_v[
                    pl.ds(y * 4 + 2 * t + z, 32, stride=32), :
                ]
        return carry

    lax.fori_loop(0, 8, own_cells, 0)

    for k in range(2):
        copies["edge", k, 0].wait_recv()
        copies["edge", k, 1].wait_recv()
        rows = vy_r[k].astype(F32)
        y = 9 - 9 * k
        vels[y, 1] = rows[0:8]
        vels[y, 2] = rows[8:16]
        fill(y, 1)
        fill(y, 2)
    inner(0)
    inner(7)

    def update(y, carry):
        for z in range(2):
            outer = slabs[pl.ds(y, 3), 3 * z].reshape(3 * SLAB, NX)
            gates = acc[y, 128 * z : 128 * z + 128, :] + dot(side[z], outer)
            turned = jnp.tanh(gates)
            new = 0.5 * (
                (turned[32:64] + 1.0) * cells[y, z] + (turned[0:32] + 1.0) * turned[64:96]
            )
            cells[y, z] = new
            hids[y, z] = (0.5 * (turned[96:128] + 1.0) * jnp.tanh(new)).astype(BF16)
        return carry

    def fill_outer(y, carry):
        fill(y, 0)
        fill(y, 3)
        return carry

    for z in range(2):
        copies["side", z].wait_recv()
        to = 3 - 3 * z
        rows = vz_r[z].astype(F32)
        for t in range(2):
            vel_t[t] = rows[:, 128 * t : 128 * t + 128]
            for y in range(8):
                vels[y + 1, to, 0:3, 128 * t : 128 * t + 128] = vel_t[t, pl.ds(y, 3, stride=8), :]
    for part, ys, rows in ((0, (0, 5), (0, 3)), (1, (5, 10), (3, 8))):
        k = 1 - part
        for z in range(2):
            copies["plane", z, part].wait_recv()
            copies["corner", k, z, 0].wait_recv()
            copies["corner", k, z, 1].wait_recv()
            vels[9 - 9 * k, 3 - 3 * z] = vc_r[2 * k + z].astype(F32)[0:8]
        lax.fori_loop(*ys, fill_outer, 0)
        lax.fori_loop(*rows, update, 0)

    for y in range(8):
        for z in range(2):
            advanced = vels[y + 1, z + 1, 0:3, :] + dot(dec_ref[...], hids[y, z])
            for t in range(2):
                at = 16 * y + 8 * z
                moved[t, at : at + 3, :] = advanced[:, 128 * t : 128 * t + 128]
    for c in range(3):
        for z in range(2):
            for t in range(2):
                start = 16 * c + 8 * z
                u_ref[start : start + 8, 128 * t : 128 * t + 128] = moved[
                    t, pl.ds(8 * z + c, 8, stride=16), :
                ]

    cell_store = pltpu.make_async_copy(cell_v, cell_out, store_sem.at[0])
    hid_store = pltpu.make_async_copy(hid_in, hid_out, store_sem.at[1])

    def store_states():
        def turn(y, carry):
            for z in range(2):
                for t in range(2):
                    rows = pl.ds(y * 4 + 2 * t + z, 32, stride=32)
                    lanes = slice(128 * t, 128 * t + 128)
                    cell_v[rows, :] = cells[y, z, :, lanes]
                    hid_f[rows, :] = hids[y, z, :, lanes].astype(F32)
            return carry

        lax.fori_loop(0, 8, turn, 0)
        cell_store.start()
        hid_in[...] = hid_f[...].astype(BF16)
        hid_store.start()

    for load in loads[6:]:
        load.wait()
    project(u_ref, tables, vel_next, send, recv, tile_send_sem, tile_recv_sem, store_states)
    vel_store = pltpu.make_async_copy(vel_next, vel_out, store_sem.at[2])
    vel_store.start()
    for copy in copies.values():
        copy.wait_send()
    cell_store.wait()
    hid_store.wait()
    vel_store.wait()


def hand_on_kernel(*refs):
    sources, results, held, sem = refs[:3], refs[3:6], refs[6:9], refs[9]
    arrive = [pltpu.make_async_copy(a, b, sem.at[0, i]) for i, (a, b) in enumerate(zip(sources, held))]
    leave = [pltpu.make_async_copy(a, b, sem.at[1, i]) for i, (a, b) in enumerate(zip(held, results))]
    for copy in arrive:
        copy.start()
    for i in (2, 0, 1):
        arrive[i].wait()
        leave[i].start()
    for copy in leave:
        copy.wait()


def to_rows(array):
    c = array.shape[0]
    return array.reshape(c, 8, 2, 2, 128).transpose(0, 1, 3, 2, 4).reshape(c * 32, 128)


def from_rows(array):
    c = array.shape[0] // 32
    return array.reshape(c, 8, 2, 2, 128).transpose(0, 1, 3, 2, 4).reshape(c, 8, 2, 256)


def per_device(velocity, hidden, cell, gate_weight, gate_bias, decoder):
    anywhere = pl.BlockSpec(memory_space=pl.ANY)
    tables = [halves(t) for t in (*x_tables(), *y_tables(), *z_tables())]
    results = (
        jax.ShapeDtypeStruct((1024, 128), BF16),
        jax.ShapeDtypeStruct((1024, 128), F32),
        jax.ShapeDtypeStruct((96, 128), F32),
    )
    outs = pl.pallas_call(
        step_kernel,
        out_shape=results,
        in_specs=[anywhere] * 12,
        out_specs=(anywhere,) * 3,
        scratch_shapes=[
            *(pltpu.VMEM(t.shape, BF16) for t in tables),
            pltpu.VMEM((1, 128), F32),
            pltpu.VMEM((3, 32), BF16),
            pltpu.VMEM((48, 256), F32),
            pltpu.VMEM((96, 128), F32),
            pltpu.VMEM((1024, 128), BF16),
            pltpu.VMEM((1024, 128), F32),
            pltpu.VMEM((96, 128), F32),
            pltpu.VMEM((1024, 128), F32),
            pltpu.VMEM((945, 128), BF16),
            pltpu.VMEM((952, 128), F32),
            pltpu.VMEM((128, 128), F32),
            pltpu.VMEM((256, 768), BF16),
            pltpu.VMEM((2, 128, 384), BF16),
            pltpu.VMEM((10, 4, SLAB, NX), BF16),
            pltpu.VMEM((10, 4, 8, NX), F32),
            pltpu.VMEM((2, 32, 128), F32),
            pltpu.VMEM((2, 32, NX), BF16),
            pltpu.VMEM((2, 32, NX), BF16),
            pltpu.VMEM((2, 16, NX), BF16),
            pltpu.VMEM((2, 16, NX), BF16),
            pltpu.VMEM((4, 16, NX), BF16),
            pltpu.VMEM((4, 16, NX), BF16),
            pltpu.VMEM((8, 256, 256), F32),
            pltpu.VMEM((8, 2, 32, NX), F32),
            pltpu.VMEM((8, 2, 32, NX), BF16),
            pltpu.VMEM((2, 128, 128), F32),
            pltpu.VMEM((4, RANKS, 8, 128), F32),
            pltpu.VMEM((4, RANKS, 8, 128), F32),
            pltpu.SemaphoreType.DMA((12,)),
            pltpu.SemaphoreType.DMA((8, 3)),
            pltpu.SemaphoreType.DMA((8, 3)),
            pltpu.SemaphoreType.DMA((3,)),
            pltpu.SemaphoreType.DMA((4,)),
            pltpu.SemaphoreType.DMA((4,)),
        ],
        compiler_params=pltpu.CompilerParams(
            collective_id=0, has_side_effects=True, vmem_limit_bytes=56 * 1024 * 1024
        ),
    )(
        to_rows(velocity),
        to_rows(hidden),
        to_rows(cell),
        gate_weight.T,
        gate_bias.reshape(1, 128),
        decoder,
        *(jnp.asarray(t) for t in tables),
    )
    outs = pl.pallas_call(
        hand_on_kernel,
        out_shape=results,
        in_specs=[anywhere] * 3,
        out_specs=(anywhere,) * 3,
        scratch_shapes=[*(pltpu.VMEM(r.shape, r.dtype) for r in results), pltpu.SemaphoreType.DMA((2, 3))],
        compiler_params=pltpu.CompilerParams(vmem_limit_bytes=56 * 1024 * 1024),
    )(*outs)
    return tuple(from_rows(out) for out in outs)


def solution(mesh):
    field = P(None, "gy", "gz", None)
    return jax.shard_map(
        per_device,
        mesh=mesh,
        in_specs=(field, field, field, P(), P(), P()),
        out_specs=(field, field, field),
        check_vma=False,
    )
```

```python
import functools

import jax
import jax.numpy as jnp
import numpy as np
from jax import lax
from jax.experimental import pallas as pl
from jax.experimental.pallas import tpu as pltpu
from jax.sharding import PartitionSpec as P

F32 = jnp.float32
BF16 = jnp.bfloat16
MESH = pl.DeviceIdType.MESH
NX, NY, NZ = 256, 128, 32
RANKS = 16
SLAB = 128
HALO = [(sy, sz) for sz in (-1, 1) for sy in (0, -1, 1)] + [(-1, 0), (1, 0)]


def halves(table):
    high = table.astype(np.float32).astype(jnp.bfloat16)
    low = (table - high.astype(np.float64)).astype(np.float32).astype(jnp.bfloat16)
    pair = np.stack([np.asarray(high), np.asarray(low)])
    if table.shape[1] == 256:
        pair = pair.reshape(2, -1, 2, 128).transpose(0, 2, 1, 3)
    return np.ascontiguousarray(pair)


def x_tables():
    mode = np.arange(128)
    n = np.arange(NX)
    angle = 2 * np.pi / NX * ((n[:, None] * mode[None, :]) % NX)
    sign = np.where(n % 2 == 0, 1.0, -1.0)
    imag = np.where(mode[None, :] == 0, sign[:, None], -np.sin(angle))
    forward = np.concatenate([np.cos(angle), imag], 1)
    weight = np.where(mode == 0, 1.0, 2.0) / NX
    inverse = forward.T * np.concatenate([weight, weight])[:, None]
    return forward, inverse


def real_waves(total):
    half = total // 2
    index = np.arange(total)
    return np.where(index < half, index, index - half).astype(np.float64)


def real_tables(total):
    half = total // 2
    cosines, sines = np.arange(half + 1), np.arange(1, half)
    place = np.arange(total)
    angle = 2 * np.pi / total * ((np.concatenate([cosines, sines])[:, None] * place[None, :]) % total)
    is_sine = np.arange(total)[:, None] > half
    analysis = np.where(is_sine, np.sin(angle), np.cos(angle))
    weight = np.full(total, 2.0 / total)
    weight[0] = weight[half] = 1.0 / total
    synthesis = analysis.T * weight[None, :]
    derivative = np.zeros((total, total))
    for k in range(1, half):
        derivative[k, half + k] = k
        derivative[half + k, k] = -k
    return analysis, synthesis, derivative


def y_tables():
    analysis, synthesis, derivative = real_tables(NY)
    forward = np.concatenate([analysis, derivative @ analysis], 0)
    inverse = np.concatenate([synthesis, -(synthesis @ derivative)], 0)
    return forward, inverse


def z_tables():
    analysis, synthesis, derivative = real_tables(NZ)
    lane = np.arange(NZ)
    z = (lane // 8 % 2) * 16 + (lane % 4) * 4 + (lane // 4 % 2) * 2 + lane // 16
    forward, inverse = np.zeros((128, 128)), np.zeros((128, 128))
    for c in range(3):
        lanes = slice(32 * c, 32 * c + 32)
        forward[lanes, :32] = (derivative @ analysis if c == 2 else analysis)[:, z].T
        inverse[:32, lanes] = (-(synthesis @ derivative) if c == 2 else synthesis)[z, :].T
    return forward, inverse


def split(value):
    high = value.astype(BF16)
    return high, (value - high.astype(F32)).astype(BF16)


def dot(a, b):
    return jnp.dot(a, b, preferred_element_type=F32)


def whole(table):
    if len(table.shape) == 3:
        return [table[0], table[1]]
    return [jnp.concatenate([table[part, 0], table[part, 1]], 1) for part in range(2)]


def data_by_table(value, table):
    table = whole(table)
    high, low = split(value)
    return dot(high, table[0]) + (dot(low, table[0]) + dot(high, table[1]))


def table_by_data(table, value):
    high, low = split(value)
    return dot(table[0], high) + (dot(table[0], low) + dot(table[1], high))


def roll_lanes(value, shift):
    return value if shift % 128 == 0 else pltpu.roll(value, shift % 128, 1)


def lane_mix(values, count, stride, base):
    digit = lax.broadcasted_iota(jnp.int32, (8, 128), 1) // stride % base
    masks = [digit == q for q in range(base)]
    rolled = [roll_lanes(v, r * stride) for r, v in enumerate(values)]
    outs = []
    for j in range(count):
        acc = rolled[0] if len(values) == base else jnp.zeros((8, 128), F32)
        for r, v in enumerate(rolled):
            if r or len(values) < base:
                acc = jnp.where(masks[(j + r) % base], v, acc)
        outs.append(roll_lanes(acc, -j * stride))
    return outs


def x_forward(rows, table):
    spectrum = data_by_table(rows, table)
    values = []
    for cz in range(6):
        part = [spectrum[8 * cz : 8 * cz + 8, 128 * p : 128 * p + 128] for p in range(2)]
        values += [-part[1], part[0]] if cz < 2 else part
    return lane_mix(values, RANKS, 8, 16)


def solve(tiles, yf_ref, yi_ref, zf_ref, zi_ref, wave_x):
    def swap(blocks, first_of, second_of):
        out = [None] * 16
        for low in range(4):
            mixed = lane_mix([blocks[first_of(low, i)] for i in range(4)], 4, 4, 4)
            for i in range(4):
                out[second_of(low, i)] = mixed[i]
        return out

    def by_source(low, i):
        return (i // 2) * 8 + low * 2 + i % 2

    def by_y(low, i):
        return i * 4 + low

    lane = lax.broadcasted_iota(jnp.int32, (NY, 128), 1)
    is_y = (lane >= 32) & (lane < 64)
    scale = jnp.where(lane < 32, wave_x, 1.0)
    rows = jnp.concatenate(swap(tiles, by_source, by_y), 0)
    out = table_by_data(yf_ref, rows)
    terms = jnp.where(is_y, out[NY:], out[:NY]) * scale
    divergence = data_by_table(terms, zf_ref)
    row = lax.broadcasted_iota(jnp.int32, (NY, 128), 0)
    wave_y = jnp.where(row < NY // 2, row, row - NY // 2).astype(F32)
    wave_z = jnp.where(lane < NZ // 2, lane, lane - NZ // 2).astype(F32)
    square = wave_x * wave_x + wave_y * wave_y + wave_z * wave_z
    potential = divergence / jnp.maximum(square, 1.0)
    out = table_by_data(yi_ref, data_by_table(potential, zi_ref))
    rows = jnp.where(is_y, out[NY:], out[:NY]) * scale
    return swap([rows[8 * i : 8 * i + 8] for i in range(16)], by_y, by_source)


def x_inverse(tiles, table):
    values = lane_mix(tiles, 12, 8, 16)
    rows = []
    for cz in range(6):
        pair = values[2 * cz : 2 * cz + 2]
        rows.append(jnp.concatenate([pair[1], -pair[0]] if cz < 2 else pair, 1))
    return data_by_table(jnp.concatenate(rows, 0), table)


def around(index, step):
    return lax.rem(index + step + RANKS, RANKS)


def positions():
    gy, gz = lax.axis_index("gy"), lax.axis_index("gz")
    y, z_low, z_high, x, core = gy // 4, gy % 4, gz // 8, gz // 2 % 4, gz % 2

    def first(index):
        return (index // 4 * 4 + z_low, z_high * 8 + index % 4 * 2 + core)

    def second(index):
        return (y * 4 + index // 2 % 4, index // 8 * 8 + x * 2 + index % 2)

    return (y * 4 + x, first), (z_high * 8 + z_low * 2 + core, second)


def project(u_ref, tables, out_ref, send, recv, send_sem, recv_sem, meanwhile):
    xf_ref, xi_ref, yf_ref, yi_ref, zf_ref, zi_ref = tables
    group_1, group_2 = positions()

    def exchange(step, group, tiles, meanwhile=None):
        me, place = group
        for j in range(RANKS):
            send[step, j] = tiles[j]

        def start(d, carry):
            to = around(me, d)
            pltpu.make_async_remote_copy(
                src_ref=send.at[step, to],
                dst_ref=recv.at[step, me],
                send_sem=send_sem.at[step],
                recv_sem=recv_sem.at[step],
                device_id=place(to),
                device_id_type=MESH,
            ).start()
            return carry

        lax.fori_loop(1, RANKS, start, 0)
        recv[step, pl.ds(me, 1)] = send[step, pl.ds(me, 1)]
        if meanwhile is not None:
            meanwhile()
        some = recv.at[step, pl.ds(0, RANKS - 1)]
        pltpu.make_async_copy(some, some, recv_sem.at[step]).wait()
        return [recv[step, j] for j in range(RANKS)]

    tiles = exchange(0, group_1, x_forward(u_ref[...], xf_ref), meanwhile)
    tiles = exchange(1, group_2, lane_mix(tiles, RANKS, 1, 16))
    wave_x = (group_1[0] * 8 + group_2[0] % 8).astype(F32)
    tiles = exchange(2, group_2, solve(tiles, yf_ref, yi_ref, zf_ref, zi_ref, wave_x))
    tiles = exchange(3, group_1, lane_mix(tiles, RANKS, 1, 16))
    gradient = x_inverse(tiles, xi_ref)
    result = u_ref[...] - gradient
    for c in range(3):
        for z in range(2):
            start = (2 * c + z) * 8
            for t in range(2):
                out_ref[pl.ds(c * 32 + 2 * t + z, 8, stride=4), :] = result[
                    start : start + 8, 128 * t : 128 * t + 128
                ]
    for step in range(4):
        some = send.at[step, pl.ds(0, RANKS - 1)]
        pltpu.make_async_copy(some, some, send_sem.at[step]).wait()


def step_kernel(
    vel_hbm, hid_hbm, cell_hbm, weight_hbm, bias_hbm, dec_hbm, *refs,
):
    tables_hbm, (hid_in, cell_v, vel_next) = refs[:6], refs[6:9]
    tables, refs = refs[9:15], refs[15:]
    (
        bias_ref, dec_ref, u_ref, hid_f, vel_f, weight_v, weight_f, block_f, wide, side, slabs, vels, vel_t,
        vz_s, vz_r, vy_s, vy_r, vc_s, vc_r, acc, cells, hids, moved, send, recv,
        load_sem, send_sem, recv_sem, tile_send_sem, tile_recv_sem,
    ) = refs
    gy, gz = lax.axis_index("gy"), lax.axis_index("gz")
    loads = [
        pltpu.make_async_copy(src, dst, load_sem.at[i])
        for i, (src, dst) in enumerate(
            [
                (hid_hbm, hid_in),
                (vel_hbm, vel_f),
                (weight_hbm, weight_v),
                (cell_hbm, cell_v),
                (bias_hbm, bias_ref),
                (dec_hbm, dec_ref),
                *zip(tables_hbm, tables),
            ]
        )
    ]
    for load in loads:
        load.start()
    barrier = pltpu.get_barrier_semaphore()
    targets = [(around(gy, sy), around(gz, sz)) for sy, sz in HALO]
    for target in targets:
        pl.semaphore_signal(barrier, inc=1, device_id=target, device_id_type=MESH)

    groups = positions()

    def greet(d, carry):
        for me, place in groups:
            pl.semaphore_signal(barrier, inc=1, device_id=place(around(me, d)), device_id_type=MESH)
        return carry

    lax.fori_loop(1, RANKS, greet, 0)
    vels[...] = jnp.zeros_like(vels)

    loads[0].wait()
    hid_f[...] = hid_in[...].astype(F32)
    loads[1].wait()

    def centre(y, carry):
        for z in range(2):
            for t in range(2):
                lanes = slice(128 * t, 128 * t + 128)
                rows = hid_f[pl.ds(y * 4 + 2 * t + z, 32, stride=32), :]
                slabs[y + 1, z + 1, 32:64, lanes] = rows.astype(BF16)
                vels[y + 1, z + 1, 0:3, lanes] = vel_f[pl.ds(y * 4 + 2 * t + z, 3, stride=32), :]
        return carry

    lax.fori_loop(0, 8, centre, 0)
    for z in range(2):
        for t in range(2):
            rows = vel_f[pl.ds(2 * t + z, 24, stride=4), :]
            rows = jnp.concatenate([rows, jnp.zeros((8, 128), F32)], 0)
            vz_s[z, :, 128 * t : 128 * t + 128] = rows.astype(BF16)
    for k in range(2):
        y = 1 + 7 * k
        vy_s[k] = jnp.concatenate([vels[y, 1], vels[y, 2]], 0).astype(BF16)
        for z in range(2):
            rows = jnp.concatenate([vels[y, z + 1], jnp.zeros((8, NX), F32)], 0)
            vc_s[2 * k + z] = rows.astype(BF16)

    pl.semaphore_wait(barrier, len(HALO) + 2 * (RANKS - 1))
    copies = {}

    def start_halo(name, i, n, src, dst):
        copies[name] = pltpu.make_async_remote_copy(
            src_ref=src,
            dst_ref=dst,
            send_sem=send_sem.at[i, n],
            recv_sem=recv_sem.at[i, n],
            device_id=targets[i],
            device_id_type=MESH,
        )
        copies[name].start()

    mids = pl.ds(32, 32)

    def send_plane(part):
        for i, (sy, sz) in enumerate(HALO):
            if sy == 0:
                z = (1 + sz) // 2
                ys = pl.ds(1 + 4 * part, 4)
                src, dst = slabs.at[ys, z + 1, mids], slabs.at[ys, 3 - 3 * z, mids]
                start_halo(("plane", z, part), i, part, src, dst)

    def send_edge(i):
        sy, sz = HALO[i]
        k, z = (1 + sy) // 2, (1 + sz) // 2
        if sz == 0:
            src, dst = slabs.at[1 + 7 * k, pl.ds(1, 2), mids], slabs.at[9 - 9 * k, pl.ds(1, 2), mids]
            start_halo(("edge", k, 0), i, 0, src, dst)
            start_halo(("edge", k, 1), i, 1, vy_s.at[k], vy_r.at[k])
        else:
            src, dst = slabs.at[1 + 7 * k, 1 + z, mids], slabs.at[9 - 9 * k, 3 - 3 * z, mids]
            start_halo(("corner", k, z, 0), i, 0, src, dst)
            start_halo(("corner", k, z, 1), i, 1, vc_s.at[2 * k + z], vc_r.at[2 * k + z])

    send_plane(0)
    for i, (sy, sz) in enumerate(HALO):
        if sy == 0:
            z = (1 + sz) // 2
            start_halo(("side", z), i, 2, vz_s.at[z], vz_r.at[z])
    for wanted in ((1, True), (-1, False), (1, False)):
        for i, (sy, sz) in enumerate(HALO):
            if (sy, sz != 0) == wanted:
                send_edge(i)
    send_plane(1)
    for i, (sy, sz) in enumerate(HALO):
        if sy == -1 and sz != 0:
            send_edge(i)

    def fill(y, z):
        mid = slabs[y, z, 32:64, :].astype(F32)
        slabs[y, z, 0:32, :] = pltpu.roll(mid, 1, 1).astype(BF16)
        slabs[y, z, 64:96, :] = pltpu.roll(mid, NX - 1, 1).astype(BF16)
        v = vels[y, z]
        first = v + pltpu.roll(pltpu.roll(v, 1, 1), 3, 0)
        tile = jnp.concatenate([first, pltpu.roll(v, NX - 1, 1), jnp.ones((16, NX), F32)], 0)
        slabs[y, z, 96:128, :] = tile.astype(BF16)

    def fill_own(y, carry):
        fill(y, 1)
        fill(y, 2)
        return carry

    lax.fori_loop(1, 9, fill_own, 0)

    loads[2].wait()
    loads[4].wait()
    weight_f[0:945, :] = weight_v[...].astype(F32)
    block_f[96:128, :] = jnp.zeros((32, 128), F32)
    gate = lax.broadcasted_iota(jnp.int32, (128, 128), 0)
    gate_scale = jnp.where((gate >= 64) & (gate < 96), 1.0, 0.5)
    for dy in range(3):
        for dz in range(3):
            first = (9 * dy + 3 * dz) * 35
            for dx in range(3):
                at = first + 35 * dx
                block_f[32 * dx : 32 * dx + 32, :] = weight_f[at + 3 : at + 35, :]
                row = 96 + (3, 0, 8)[dx]
                block_f[row : row + 3, :] = weight_f[at : at + 3, :]
            if dy == 1 and dz == 1:
                rest = bias_ref[...]
                for part in range(3):
                    high = rest.astype(BF16).astype(F32)
                    block_f[112 + part : 113 + part, :] = high
                    rest = rest - high
            turned = (block_f[...].T * gate_scale).astype(BF16)
            if dy == 1 and dz == 1:
                block_f[112:120, :] = jnp.zeros((8, 128), F32)
            if dz == 0:
                side[0, :, 128 * dy : 128 * dy + 128] = turned
            if dz == 2:
                side[1, :, 128 * dy : 128 * dy + 128] = turned
            for z in range(2):
                own = z + dz - 1
                if 0 <= own < 2:
                    at = (2 * dy + own) * 128
                    wide[128 * z : 128 * z + 128, at : at + 128] = turned

    def inner(y):
        acc[y] = dot(wide[...], slabs[pl.ds(y, 3), 1:3].reshape(6 * SLAB, NX))

    def inner_step(y, carry):
        inner(y)
        return carry

    lax.fori_loop(1, 7, inner_step, 0)

    loads[3].wait()
    loads[5].wait()

    def own_cells(y, carry):
        for z in range(2):
            for t in range(2):
                cells[y, z, :, 128 * t : 128 * t + 128] = cell_v[
                    pl.ds(y * 4 + 2 * t + z, 32, stride=32), :
                ]
        return carry

    lax.fori_loop(0, 8, own_cells, 0)

    for k in range(2):
        copies["edge", k, 0].wait_recv()
        copies["edge", k, 1].wait_recv()
        rows = vy_r[k].astype(F32)
        y = 9 - 9 * k
        vels[y, 1] = rows[0:8]
        vels[y, 2] = rows[8:16]
        fill(y, 1)
        fill(y, 2)
    inner(0)
    inner(7)

    def update(y, carry):
        for z in range(2):
            outer = slabs[pl.ds(y, 3), 3 * z].reshape(3 * SLAB, NX)
            gates = acc[y, 128 * z : 128 * z + 128, :] + dot(side[z], outer)
            turned = jnp.tanh(gates)
            new = 0.5 * (
                (turned[32:64] + 1.0) * cells[y, z] + (turned[0:32] + 1.0) * turned[64:96]
            )
            cells[y, z] = new
            hids[y, z] = (0.5 * (turned[96:128] + 1.0) * jnp.tanh(new)).astype(BF16)
        return carry

    def fill_outer(y, carry):
        fill(y, 0)
        fill(y, 3)
        return carry

    for z in range(2):
        copies["side", z].wait_recv()
        to = 3 - 3 * z
        rows = vz_r[z].astype(F32)
        for t in range(2):
            vel_t[t] = rows[:, 128 * t : 128 * t + 128]
            for y in range(8):
                vels[y + 1, to, 0:3, 128 * t : 128 * t + 128] = vel_t[t, pl.ds(y, 3, stride=8), :]
    for part, ys, rows in ((0, (0, 5), (0, 3)), (1, (5, 10), (3, 8))):
        k = 1 - part
        for z in range(2):
            copies["plane", z, part].wait_recv()
            copies["corner", k, z, 0].wait_recv()
            copies["corner", k, z, 1].wait_recv()
            vels[9 - 9 * k, 3 - 3 * z] = vc_r[2 * k + z].astype(F32)[0:8]
        lax.fori_loop(*ys, fill_outer, 0)
        lax.fori_loop(*rows, update, 0)

    for y in range(8):
        for z in range(2):
            advanced = vels[y + 1, z + 1, 0:3, :] + dot(dec_ref[...], hids[y, z])
            for t in range(2):
                at = 16 * y + 8 * z
                moved[t, at : at + 3, :] = advanced[:, 128 * t : 128 * t + 128]
    for c in range(3):
        for z in range(2):
            for t in range(2):
                start = 16 * c + 8 * z
                u_ref[start : start + 8, 128 * t : 128 * t + 128] = moved[
                    t, pl.ds(8 * z + c, 8, stride=16), :
                ]

    def store_states():
        def turn(y, carry):
            for z in range(2):
                for t in range(2):
                    rows = pl.ds(y * 4 + 2 * t + z, 32, stride=32)
                    lanes = slice(128 * t, 128 * t + 128)
                    cell_v[rows, :] = cells[y, z, :, lanes]
                    hid_f[rows, :] = hids[y, z, :, lanes].astype(F32)
            return carry

        lax.fori_loop(0, 8, turn, 0)
        hid_in[...] = hid_f[...].astype(BF16)

    for load in loads[6:]:
        load.wait()
    project(u_ref, tables, vel_next, send, recv, tile_send_sem, tile_recv_sem, store_states)
    for copy in copies.values():
        copy.wait_send()


def hand_on_kernel(*refs):
    sources, results, sem = refs[:3], refs[3:6], refs[6]
    copies = [pltpu.make_async_copy(a, b, sem.at[i]) for i, (a, b) in enumerate(zip(sources, results))]
    for copy in copies:
        copy.start()
    for copy in copies:
        copy.wait()


def to_rows(array):
    c = array.shape[0]
    return array.reshape(c, 8, 2, 2, 128).transpose(0, 1, 3, 2, 4).reshape(c * 32, 128)


def from_rows(array):
    c = array.shape[0] // 32
    return array.reshape(c, 8, 2, 2, 128).transpose(0, 1, 3, 2, 4).reshape(c, 8, 2, 256)


def per_device(velocity, hidden, cell, gate_weight, gate_bias, decoder):
    anywhere = pl.BlockSpec(memory_space=pl.ANY)
    vmem = pl.BlockSpec(memory_space=pltpu.VMEM)
    tables = [halves(t) for t in (*x_tables(), *y_tables(), *z_tables())]
    results = (
        jax.ShapeDtypeStruct((1024, 128), BF16),
        jax.ShapeDtypeStruct((1024, 128), F32),
        jax.ShapeDtypeStruct((96, 128), F32),
    )
    outs = pl.pallas_call(
        step_kernel,
        out_shape=tuple(pltpu.VMEM(r.shape, r.dtype) for r in results),
        in_specs=[anywhere] * 12,
        out_specs=(vmem,) * 3,
        scratch_shapes=[
            *(pltpu.VMEM(t.shape, BF16) for t in tables),
            pltpu.VMEM((1, 128), F32),
            pltpu.VMEM((3, 32), BF16),
            pltpu.VMEM((48, 256), F32),
            pltpu.VMEM((1024, 128), F32),
            pltpu.VMEM((96, 128), F32),
            pltpu.VMEM((945, 128), BF16),
            pltpu.VMEM((952, 128), F32),
            pltpu.VMEM((128, 128), F32),
            pltpu.VMEM((256, 768), BF16),
            pltpu.VMEM((2, 128, 384), BF16),
            pltpu.VMEM((10, 4, SLAB, NX), BF16),
            pltpu.VMEM((10, 4, 8, NX), F32),
            pltpu.VMEM((2, 32, 128), F32),
            pltpu.VMEM((2, 32, NX), BF16),
            pltpu.VMEM((2, 32, NX), BF16),
            pltpu.VMEM((2, 16, NX), BF16),
            pltpu.VMEM((2, 16, NX), BF16),
            pltpu.VMEM((4, 16, NX), BF16),
            pltpu.VMEM((4, 16, NX), BF16),
            pltpu.VMEM((8, 256, 256), F32),
            pltpu.VMEM((8, 2, 32, NX), F32),
            pltpu.VMEM((8, 2, 32, NX), BF16),
            pltpu.VMEM((2, 128, 128), F32),
            pltpu.VMEM((4, RANKS, 8, 128), F32),
            pltpu.VMEM((4, RANKS, 8, 128), F32),
            pltpu.SemaphoreType.DMA((12,)),
            pltpu.SemaphoreType.DMA((8, 3)),
            pltpu.SemaphoreType.DMA((8, 3)),
            pltpu.SemaphoreType.DMA((4,)),
            pltpu.SemaphoreType.DMA((4,)),
        ],
        compiler_params=pltpu.CompilerParams(
            collective_id=0, has_side_effects=True, vmem_limit_bytes=58 * 1024 * 1024
        ),
    )(
        to_rows(velocity),
        to_rows(hidden),
        to_rows(cell),
        gate_weight.T,
        gate_bias.reshape(1, 128),
        decoder,
        *(jnp.asarray(t) for t in tables),
    )
    outs = pl.pallas_call(
        hand_on_kernel,
        out_shape=results,
        in_specs=[vmem] * 3,
        out_specs=(anywhere,) * 3,
        scratch_shapes=[pltpu.SemaphoreType.DMA((3,))],
        compiler_params=pltpu.CompilerParams(vmem_limit_bytes=58 * 1024 * 1024),
    )(*outs)
    return tuple(from_rows(out) for out in outs)


def solution(mesh):
    field = P(None, "gy", "gz", None)
    return jax.shard_map(
        per_device,
        mesh=mesh,
        in_specs=(field, field, field, P(), P(), P()),
        out_specs=(field, field, field),
        check_vma=False,
    )
```

```python
import functools

import jax
import jax.numpy as jnp
import numpy as np
from jax import lax
from jax.experimental import pallas as pl
from jax.experimental.pallas import tpu as pltpu
from jax.sharding import PartitionSpec as P

F32 = jnp.float32
BF16 = jnp.bfloat16
MESH = pl.DeviceIdType.MESH
NX, NY, NZ = 256, 128, 32
RANKS = 16
SLAB = 128
HALO = [(sy, sz) for sz in (-1, 1) for sy in (0, -1, 1)] + [(-1, 0), (1, 0)]


def halves(table):
    high = table.astype(np.float32).astype(jnp.bfloat16)
    low = (table - high.astype(np.float64)).astype(np.float32).astype(jnp.bfloat16)
    pair = np.stack([np.asarray(high), np.asarray(low)])
    if table.shape[1] == 256:
        pair = pair.reshape(2, -1, 2, 128).transpose(0, 2, 1, 3)
    return np.ascontiguousarray(pair)


def x_tables():
    mode = np.arange(128)
    n = np.arange(NX)
    angle = 2 * np.pi / NX * ((n[:, None] * mode[None, :]) % NX)
    sign = np.where(n % 2 == 0, 1.0, -1.0)
    imag = np.where(mode[None, :] == 0, sign[:, None], -np.sin(angle))
    forward = np.concatenate([np.cos(angle), imag], 1)
    weight = np.where(mode == 0, 1.0, 2.0) / NX
    inverse = forward.T * np.concatenate([weight, weight])[:, None]
    return forward, inverse


def real_waves(total):
    half = total // 2
    index = np.arange(total)
    return np.where(index < half, index, index - half).astype(np.float64)


def real_tables(total):
    half = total // 2
    cosines, sines = np.arange(half + 1), np.arange(1, half)
    place = np.arange(total)
    angle = 2 * np.pi / total * ((np.concatenate([cosines, sines])[:, None] * place[None, :]) % total)
    is_sine = np.arange(total)[:, None] > half
    analysis = np.where(is_sine, np.sin(angle), np.cos(angle))
    weight = np.full(total, 2.0 / total)
    weight[0] = weight[half] = 1.0 / total
    synthesis = analysis.T * weight[None, :]
    derivative = np.zeros((total, total))
    for k in range(1, half):
        derivative[k, half + k] = k
        derivative[half + k, k] = -k
    return analysis, synthesis, derivative


def y_tables():
    analysis, synthesis, derivative = real_tables(NY)
    forward = np.concatenate([analysis, derivative @ analysis], 0)
    inverse = np.concatenate([synthesis, -(synthesis @ derivative)], 0)
    return forward, inverse


def z_tables():
    analysis, synthesis, derivative = real_tables(NZ)
    lane = np.arange(NZ)
    z = (lane // 8 % 2) * 16 + (lane % 4) * 4 + (lane // 4 % 2) * 2 + lane // 16
    forward, inverse = np.zeros((128, 128)), np.zeros((128, 128))
    for c in range(3):
        lanes = slice(32 * c, 32 * c + 32)
        forward[lanes, :32] = (derivative @ analysis if c == 2 else analysis)[:, z].T
        inverse[:32, lanes] = (-(synthesis @ derivative) if c == 2 else synthesis)[z, :].T
    return forward, inverse


def split(value):
    high = value.astype(BF16)
    return high, (value - high.astype(F32)).astype(BF16)


def dot(a, b):
    return jnp.dot(a, b, preferred_element_type=F32)


def whole(table):
    if len(table.shape) == 3:
        return [table[0], table[1]]
    return [jnp.concatenate([table[part, 0], table[part, 1]], 1) for part in range(2)]


def data_by_table(value, table):
    table = whole(table)
    high, low = split(value)
    return dot(high, table[0]) + (dot(low, table[0]) + dot(high, table[1]))


def table_by_data(table, value):
    high, low = split(value)
    return dot(table[0], high) + (dot(table[0], low) + dot(table[1], high))


def roll_lanes(value, shift):
    return value if shift % 128 == 0 else pltpu.roll(value, shift % 128, 1)


def lane_mix(values, count, stride, base):
    digit = lax.broadcasted_iota(jnp.int32, (8, 128), 1) // stride % base
    masks = [digit == q for q in range(base)]
    rolled = [roll_lanes(v, r * stride) for r, v in enumerate(values)]
    outs = []
    for j in range(count):
        acc = rolled[0] if len(values) == base else jnp.zeros((8, 128), F32)
        for r, v in enumerate(rolled):
            if r or len(values) < base:
                acc = jnp.where(masks[(j + r) % base], v, acc)
        outs.append(roll_lanes(acc, -j * stride))
    return outs


def x_forward(rows, table):
    spectrum = data_by_table(rows, table)
    values = []
    for cz in range(6):
        part = [spectrum[8 * cz : 8 * cz + 8, 128 * p : 128 * p + 128] for p in range(2)]
        values += [-part[1], part[0]] if cz < 2 else part
    return lane_mix(values, RANKS, 8, 16)


def solve(tiles, yf_ref, yi_ref, zf_ref, zi_ref, wave_x):
    def swap(blocks, first_of, second_of):
        out = [None] * 16
        for low in range(4):
            mixed = lane_mix([blocks[first_of(low, i)] for i in range(4)], 4, 4, 4)
            for i in range(4):
                out[second_of(low, i)] = mixed[i]
        return out

    def by_source(low, i):
        return (i // 2) * 8 + low * 2 + i % 2

    def by_y(low, i):
        return i * 4 + low

    lane = lax.broadcasted_iota(jnp.int32, (NY, 128), 1)
    is_y = (lane >= 32) & (lane < 64)
    scale = jnp.where(lane < 32, wave_x, 1.0)
    rows = jnp.concatenate(swap(tiles, by_source, by_y), 0)
    out = table_by_data(yf_ref, rows)
    terms = jnp.where(is_y, out[NY:], out[:NY]) * scale
    divergence = data_by_table(terms, zf_ref)
    row = lax.broadcasted_iota(jnp.int32, (NY, 128), 0)
    wave_y = jnp.where(row < NY // 2, row, row - NY // 2).astype(F32)
    wave_z = jnp.where(lane < NZ // 2, lane, lane - NZ // 2).astype(F32)
    square = wave_x * wave_x + wave_y * wave_y + wave_z * wave_z
    potential = divergence / jnp.maximum(square, 1.0)
    out = table_by_data(yi_ref, data_by_table(potential, zi_ref))
    rows = jnp.where(is_y, out[NY:], out[:NY]) * scale
    return swap([rows[8 * i : 8 * i + 8] for i in range(16)], by_y, by_source)


def x_inverse(tiles, table):
    values = lane_mix(tiles, 12, 8, 16)
    rows = []
    for cz in range(6):
        pair = values[2 * cz : 2 * cz + 2]
        rows.append(jnp.concatenate([pair[1], -pair[0]] if cz < 2 else pair, 1))
    return data_by_table(jnp.concatenate(rows, 0), table)


def around(index, step):
    return lax.rem(index + step + RANKS, RANKS)


def positions():
    gy, gz = lax.axis_index("gy"), lax.axis_index("gz")
    y, z_low, z_high, x, core = gy // 4, gy % 4, gz // 8, gz // 2 % 4, gz % 2

    def first(index):
        return (index // 4 * 4 + z_low, z_high * 8 + index % 4 * 2 + core)

    def second(index):
        return (y * 4 + index // 2 % 4, index // 8 * 8 + x * 2 + index % 2)

    return (y * 4 + x, first), (z_high * 8 + z_low * 2 + core, second)


def project(u_ref, tables, out_ref, send, recv, send_sem, recv_sem, meanwhile):
    xf_ref, xi_ref, yf_ref, yi_ref, zf_ref, zi_ref = tables
    group_1, group_2 = positions()

    def exchange(step, group, tiles, meanwhile=None):
        me, place = group
        for j in range(RANKS):
            send[step, j] = tiles[j]

        def start(d, carry):
            to = around(me, d)
            pltpu.make_async_remote_copy(
                src_ref=send.at[step, to],
                dst_ref=recv.at[step, me],
                send_sem=send_sem.at[step],
                recv_sem=recv_sem.at[step],
                device_id=place(to),
                device_id_type=MESH,
            ).start()
            return carry

        lax.fori_loop(1, RANKS, start, 0)
        recv[step, pl.ds(me, 1)] = send[step, pl.ds(me, 1)]
        if meanwhile is not None:
            meanwhile()
        some = recv.at[step, pl.ds(0, RANKS - 1)]
        pltpu.make_async_copy(some, some, recv_sem.at[step]).wait()
        return [recv[step, j] for j in range(RANKS)]

    tiles = exchange(0, group_1, x_forward(u_ref[...], xf_ref), meanwhile)
    tiles = exchange(1, group_2, lane_mix(tiles, RANKS, 1, 16))
    wave_x = (group_1[0] * 8 + group_2[0] % 8).astype(F32)
    tiles = exchange(2, group_2, solve(tiles, yf_ref, yi_ref, zf_ref, zi_ref, wave_x))
    tiles = exchange(3, group_1, lane_mix(tiles, RANKS, 1, 16))
    gradient = x_inverse(tiles, xi_ref)
    result = u_ref[...] - gradient
    for c in range(3):
        for z in range(2):
            start = (2 * c + z) * 8
            for t in range(2):
                out_ref[pl.ds(c * 32 + 2 * t + z, 8, stride=4), :] = result[
                    start : start + 8, 128 * t : 128 * t + 128
                ]
    for step in range(4):
        some = send.at[step, pl.ds(0, RANKS - 1)]
        pltpu.make_async_copy(some, some, send_sem.at[step]).wait()


def step_kernel(
    vel_hbm, hid_hbm, cell_hbm, weight_hbm, bias_hbm, dec_hbm, *refs,
):
    tables_hbm, (hid_in, cell_v, vel_next) = refs[:6], refs[6:9]
    tables, refs = refs[9:15], refs[15:]
    (
        bias_ref, dec_ref, u_ref, hid_f, vel_f, weight_v, weight_f, block_f, wide, side, slabs, vels, vel_t,
        vz_s, vz_r, vy_s, vy_r, vc_s, vc_r, acc, cells, hids, moved, send, recv,
        load_sem, send_sem, recv_sem, tile_send_sem, tile_recv_sem,
    ) = refs
    gy, gz = lax.axis_index("gy"), lax.axis_index("gz")
    loads = [
        pltpu.make_async_copy(src, dst, load_sem.at[i])
        for i, (src, dst) in enumerate(
            [
                (hid_hbm, hid_in),
                (vel_hbm, vel_f),
                (weight_hbm, weight_v),
                (cell_hbm, cell_v),
                (bias_hbm, bias_ref),
                (dec_hbm, dec_ref),
                *zip(tables_hbm, tables),
            ]
        )
    ]
    for load in loads:
        load.start()
    barrier = pltpu.get_barrier_semaphore()
    targets = [(around(gy, sy), around(gz, sz)) for sy, sz in HALO]
    for target in targets:
        pl.semaphore_signal(barrier, inc=1, device_id=target, device_id_type=MESH)

    groups = positions()

    def greet(d, carry):
        for me, place in groups:
            pl.semaphore_signal(barrier, inc=1, device_id=place(around(me, d)), device_id_type=MESH)
        return carry

    lax.fori_loop(1, RANKS, greet, 0)
    vels[...] = jnp.zeros_like(vels)

    loads[0].wait()
    hid_f[...] = hid_in[...].astype(F32)
    loads[1].wait()

    def centre(y, carry):
        for z in range(2):
            for t in range(2):
                lanes = slice(128 * t, 128 * t + 128)
                rows = hid_f[pl.ds(y * 4 + 2 * t + z, 32, stride=32), :]
                slabs[y + 1, z + 1, 32:64, lanes] = rows.astype(BF16)
                vels[y + 1, z + 1, 0:3, lanes] = vel_f[pl.ds(y * 4 + 2 * t + z, 3, stride=32), :]
        return carry

    lax.fori_loop(0, 8, centre, 0)
    for z in range(2):
        for t in range(2):
            rows = vel_f[pl.ds(2 * t + z, 24, stride=4), :]
            rows = jnp.concatenate([rows, jnp.zeros((8, 128), F32)], 0)
            vz_s[z, :, 128 * t : 128 * t + 128] = rows.astype(BF16)
    for k in range(2):
        y = 1 + 7 * k
        vy_s[k] = jnp.concatenate([vels[y, 1], vels[y, 2]], 0).astype(BF16)
        for z in range(2):
            rows = jnp.concatenate([vels[y, z + 1], jnp.zeros((8, NX), F32)], 0)
            vc_s[2 * k + z] = rows.astype(BF16)

    pl.semaphore_wait(barrier, len(HALO) + 2 * (RANKS - 1))
    copies = {}

    def start_halo(name, i, n, src, dst):
        copies[name] = pltpu.make_async_remote_copy(
            src_ref=src,
            dst_ref=dst,
            send_sem=send_sem.at[i, n],
            recv_sem=recv_sem.at[i, n],
            device_id=targets[i],
            device_id_type=MESH,
        )
        copies[name].start()

    mids = pl.ds(32, 32)

    def send_plane(part):
        for i, (sy, sz) in enumerate(HALO):
            if sy == 0:
                z = (1 + sz) // 2
                ys = pl.ds(1 + 4 * part, 4)
                src, dst = slabs.at[ys, z + 1, mids], slabs.at[ys, 3 - 3 * z, mids]
                start_halo(("plane", z, part), i, part, src, dst)

    def send_edge(i):
        sy, sz = HALO[i]
        k, z = (1 + sy) // 2, (1 + sz) // 2
        if sz == 0:
            src, dst = slabs.at[1 + 7 * k, pl.ds(1, 2), mids], slabs.at[9 - 9 * k, pl.ds(1, 2), mids]
            start_halo(("edge", k, 0), i, 0, src, dst)
            start_halo(("edge", k, 1), i, 1, vy_s.at[k], vy_r.at[k])
        else:
            src, dst = slabs.at[1 + 7 * k, 1 + z, mids], slabs.at[9 - 9 * k, 3 - 3 * z, mids]
            start_halo(("corner", k, z, 0), i, 0, src, dst)
            start_halo(("corner", k, z, 1), i, 1, vc_s.at[2 * k + z], vc_r.at[2 * k + z])

    send_plane(0)
    for i, (sy, sz) in enumerate(HALO):
        if sy == 0:
            z = (1 + sz) // 2
            start_halo(("side", z), i, 2, vz_s.at[z], vz_r.at[z])
    for wanted in ((1, True), (-1, False), (1, False)):
        for i, (sy, sz) in enumerate(HALO):
            if (sy, sz != 0) == wanted:
                send_edge(i)
    send_plane(1)
    for i, (sy, sz) in enumerate(HALO):
        if sy == -1 and sz != 0:
            send_edge(i)

    def fill(y, z):
        mid = slabs[y, z, 32:64, :].astype(F32)
        slabs[y, z, 0:32, :] = pltpu.roll(mid, 1, 1).astype(BF16)
        slabs[y, z, 64:96, :] = pltpu.roll(mid, NX - 1, 1).astype(BF16)
        v = vels[y, z]
        first = v + pltpu.roll(pltpu.roll(v, 1, 1), 3, 0)
        tile = jnp.concatenate([first, pltpu.roll(v, NX - 1, 1), jnp.ones((16, NX), F32)], 0)
        slabs[y, z, 96:128, :] = tile.astype(BF16)

    def fill_own(y, carry):
        fill(y, 1)
        fill(y, 2)
        return carry

    lax.fori_loop(1, 9, fill_own, 0)

    loads[2].wait()
    loads[4].wait()
    weight_f[0:945, :] = weight_v[...].astype(F32)
    block_f[96:128, :] = jnp.zeros((32, 128), F32)
    gate = lax.broadcasted_iota(jnp.int32, (128, 128), 0)
    gate_scale = jnp.where((gate >= 64) & (gate < 96), 1.0, 0.5)
    for dy in range(3):
        for dz in range(3):
            first = (9 * dy + 3 * dz) * 35
            for dx in range(3):
                at = first + 35 * dx
                block_f[32 * dx : 32 * dx + 32, :] = weight_f[at + 3 : at + 35, :]
                row = 96 + (3, 0, 8)[dx]
                block_f[row : row + 3, :] = weight_f[at : at + 3, :]
            if dy == 1 and dz == 1:
                rest = bias_ref[...]
                for part in range(3):
                    high = rest.astype(BF16).astype(F32)
                    block_f[112 + part : 113 + part, :] = high
                    rest = rest - high
            turned = (block_f[...].T * gate_scale).astype(BF16)
            if dy == 1 and dz == 1:
                block_f[112:120, :] = jnp.zeros((8, 128), F32)
            if dz == 0:
                side[0, :, 128 * dy : 128 * dy + 128] = turned
            if dz == 2:
                side[1, :, 128 * dy : 128 * dy + 128] = turned
            for z in range(2):
                own = z + dz - 1
                if 0 <= own < 2:
                    at = (2 * dy + own) * 128
                    wide[128 * z : 128 * z + 128, at : at + 128] = turned

    def inner(y):
        acc[y] = dot(wide[...], slabs[pl.ds(y, 3), 1:3].reshape(6 * SLAB, NX))

    def inner_step(y, carry):
        inner(y)
        return carry

    lax.fori_loop(1, 7, inner_step, 0)

    loads[3].wait()
    loads[5].wait()

    def own_cells(y, carry):
        for z in range(2):
            for t in range(2):
                cells[y, z, :, 128 * t : 128 * t + 128] = cell_v[
                    pl.ds(y * 4 + 2 * t + z, 32, stride=32), :
                ]
        return carry

    lax.fori_loop(0, 8, own_cells, 0)

    for k in range(2):
        copies["edge", k, 0].wait_recv()
        copies["edge", k, 1].wait_recv()
        rows = vy_r[k].astype(F32)
        y = 9 - 9 * k
        vels[y, 1] = rows[0:8]
        vels[y, 2] = rows[8:16]
        fill(y, 1)
        fill(y, 2)
    inner(0)
    inner(7)

    def update(y, carry):
        for z in range(2):
            outer = slabs[pl.ds(y, 3), 3 * z].reshape(3 * SLAB, NX)
            gates = acc[y, 128 * z : 128 * z + 128, :] + dot(side[z], outer)
            turned = jnp.tanh(gates)
            new = 0.5 * (
                (turned[32:64] + 1.0) * cells[y, z] + (turned[0:32] + 1.0) * turned[64:96]
            )
            cells[y, z] = new
            hids[y, z] = (0.5 * (turned[96:128] + 1.0) * jnp.tanh(new)).astype(BF16)
        return carry

    def fill_outer(y, carry):
        fill(y, 0)
        fill(y, 3)
        return carry

    for z in range(2):
        copies["side", z].wait_recv()
        to = 3 - 3 * z
        rows = vz_r[z].astype(F32)
        for t in range(2):
            vel_t[t] = rows[:, 128 * t : 128 * t + 128]
            for y in range(8):
                vels[y + 1, to, 0:3, 128 * t : 128 * t + 128] = vel_t[t, pl.ds(y, 3, stride=8), :]
    for part, ys, rows in ((0, (0, 5), (0, 3)), (1, (5, 10), (3, 8))):
        k = 1 - part
        for z in range(2):
            copies["plane", z, part].wait_recv()
            copies["corner", k, z, 0].wait_recv()
            copies["corner", k, z, 1].wait_recv()
            vels[9 - 9 * k, 3 - 3 * z] = vc_r[2 * k + z].astype(F32)[0:8]
        lax.fori_loop(*ys, fill_outer, 0)
        lax.fori_loop(*rows, update, 0)

    for y in range(8):
        for z in range(2):
            advanced = vels[y + 1, z + 1, 0:3, :] + dot(dec_ref[...], hids[y, z])
            for t in range(2):
                at = 16 * y + 8 * z
                moved[t, at : at + 3, :] = advanced[:, 128 * t : 128 * t + 128]
    for c in range(3):
        for z in range(2):
            for t in range(2):
                start = 16 * c + 8 * z
                u_ref[start : start + 8, 128 * t : 128 * t + 128] = moved[
                    t, pl.ds(8 * z + c, 8, stride=16), :
                ]

    def store_states():
        def turn(y, carry):
            for z in range(2):
                for t in range(2):
                    rows = pl.ds(y * 4 + 2 * t + z, 32, stride=32)
                    lanes = slice(128 * t, 128 * t + 128)
                    cell_v[rows, :] = cells[y, z, :, lanes]
                    hid_f[rows, :] = hids[y, z, :, lanes].astype(F32)
            return carry

        lax.fori_loop(0, 8, turn, 0)
        hid_in[...] = hid_f[...].astype(BF16)

    for load in loads[6:]:
        load.wait()
    project(u_ref, tables, vel_next, send, recv, tile_send_sem, tile_recv_sem, store_states)
    for copy in copies.values():
        copy.wait_send()


def hand_on_kernel(*refs):
    sources, results, sem = refs[:3], refs[3:6], refs[6]
    copies = [pltpu.make_async_copy(a, b, sem.at[i]) for i, (a, b) in enumerate(zip(sources, results))]
    for copy in copies:
        copy.start()
    for copy in copies:
        copy.wait()


def to_rows(array):
    c = array.shape[0]
    return array.reshape(c, 8, 2, 2, 128).transpose(0, 1, 3, 2, 4).reshape(c * 32, 128)


def from_rows(array):
    c = array.shape[0] // 32
    return array.reshape(c, 8, 2, 2, 128).transpose(0, 1, 3, 2, 4).reshape(c, 8, 2, 256)


def per_device(velocity, hidden, cell, gate_weight, gate_bias, decoder):
    anywhere = pl.BlockSpec(memory_space=pl.ANY)
    vmem = pl.BlockSpec(memory_space=pltpu.VMEM)
    tables = [halves(t) for t in (*x_tables(), *y_tables(), *z_tables())]
    results = (
        jax.ShapeDtypeStruct((1024, 128), BF16),
        jax.ShapeDtypeStruct((1024, 128), F32),
        jax.ShapeDtypeStruct((96, 128), F32),
    )
    outs = pl.pallas_call(
        step_kernel,
        out_shape=tuple(pltpu.VMEM(r.shape, r.dtype) for r in results),
        in_specs=[anywhere] * 12,
        out_specs=(vmem,) * 3,
        scratch_shapes=[
            *(pltpu.VMEM(t.shape, BF16) for t in tables),
            pltpu.VMEM((1, 128), F32),
            pltpu.VMEM((3, 32), BF16),
            pltpu.VMEM((48, 256), F32),
            pltpu.VMEM((1024, 128), F32),
            pltpu.VMEM((96, 128), F32),
            pltpu.VMEM((945, 128), BF16),
            pltpu.VMEM((952, 128), F32),
            pltpu.VMEM((128, 128), F32),
            pltpu.VMEM((256, 768), BF16),
            pltpu.VMEM((2, 128, 384), BF16),
            pltpu.VMEM((10, 4, SLAB, NX), BF16),
            pltpu.VMEM((10, 4, 8, NX), F32),
            pltpu.VMEM((2, 32, 128), F32),
            pltpu.VMEM((2, 32, NX), BF16),
            pltpu.VMEM((2, 32, NX), BF16),
            pltpu.VMEM((2, 16, NX), BF16),
            pltpu.VMEM((2, 16, NX), BF16),
            pltpu.VMEM((4, 16, NX), BF16),
            pltpu.VMEM((4, 16, NX), BF16),
            pltpu.VMEM((8, 256, 256), F32),
            pltpu.VMEM((8, 2, 32, NX), F32),
            pltpu.VMEM((8, 2, 32, NX), BF16),
            pltpu.VMEM((2, 128, 128), F32),
            pltpu.VMEM((4, RANKS, 8, 128), F32),
            pltpu.VMEM((4, RANKS, 8, 128), F32),
            pltpu.SemaphoreType.DMA((12,)),
            pltpu.SemaphoreType.DMA((8, 3)),
            pltpu.SemaphoreType.DMA((8, 3)),
            pltpu.SemaphoreType.DMA((4,)),
            pltpu.SemaphoreType.DMA((4,)),
        ],
        compiler_params=pltpu.CompilerParams(
            collective_id=0, has_side_effects=True, vmem_limit_bytes=58 * 1024 * 1024
        ),
    )(
        to_rows(velocity),
        to_rows(hidden),
        to_rows(cell),
        gate_weight.T,
        gate_bias.reshape(1, 128),
        decoder,
        *(jnp.asarray(t) for t in tables),
    )
    outs = pl.pallas_call(
        hand_on_kernel,
        out_shape=results,
        in_specs=[vmem] * 3,
        out_specs=(anywhere,) * 3,
        scratch_shapes=[pltpu.SemaphoreType.DMA((3,))],
        compiler_params=pltpu.CompilerParams(vmem_limit_bytes=1024 * 1024),
    )(*outs)
    return tuple(from_rows(out) for out in outs)


def solution(mesh):
    field = P(None, "gy", "gz", None)
    return jax.shard_map(
        per_device,
        mesh=mesh,
        in_specs=(field, field, field, P(), P(), P()),
        out_specs=(field, field, field),
        check_vma=False,
    )
```

```python
import functools

import jax
import jax.numpy as jnp
import numpy as np
from jax import lax
from jax.experimental import pallas as pl
from jax.experimental.pallas import tpu as pltpu
from jax.sharding import PartitionSpec as P

F32 = jnp.float32
BF16 = jnp.bfloat16
MESH = pl.DeviceIdType.MESH
NX, NY, NZ = 256, 128, 32
RANKS = 16
SLAB = 128
HALO = [(sy, sz) for sz in (-1, 1) for sy in (0, -1, 1)] + [(-1, 0), (1, 0)]


def halves(table):
    high = table.astype(np.float32).astype(jnp.bfloat16)
    low = (table - high.astype(np.float64)).astype(np.float32).astype(jnp.bfloat16)
    pair = np.stack([np.asarray(high), np.asarray(low)])
    if table.shape[1] == 256:
        pair = pair.reshape(2, -1, 2, 128).transpose(0, 2, 1, 3)
    return np.ascontiguousarray(pair)


def x_tables():
    mode = np.arange(128)
    n = np.arange(NX)
    angle = 2 * np.pi / NX * ((n[:, None] * mode[None, :]) % NX)
    sign = np.where(n % 2 == 0, 1.0, -1.0)
    imag = np.where(mode[None, :] == 0, sign[:, None], -np.sin(angle))
    forward = np.concatenate([np.cos(angle), imag], 1)
    weight = np.where(mode == 0, 1.0, 2.0) / NX
    inverse = forward.T * np.concatenate([weight, weight])[:, None]
    return forward, inverse


def real_waves(total):
    half = total // 2
    index = np.arange(total)
    return np.where(index < half, index, index - half).astype(np.float64)


def real_tables(total):
    half = total // 2
    cosines, sines = np.arange(half + 1), np.arange(1, half)
    place = np.arange(total)
    angle = 2 * np.pi / total * ((np.concatenate([cosines, sines])[:, None] * place[None, :]) % total)
    is_sine = np.arange(total)[:, None] > half
    analysis = np.where(is_sine, np.sin(angle), np.cos(angle))
    weight = np.full(total, 2.0 / total)
    weight[0] = weight[half] = 1.0 / total
    synthesis = analysis.T * weight[None, :]
    derivative = np.zeros((total, total))
    for k in range(1, half):
        derivative[k, half + k] = k
        derivative[half + k, k] = -k
    return analysis, synthesis, derivative


def y_tables():
    analysis, synthesis, derivative = real_tables(NY)
    forward = np.concatenate([analysis, derivative @ analysis], 0)
    inverse = np.concatenate([synthesis, -(synthesis @ derivative)], 0)
    return forward, inverse


def z_tables():
    analysis, synthesis, derivative = real_tables(NZ)
    lane = np.arange(NZ)
    z = (lane // 8 % 2) * 16 + (lane % 4) * 4 + (lane // 4 % 2) * 2 + lane // 16
    forward, inverse = np.zeros((128, 128)), np.zeros((128, 128))
    for c in range(3):
        lanes = slice(32 * c, 32 * c + 32)
        forward[lanes, :32] = (derivative @ analysis if c == 2 else analysis)[:, z].T
        inverse[:32, lanes] = (-(synthesis @ derivative) if c == 2 else synthesis)[z, :].T
    return forward, inverse


def split(value):
    high = value.astype(BF16)
    return high, (value - high.astype(F32)).astype(BF16)


def dot(a, b):
    return jnp.dot(a, b, preferred_element_type=F32)


def whole(table):
    if len(table.shape) == 3:
        return [table[0], table[1]]
    return [jnp.concatenate([table[part, 0], table[part, 1]], 1) for part in range(2)]


def data_by_table(value, table):
    table = whole(table)
    high, low = split(value)
    return dot(high, table[0]) + (dot(low, table[0]) + dot(high, table[1]))


def table_by_data(table, value):
    high, low = split(value)
    return dot(table[0], high) + (dot(table[0], low) + dot(table[1], high))


def roll_lanes(value, shift):
    return value if shift % 128 == 0 else pltpu.roll(value, shift % 128, 1)


def lane_mix(values, count, stride, base):
    digit = lax.broadcasted_iota(jnp.int32, (8, 128), 1) // stride % base
    masks = [digit == q for q in range(base)]
    rolled = [roll_lanes(v, r * stride) for r, v in enumerate(values)]
    outs = []
    for j in range(count):
        acc = rolled[0] if len(values) == base else jnp.zeros((8, 128), F32)
        for r, v in enumerate(rolled):
            if r or len(values) < base:
                acc = jnp.where(masks[(j + r) % base], v, acc)
        outs.append(roll_lanes(acc, -j * stride))
    return outs


def x_forward(rows, table):
    spectrum = data_by_table(rows, table)
    values = []
    for cz in range(6):
        part = [spectrum[8 * cz : 8 * cz + 8, 128 * p : 128 * p + 128] for p in range(2)]
        values += [-part[1], part[0]] if cz < 2 else part
    return lane_mix(values, RANKS, 8, 16)


def solve(tiles, yf_ref, yi_ref, zf_ref, zi_ref, wave_x):
    def swap(blocks, first_of, second_of):
        out = [None] * 16
        for low in range(4):
            mixed = lane_mix([blocks[first_of(low, i)] for i in range(4)], 4, 4, 4)
            for i in range(4):
                out[second_of(low, i)] = mixed[i]
        return out

    def by_source(low, i):
        return (i // 2) * 8 + low * 2 + i % 2

    def by_y(low, i):
        return i * 4 + low

    lane = lax.broadcasted_iota(jnp.int32, (NY, 128), 1)
    is_y = (lane >= 32) & (lane < 64)
    scale = jnp.where(lane < 32, wave_x, 1.0)
    rows = jnp.concatenate(swap(tiles, by_source, by_y), 0)
    out = table_by_data(yf_ref, rows)
    terms = jnp.where(is_y, out[NY:], out[:NY]) * scale
    divergence = data_by_table(terms, zf_ref)
    row = lax.broadcasted_iota(jnp.int32, (NY, 128), 0)
    wave_y = jnp.where(row < NY // 2, row, row - NY // 2).astype(F32)
    wave_z = jnp.where(lane < NZ // 2, lane, lane - NZ // 2).astype(F32)
    square = wave_x * wave_x + wave_y * wave_y + wave_z * wave_z
    potential = divergence / jnp.maximum(square, 1.0)
    out = table_by_data(yi_ref, data_by_table(potential, zi_ref))
    rows = jnp.where(is_y, out[NY:], out[:NY]) * scale
    return swap([rows[8 * i : 8 * i + 8] for i in range(16)], by_y, by_source)


def x_inverse(tiles, table):
    values = lane_mix(tiles, 12, 8, 16)
    rows = []
    for cz in range(6):
        pair = values[2 * cz : 2 * cz + 2]
        rows.append(jnp.concatenate([pair[1], -pair[0]] if cz < 2 else pair, 1))
    return data_by_table(jnp.concatenate(rows, 0), table)


def around(index, step):
    return lax.rem(index + step + RANKS, RANKS)


def positions():
    gy, gz = lax.axis_index("gy"), lax.axis_index("gz")
    y, z_low, z_high, x, core = gy // 4, gy % 4, gz // 8, gz // 2 % 4, gz % 2

    def first(index):
        return (index // 4 * 4 + z_low, z_high * 8 + index % 4 * 2 + core)

    def second(index):
        return (y * 4 + index // 2 % 4, index // 8 * 8 + x * 2 + index % 2)

    return (y * 4 + x, first), (z_high * 8 + z_low * 2 + core, second)


def project(u_ref, tables, out_ref, send, recv, send_sem, recv_sem, meanwhile):
    xf_ref, xi_ref, yf_ref, yi_ref, zf_ref, zi_ref = tables
    group_1, group_2 = positions()

    def exchange(step, group, tiles, meanwhile=None):
        me, place = group
        for j in range(RANKS):
            send[step, j] = tiles[j]

        for d in (8, 10, 9, 7, 6, 11, 5, 12, 4, 13, 3, 14, 2, 15, 1):
            to = around(me, d)
            pltpu.make_async_remote_copy(
                src_ref=send.at[step, to],
                dst_ref=recv.at[step, me],
                send_sem=send_sem.at[step],
                recv_sem=recv_sem.at[step],
                device_id=place(to),
                device_id_type=MESH,
            ).start()
        recv[step, pl.ds(me, 1)] = send[step, pl.ds(me, 1)]
        if meanwhile is not None:
            meanwhile()
        some = recv.at[step, pl.ds(0, RANKS - 1)]
        pltpu.make_async_copy(some, some, recv_sem.at[step]).wait()
        return [recv[step, j] for j in range(RANKS)]

    tiles = exchange(0, group_1, x_forward(u_ref[...], xf_ref), meanwhile)
    tiles = exchange(1, group_2, lane_mix(tiles, RANKS, 1, 16))
    wave_x = (group_1[0] * 8 + group_2[0] % 8).astype(F32)
    tiles = exchange(2, group_2, solve(tiles, yf_ref, yi_ref, zf_ref, zi_ref, wave_x))
    tiles = exchange(3, group_1, lane_mix(tiles, RANKS, 1, 16))
    gradient = x_inverse(tiles, xi_ref)
    result = u_ref[...] - gradient
    for c in range(3):
        for z in range(2):
            start = (2 * c + z) * 8
            for t in range(2):
                out_ref[pl.ds(c * 32 + 2 * t + z, 8, stride=4), :] = result[
                    start : start + 8, 128 * t : 128 * t + 128
                ]
    for step in range(4):
        some = send.at[step, pl.ds(0, RANKS - 1)]
        pltpu.make_async_copy(some, some, send_sem.at[step]).wait()


def step_kernel(
    vel_hbm, hid_hbm, cell_hbm, weight_hbm, bias_hbm, dec_hbm, *refs,
):
    tables_hbm, (hid_in, cell_v, vel_next) = refs[:6], refs[6:9]
    tables, refs = refs[9:15], refs[15:]
    (
        bias_ref, dec_ref, u_ref, hid_f, vel_f, weight_v, weight_f, block_f, wide, side, slabs, vels, vel_t,
        vz_s, vz_r, vy_s, vy_r, vc_s, vc_r, acc, cells, hids, moved, send, recv,
        load_sem, send_sem, recv_sem, tile_send_sem, tile_recv_sem,
    ) = refs
    gy, gz = lax.axis_index("gy"), lax.axis_index("gz")
    loads = [
        pltpu.make_async_copy(src, dst, load_sem.at[i])
        for i, (src, dst) in enumerate(
            [
                (hid_hbm, hid_in),
                (vel_hbm, vel_f),
                (weight_hbm, weight_v),
                (cell_hbm, cell_v),
                (bias_hbm, bias_ref),
                (dec_hbm, dec_ref),
                *zip(tables_hbm, tables),
            ]
        )
    ]
    for load in loads[:2]:
        load.start()
    barrier = pltpu.get_barrier_semaphore()
    targets = [(around(gy, sy), around(gz, sz)) for sy, sz in HALO]
    for target in targets:
        pl.semaphore_signal(barrier, inc=1, device_id=target, device_id_type=MESH)

    groups = positions()

    def greet(d, carry):
        for me, place in groups:
            pl.semaphore_signal(barrier, inc=1, device_id=place(around(me, d)), device_id_type=MESH)
        return carry

    lax.fori_loop(1, RANKS, greet, 0)
    vels[...] = jnp.zeros_like(vels)

    loads[0].wait()
    hid_f[...] = hid_in[...].astype(F32)
    loads[1].wait()

    def centre(y, carry):
        for z in range(2):
            for t in range(2):
                lanes = slice(128 * t, 128 * t + 128)
                rows = hid_f[pl.ds(y * 4 + 2 * t + z, 32, stride=32), :]
                slabs[y + 1, z + 1, 32:64, lanes] = rows.astype(BF16)
                vels[y + 1, z + 1, 0:3, lanes] = vel_f[pl.ds(y * 4 + 2 * t + z, 3, stride=32), :]
        return carry

    lax.fori_loop(0, 8, centre, 0)
    for z in range(2):
        for t in range(2):
            rows = vel_f[pl.ds(2 * t + z, 24, stride=4), :]
            rows = jnp.concatenate([rows, jnp.zeros((8, 128), F32)], 0)
            vz_s[z, :, 128 * t : 128 * t + 128] = rows.astype(BF16)
    for k in range(2):
        y = 1 + 7 * k
        vy_s[k] = jnp.concatenate([vels[y, 1], vels[y, 2]], 0).astype(BF16)
        for z in range(2):
            rows = jnp.concatenate([vels[y, z + 1], jnp.zeros((8, NX), F32)], 0)
            vc_s[2 * k + z] = rows.astype(BF16)

    pl.semaphore_wait(barrier, len(HALO) + 2 * (RANKS - 1))
    copies = {}

    def start_halo(name, i, n, src, dst):
        copies[name] = pltpu.make_async_remote_copy(
            src_ref=src,
            dst_ref=dst,
            send_sem=send_sem.at[i, n],
            recv_sem=recv_sem.at[i, n],
            device_id=targets[i],
            device_id_type=MESH,
        )
        copies[name].start()

    mids = pl.ds(32, 32)

    def send_plane(part):
        for i, (sy, sz) in enumerate(HALO):
            if sy == 0:
                z = (1 + sz) // 2
                ys = pl.ds(1 + 2 * part, 2)
                src, dst = slabs.at[ys, z + 1, mids], slabs.at[ys, 3 - 3 * z, mids]
                start_halo(("plane", z, part), i, part, src, dst)

    def send_edge(i):
        sy, sz = HALO[i]
        k, z = (1 + sy) // 2, (1 + sz) // 2
        if sz == 0:
            src, dst = slabs.at[1 + 7 * k, pl.ds(1, 2), mids], slabs.at[9 - 9 * k, pl.ds(1, 2), mids]
            start_halo(("edge", k, 0), i, 0, src, dst)
            start_halo(("edge", k, 1), i, 1, vy_s.at[k], vy_r.at[k])
        else:
            src, dst = slabs.at[1 + 7 * k, 1 + z, mids], slabs.at[9 - 9 * k, 3 - 3 * z, mids]
            start_halo(("corner", k, z, 0), i, 0, src, dst)
            start_halo(("corner", k, z, 1), i, 1, vc_s.at[2 * k + z], vc_r.at[2 * k + z])

    send_plane(0)
    for i, (sy, sz) in enumerate(HALO):
        if sy == 0:
            z = (1 + sz) // 2
            start_halo(("side", z), i, 4, vz_s.at[z], vz_r.at[z])
    for wanted in ((1, True), (-1, False), (1, False)):
        for i, (sy, sz) in enumerate(HALO):
            if (sy, sz != 0) == wanted:
                send_edge(i)
    send_plane(1)
    send_plane(2)
    for i, (sy, sz) in enumerate(HALO):
        if sy == -1 and sz != 0:
            send_edge(i)
    send_plane(3)

    for load in loads[2:]:
        load.start()

    def fill(y, z):
        mid = slabs[y, z, 32:64, :]
        slabs[y, z, 0:32, :] = pltpu.roll(mid, 1, 1)
        slabs[y, z, 64:96, :] = pltpu.roll(mid, NX - 1, 1)
        v = vels[y, z]
        first = v + pltpu.roll(pltpu.roll(v, 1, 1), 3, 0)
        tile = jnp.concatenate([first, pltpu.roll(v, NX - 1, 1), jnp.ones((16, NX), F32)], 0)
        slabs[y, z, 96:128, :] = tile.astype(BF16)

    def fill_own(y, carry):
        fill(y, 1)
        fill(y, 2)
        return carry

    lax.fori_loop(1, 9, fill_own, 0)

    loads[2].wait()
    loads[4].wait()
    weight_f[0:945, :] = weight_v[...].astype(F32)
    block_f[96:128, :] = jnp.zeros((32, 128), F32)
    gate = lax.broadcasted_iota(jnp.int32, (128, 128), 0)
    gate_scale = jnp.where((gate >= 64) & (gate < 96), 1.0, 0.5)
    for dy in range(3):
        for dz in range(3):
            first = (9 * dy + 3 * dz) * 35
            for dx in range(3):
                at = first + 35 * dx
                block_f[32 * dx : 32 * dx + 32, :] = weight_f[at + 3 : at + 35, :]
                row = 96 + (3, 0, 8)[dx]
                block_f[row : row + 3, :] = weight_f[at : at + 3, :]
            if dy == 1 and dz == 1:
                rest = bias_ref[...]
                for part in range(3):
                    high = rest.astype(BF16).astype(F32)
                    block_f[112 + part : 113 + part, :] = high
                    rest = rest - high
            turned = (block_f[...].T * gate_scale).astype(BF16)
            if dy == 1 and dz == 1:
                block_f[112:120, :] = jnp.zeros((8, 128), F32)
            if dz == 0:
                side[0, :, 128 * dy : 128 * dy + 128] = turned
            if dz == 2:
                side[1, :, 128 * dy : 128 * dy + 128] = turned
            for z in range(2):
                own = z + dz - 1
                if 0 <= own < 2:
                    at = (2 * dy + own) * 128
                    wide[128 * z : 128 * z + 128, at : at + 128] = turned

    def inner(y):
        acc[y] = dot(wide[...], slabs[pl.ds(y, 3), 1:3].reshape(6 * SLAB, NX))

    def inner_step(y, carry):
        inner(y)
        return carry

    lax.fori_loop(1, 7, inner_step, 0)

    loads[3].wait()
    loads[5].wait()

    def own_cells(y, carry):
        for z in range(2):
            for t in range(2):
                cells[y, z, :, 128 * t : 128 * t + 128] = cell_v[
                    pl.ds(y * 4 + 2 * t + z, 32, stride=32), :
                ]
        return carry

    lax.fori_loop(0, 8, own_cells, 0)

    for k in range(2):
        copies["edge", k, 0].wait_recv()
        copies["edge", k, 1].wait_recv()
        rows = vy_r[k].astype(F32)
        y = 9 - 9 * k
        vels[y, 1] = rows[0:8]
        vels[y, 2] = rows[8:16]
        fill(y, 1)
        fill(y, 2)
    inner(0)
    inner(7)

    def update(y, carry):
        for z in range(2):
            outer = slabs[pl.ds(y, 3), 3 * z].reshape(3 * SLAB, NX)
            gates = acc[y, 128 * z : 128 * z + 128, :] + dot(side[z], outer)
            turned = jnp.tanh(gates)
            new = 0.5 * (
                (turned[32:64] + 1.0) * cells[y, z] + (turned[0:32] + 1.0) * turned[64:96]
            )
            cells[y, z] = new
            hids[y, z] = (0.5 * (turned[96:128] + 1.0) * jnp.tanh(new)).astype(BF16)
        return carry

    def fill_outer(y, carry):
        fill(y, 0)
        fill(y, 3)
        return carry

    for z in range(2):
        copies["side", z].wait_recv()
        to = 3 - 3 * z
        rows = vz_r[z].astype(F32)
        for t in range(2):
            vel_t[t] = rows[:, 128 * t : 128 * t + 128]
            for y in range(8):
                vels[y + 1, to, 0:3, 128 * t : 128 * t + 128] = vel_t[t, pl.ds(y, 3, stride=8), :]
    for part, ys, rows in (
        (0, (0, 3), (0, 1)), (1, (3, 5), (1, 3)), (2, (5, 7), (3, 5)), (3, (7, 10), (5, 8))
    ):
        for z in range(2):
            copies["plane", z, part].wait_recv()
            if part in (0, 3):
                k = 1 - part // 3
                copies["corner", k, z, 0].wait_recv()
                copies["corner", k, z, 1].wait_recv()
                vels[9 - 9 * k, 3 - 3 * z] = vc_r[2 * k + z].astype(F32)[0:8]
        for y in range(*ys):
            fill_outer(y, 0)
        for y in range(*rows):
            update(y, 0)

    for y in range(8):
        for z in range(2):
            advanced = vels[y + 1, z + 1, 0:3, :] + dot(dec_ref[...], hids[y, z])
            for t in range(2):
                at = 16 * y + 8 * z
                moved[t, at : at + 3, :] = advanced[:, 128 * t : 128 * t + 128]
    for c in range(3):
        for z in range(2):
            for t in range(2):
                start = 16 * c + 8 * z
                u_ref[start : start + 8, 128 * t : 128 * t + 128] = moved[
                    t, pl.ds(8 * z + c, 8, stride=16), :
                ]

    def store_states():
        def turn(y, carry):
            for z in range(2):
                for t in range(2):
                    rows = pl.ds(y * 4 + 2 * t + z, 32, stride=32)
                    lanes = slice(128 * t, 128 * t + 128)
                    cell_v[rows, :] = cells[y, z, :, lanes]
                    hid_f[rows, :] = hids[y, z, :, lanes].astype(F32)
            return carry

        lax.fori_loop(0, 8, turn, 0)
        hid_in[...] = hid_f[...].astype(BF16)

    for load in loads[6:]:
        load.wait()
    project(u_ref, tables, vel_next, send, recv, tile_send_sem, tile_recv_sem, store_states)
    for copy in copies.values():
        copy.wait_send()


def hand_on_kernel(*refs):
    sources, results, sem = refs[:3], refs[3:6], refs[6]
    copies = [pltpu.make_async_copy(a, b, sem.at[i]) for i, (a, b) in enumerate(zip(sources, results))]
    for copy in copies:
        copy.start()
    for copy in copies:
        copy.wait()


def to_rows(array):
    c = array.shape[0]
    return array.reshape(c, 8, 2, 2, 128).transpose(0, 1, 3, 2, 4).reshape(c * 32, 128)


def from_rows(array):
    c = array.shape[0] // 32
    return array.reshape(c, 8, 2, 2, 128).transpose(0, 1, 3, 2, 4).reshape(c, 8, 2, 256)


def per_device(velocity, hidden, cell, gate_weight, gate_bias, decoder):
    anywhere = pl.BlockSpec(memory_space=pl.ANY)
    vmem = pl.BlockSpec(memory_space=pltpu.VMEM)
    tables = [halves(t) for t in (*x_tables(), *y_tables(), *z_tables())]
    results = (
        jax.ShapeDtypeStruct((1024, 128), BF16),
        jax.ShapeDtypeStruct((1024, 128), F32),
        jax.ShapeDtypeStruct((96, 128), F32),
    )
    outs = pl.pallas_call(
        step_kernel,
        out_shape=tuple(pltpu.VMEM(r.shape, r.dtype) for r in results),
        in_specs=[anywhere] * 12,
        out_specs=(vmem,) * 3,
        scratch_shapes=[
            *(pltpu.VMEM(t.shape, BF16) for t in tables),
            pltpu.VMEM((1, 128), F32),
            pltpu.VMEM((3, 32), BF16),
            pltpu.VMEM((48, 256), F32),
            pltpu.VMEM((1024, 128), F32),
            pltpu.VMEM((96, 128), F32),
            pltpu.VMEM((945, 128), BF16),
            pltpu.VMEM((952, 128), F32),
            pltpu.VMEM((128, 128), F32),
            pltpu.VMEM((256, 768), BF16),
            pltpu.VMEM((2, 128, 384), BF16),
            pltpu.VMEM((10, 4, SLAB, NX), BF16),
            pltpu.VMEM((10, 4, 8, NX), F32),
            pltpu.VMEM((2, 32, 128), F32),
            pltpu.VMEM((2, 32, NX), BF16),
            pltpu.VMEM((2, 32, NX), BF16),
            pltpu.VMEM((2, 16, NX), BF16),
            pltpu.VMEM((2, 16, NX), BF16),
            pltpu.VMEM((4, 16, NX), BF16),
            pltpu.VMEM((4, 16, NX), BF16),
            pltpu.VMEM((8, 256, 256), F32),
            pltpu.VMEM((8, 2, 32, NX), F32),
            pltpu.VMEM((8, 2, 32, NX), BF16),
            pltpu.VMEM((2, 128, 128), F32),
            pltpu.VMEM((4, RANKS, 8, 128), F32),
            pltpu.VMEM((4, RANKS, 8, 128), F32),
            pltpu.SemaphoreType.DMA((12,)),
            pltpu.SemaphoreType.DMA((8, 5)),
            pltpu.SemaphoreType.DMA((8, 5)),
            pltpu.SemaphoreType.DMA((4,)),
            pltpu.SemaphoreType.DMA((4,)),
        ],
        compiler_params=pltpu.CompilerParams(
            collective_id=0, has_side_effects=True, vmem_limit_bytes=58 * 1024 * 1024
        ),
    )(
        to_rows(velocity),
        to_rows(hidden),
        to_rows(cell),
        gate_weight.T,
        gate_bias.reshape(1, 128),
        decoder,
        *(jnp.asarray(t) for t in tables),
    )
    outs = pl.pallas_call(
        hand_on_kernel,
        out_shape=results,
        in_specs=[vmem] * 3,
        out_specs=(anywhere,) * 3,
        scratch_shapes=[pltpu.SemaphoreType.DMA((3,))],
        compiler_params=pltpu.CompilerParams(vmem_limit_bytes=1024 * 1024),
    )(*outs)
    return tuple(from_rows(out) for out in outs)


def solution(mesh):
    field = P(None, "gy", "gz", None)
    return jax.shard_map(
        per_device,
        mesh=mesh,
        in_specs=(field, field, field, P(), P(), P()),
        out_specs=(field, field, field),
        check_vma=False,
    )
```

```python
import functools

import jax
import jax.numpy as jnp
import numpy as np
from jax import lax
from jax.experimental import pallas as pl
from jax.experimental.pallas import tpu as pltpu
from jax.sharding import PartitionSpec as P

F32 = jnp.float32
BF16 = jnp.bfloat16
MESH = pl.DeviceIdType.MESH
NX, NY, NZ = 256, 128, 32
RANKS = 16
SLAB = 128
HALO = [(sy, sz) for sz in (-1, 1) for sy in (0, -1, 1)] + [(-1, 0), (1, 0)]


def halves(table):
    high = table.astype(np.float32).astype(jnp.bfloat16)
    low = (table - high.astype(np.float64)).astype(np.float32).astype(jnp.bfloat16)
    pair = np.stack([np.asarray(high), np.asarray(low)])
    if table.shape[1] == 256:
        pair = pair.reshape(2, -1, 2, 128).transpose(0, 2, 1, 3)
    return np.ascontiguousarray(pair)


def x_tables():
    mode = np.arange(128)
    n = np.arange(NX)
    angle = 2 * np.pi / NX * ((n[:, None] * mode[None, :]) % NX)
    sign = np.where(n % 2 == 0, 1.0, -1.0)
    imag = np.where(mode[None, :] == 0, sign[:, None], -np.sin(angle))
    forward = np.concatenate([np.cos(angle), imag], 1)
    weight = np.where(mode == 0, 1.0, 2.0) / NX
    inverse = forward.T * np.concatenate([weight, weight])[:, None]
    return forward, inverse


def real_waves(total):
    half = total // 2
    index = np.arange(total)
    return np.where(index < half, index, index - half).astype(np.float64)


def real_tables(total):
    half = total // 2
    cosines, sines = np.arange(half + 1), np.arange(1, half)
    place = np.arange(total)
    angle = 2 * np.pi / total * ((np.concatenate([cosines, sines])[:, None] * place[None, :]) % total)
    is_sine = np.arange(total)[:, None] > half
    analysis = np.where(is_sine, np.sin(angle), np.cos(angle))
    weight = np.full(total, 2.0 / total)
    weight[0] = weight[half] = 1.0 / total
    synthesis = analysis.T * weight[None, :]
    derivative = np.zeros((total, total))
    for k in range(1, half):
        derivative[k, half + k] = k
        derivative[half + k, k] = -k
    return analysis, synthesis, derivative


def y_tables():
    analysis, synthesis, derivative = real_tables(NY)
    forward = np.concatenate([analysis, derivative @ analysis], 0)
    inverse = np.concatenate([synthesis, -(synthesis @ derivative)], 0)
    return forward, inverse


def z_tables():
    analysis, synthesis, derivative = real_tables(NZ)
    lane = np.arange(NZ)
    z = (lane // 8 % 2) * 16 + (lane % 4) * 4 + (lane // 4 % 2) * 2 + lane // 16
    forward, inverse = np.zeros((128, 128)), np.zeros((128, 128))
    for c in range(3):
        lanes = slice(32 * c, 32 * c + 32)
        forward[lanes, :32] = (derivative @ analysis if c == 2 else analysis)[:, z].T
        inverse[:32, lanes] = (-(synthesis @ derivative) if c == 2 else synthesis)[z, :].T
    return forward, inverse


def split(value):
    high = value.astype(BF16)
    return high, (value - high.astype(F32)).astype(BF16)


def dot(a, b):
    return jnp.dot(a, b, preferred_element_type=F32)


def whole(table):
    if len(table.shape) == 3:
        return [table[0], table[1]]
    return [jnp.concatenate([table[part, 0], table[part, 1]], 1) for part in range(2)]


def data_by_table(value, table):
    table = whole(table)
    high, low = split(value)
    return dot(high, table[0]) + (dot(low, table[0]) + dot(high, table[1]))


def table_by_data(table, value):
    high, low = split(value)
    return dot(table[0], high) + (dot(table[0], low) + dot(table[1], high))


def roll_lanes(value, shift):
    return value if shift % 128 == 0 else pltpu.roll(value, shift % 128, 1)


def lane_mix(values, count, stride, base):
    digit = lax.broadcasted_iota(jnp.int32, (8, 128), 1) // stride % base
    masks = [digit == q for q in range(base)]
    rolled = [roll_lanes(v, r * stride) for r, v in enumerate(values)]
    outs = []
    for j in range(count):
        acc = rolled[0] if len(values) == base else jnp.zeros((8, 128), F32)
        for r, v in enumerate(rolled):
            if r or len(values) < base:
                acc = jnp.where(masks[(j + r) % base], v, acc)
        outs.append(roll_lanes(acc, -j * stride))
    return outs


def x_forward(rows, table):
    spectrum = data_by_table(rows, table)
    values = []
    for cz in range(6):
        part = [spectrum[8 * cz : 8 * cz + 8, 128 * p : 128 * p + 128] for p in range(2)]
        values += [-part[1], part[0]] if cz < 2 else part
    return lane_mix(values, RANKS, 8, 16)


def solve(tiles, yf_ref, yi_ref, zf_ref, zi_ref, wave_x):
    def swap(blocks, first_of, second_of):
        out = [None] * 16
        for low in range(4):
            mixed = lane_mix([blocks[first_of(low, i)] for i in range(4)], 4, 4, 4)
            for i in range(4):
                out[second_of(low, i)] = mixed[i]
        return out

    def by_source(low, i):
        return (i // 2) * 8 + low * 2 + i % 2

    def by_y(low, i):
        return i * 4 + low

    lane = lax.broadcasted_iota(jnp.int32, (NY, 128), 1)
    is_y = (lane >= 32) & (lane < 64)
    scale = jnp.where(lane < 32, wave_x, 1.0)
    rows = jnp.concatenate(swap(tiles, by_source, by_y), 0)
    out = table_by_data(yf_ref, rows)
    terms = jnp.where(is_y, out[NY:], out[:NY]) * scale
    divergence = data_by_table(terms, zf_ref)
    row = lax.broadcasted_iota(jnp.int32, (NY, 128), 0)
    wave_y = jnp.where(row < NY // 2, row, row - NY // 2).astype(F32)
    wave_z = jnp.where(lane < NZ // 2, lane, lane - NZ // 2).astype(F32)
    square = wave_x * wave_x + wave_y * wave_y + wave_z * wave_z
    potential = divergence / jnp.maximum(square, 1.0)
    out = table_by_data(yi_ref, data_by_table(potential, zi_ref))
    rows = jnp.where(is_y, out[NY:], out[:NY]) * scale
    return swap([rows[8 * i : 8 * i + 8] for i in range(16)], by_y, by_source)


def x_inverse(tiles, table):
    values = lane_mix(tiles, 12, 8, 16)
    rows = []
    for cz in range(6):
        pair = values[2 * cz : 2 * cz + 2]
        rows.append(jnp.concatenate([pair[1], -pair[0]] if cz < 2 else pair, 1))
    return data_by_table(jnp.concatenate(rows, 0), table)


def around(index, step):
    return lax.rem(index + step + RANKS, RANKS)


def ring(step, length):
    return min(step, length - step)


def positions():
    gy, gz = lax.axis_index("gy"), lax.axis_index("gz")
    y, z_low, z_high, x, core = gy // 4, gy % 4, gz // 8, gz // 2 % 4, gz % 2

    def first(index):
        return (index // 4 * 4 + z_low, z_high * 8 + index % 4 * 2 + core)

    def second(index):
        return (y * 4 + index // 2 % 4, index // 8 * 8 + x * 2 + index % 2)

    z = z_high * 4 + z_low
    first_others = [
        lax.rem(y + dy, 4) * 4 + lax.rem(x + dx, 4)
        for dy, dx in sorted(np.ndindex(4, 4), key=lambda d: -ring(d[0], 4) - ring(d[1], 4))[:-1]
    ]
    second_others = [
        lax.rem(z + dz, 8) * 2 + lax.rem(core + dc, 2)
        for dz, dc in sorted(np.ndindex(8, 2), key=lambda d: -ring(d[0], 8) - d[1])[:-1]
    ]
    return (y * 4 + x, first, first_others), (z * 2 + core, second, second_others)


def project(u_ref, tables, out_ref, send, recv, send_sem, recv_sem, meanwhile):
    xf_ref, xi_ref, yf_ref, yi_ref, zf_ref, zi_ref = tables
    group_1, group_2 = positions()

    def exchange(step, group, tiles, meanwhile=None):
        me, place, others = group
        for j in range(RANKS):
            send[step, j] = tiles[j]

        for to in others:
            pltpu.make_async_remote_copy(
                src_ref=send.at[step, to],
                dst_ref=recv.at[step, me],
                send_sem=send_sem.at[step],
                recv_sem=recv_sem.at[step],
                device_id=place(to),
                device_id_type=MESH,
            ).start()
        recv[step, pl.ds(me, 1)] = send[step, pl.ds(me, 1)]
        if meanwhile is not None:
            meanwhile()
        some = recv.at[step, pl.ds(0, RANKS - 1)]
        pltpu.make_async_copy(some, some, recv_sem.at[step]).wait()
        return [recv[step, j] for j in range(RANKS)]

    tiles = exchange(0, group_1, x_forward(u_ref[...], xf_ref), meanwhile)
    tiles = exchange(1, group_2, lane_mix(tiles, RANKS, 1, 16))
    wave_x = (group_1[0] * 8 + group_2[0] % 8).astype(F32)
    tiles = exchange(2, group_2, solve(tiles, yf_ref, yi_ref, zf_ref, zi_ref, wave_x))
    tiles = exchange(3, group_1, lane_mix(tiles, RANKS, 1, 16))
    gradient = x_inverse(tiles, xi_ref)
    result = u_ref[...] - gradient
    for c in range(3):
        for z in range(2):
            start = (2 * c + z) * 8
            for t in range(2):
                out_ref[pl.ds(c * 32 + 2 * t + z, 8, stride=4), :] = result[
                    start : start + 8, 128 * t : 128 * t + 128
                ]
    for step in range(4):
        some = send.at[step, pl.ds(0, RANKS - 1)]
        pltpu.make_async_copy(some, some, send_sem.at[step]).wait()


def step_kernel(
    vel_hbm, hid_hbm, cell_hbm, weight_hbm, bias_hbm, dec_hbm, *refs,
):
    tables_hbm, (hid_in, cell_v, vel_next) = refs[:6], refs[6:9]
    tables, refs = refs[9:15], refs[15:]
    (
        bias_ref, dec_ref, u_ref, hid_f, vel_f, weight_v, weight_f, block_f, wide, side, slabs, vels, vel_t,
        vz_s, vz_r, vy_s, vy_r, vc_s, vc_r, acc, cells, hids, moved, send, recv,
        load_sem, send_sem, recv_sem, tile_send_sem, tile_recv_sem,
    ) = refs
    gy, gz = lax.axis_index("gy"), lax.axis_index("gz")
    loads = [
        pltpu.make_async_copy(src, dst, load_sem.at[i])
        for i, (src, dst) in enumerate(
            [
                (hid_hbm, hid_in),
                (vel_hbm, vel_f),
                (weight_hbm, weight_v),
                (cell_hbm, cell_v),
                (bias_hbm, bias_ref),
                (dec_hbm, dec_ref),
                *zip(tables_hbm, tables),
            ]
        )
    ]
    for load in loads[:2]:
        load.start()
    barrier = pltpu.get_barrier_semaphore()
    targets = [(around(gy, sy), around(gz, sz)) for sy, sz in HALO]
    for target in targets:
        pl.semaphore_signal(barrier, inc=1, device_id=target, device_id_type=MESH)

    for _, place, others in positions():
        for to in others:
            pl.semaphore_signal(barrier, inc=1, device_id=place(to), device_id_type=MESH)
    vels[...] = jnp.zeros_like(vels)

    loads[0].wait()
    hid_f[...] = hid_in[...].astype(F32)
    loads[1].wait()

    def centre(y, carry):
        for z in range(2):
            for t in range(2):
                lanes = slice(128 * t, 128 * t + 128)
                rows = hid_f[pl.ds(y * 4 + 2 * t + z, 32, stride=32), :]
                slabs[y + 1, z + 1, 32:64, lanes] = rows.astype(BF16)
                vels[y + 1, z + 1, 0:3, lanes] = vel_f[pl.ds(y * 4 + 2 * t + z, 3, stride=32), :]
        return carry

    lax.fori_loop(0, 8, centre, 0)
    for z in range(2):
        for t in range(2):
            rows = vel_f[pl.ds(2 * t + z, 24, stride=4), :]
            rows = jnp.concatenate([rows, jnp.zeros((8, 128), F32)], 0)
            vz_s[z, :, 128 * t : 128 * t + 128] = rows.astype(BF16)
    for k in range(2):
        y = 1 + 7 * k
        vy_s[k] = jnp.concatenate([vels[y, 1], vels[y, 2]], 0).astype(BF16)
        for z in range(2):
            rows = jnp.concatenate([vels[y, z + 1], jnp.zeros((8, NX), F32)], 0)
            vc_s[2 * k + z] = rows.astype(BF16)

    pl.semaphore_wait(barrier, len(HALO) + 2 * (RANKS - 1))
    copies = {}

    def start_halo(name, i, n, src, dst):
        copies[name] = pltpu.make_async_remote_copy(
            src_ref=src,
            dst_ref=dst,
            send_sem=send_sem.at[i, n],
            recv_sem=recv_sem.at[i, n],
            device_id=targets[i],
            device_id_type=MESH,
        )
        copies[name].start()

    mids = pl.ds(32, 32)

    def send_plane(part):
        for i, (sy, sz) in enumerate(HALO):
            if sy == 0:
                z = (1 + sz) // 2
                ys = pl.ds(1 + 2 * part, 2)
                src, dst = slabs.at[ys, z + 1, mids], slabs.at[ys, 3 - 3 * z, mids]
                start_halo(("plane", z, part), i, part, src, dst)

    def send_edge(i):
        sy, sz = HALO[i]
        k, z = (1 + sy) // 2, (1 + sz) // 2
        if sz == 0:
            src, dst = slabs.at[1 + 7 * k, pl.ds(1, 2), mids], slabs.at[9 - 9 * k, pl.ds(1, 2), mids]
            start_halo(("edge", k, 0), i, 0, src, dst)
            start_halo(("edge", k, 1), i, 1, vy_s.at[k], vy_r.at[k])
        else:
            src, dst = slabs.at[1 + 7 * k, 1 + z, mids], slabs.at[9 - 9 * k, 3 - 3 * z, mids]
            start_halo(("corner", k, z, 0), i, 0, src, dst)
            start_halo(("corner", k, z, 1), i, 1, vc_s.at[2 * k + z], vc_r.at[2 * k + z])

    send_plane(0)
    for i, (sy, sz) in enumerate(HALO):
        if sy == 0:
            z = (1 + sz) // 2
            start_halo(("side", z), i, 4, vz_s.at[z], vz_r.at[z])
    for wanted in ((1, True), (-1, False), (1, False)):
        for i, (sy, sz) in enumerate(HALO):
            if (sy, sz != 0) == wanted:
                send_edge(i)
    send_plane(1)
    send_plane(2)
    for i, (sy, sz) in enumerate(HALO):
        if sy == -1 and sz != 0:
            send_edge(i)
    send_plane(3)

    for load in loads[2:]:
        load.start()

    def fill(y, z):
        mid = slabs[y, z, 32:64, :]
        slabs[y, z, 0:32, :] = pltpu.roll(mid, 1, 1)
        slabs[y, z, 64:96, :] = pltpu.roll(mid, NX - 1, 1)
        v = vels[y, z]
        first = v + pltpu.roll(pltpu.roll(v, 1, 1), 3, 0)
        tile = jnp.concatenate([first, pltpu.roll(v, NX - 1, 1), jnp.ones((16, NX), F32)], 0)
        slabs[y, z, 96:128, :] = tile.astype(BF16)

    def fill_own(y, carry):
        fill(y, 1)
        fill(y, 2)
        return carry

    lax.fori_loop(1, 9, fill_own, 0)

    loads[2].wait()
    loads[4].wait()
    weight_f[0:945, :] = weight_v[...].astype(F32)
    block_f[96:128, :] = jnp.zeros((32, 128), F32)
    gate = lax.broadcasted_iota(jnp.int32, (128, 128), 0)
    gate_scale = jnp.where((gate >= 64) & (gate < 96), 1.0, 0.5)
    for dy in range(3):
        for dz in range(3):
            first = (9 * dy + 3 * dz) * 35
            for dx in range(3):
                at = first + 35 * dx
                block_f[32 * dx : 32 * dx + 32, :] = weight_f[at + 3 : at + 35, :]
                row = 96 + (3, 0, 8)[dx]
                block_f[row : row + 3, :] = weight_f[at : at + 3, :]
            if dy == 1 and dz == 1:
                rest = bias_ref[...]
                for part in range(3):
                    high = rest.astype(BF16).astype(F32)
                    block_f[112 + part : 113 + part, :] = high
                    rest = rest - high
            turned = (block_f[...].T * gate_scale).astype(BF16)
            if dy == 1 and dz == 1:
                block_f[112:120, :] = jnp.zeros((8, 128), F32)
            if dz == 0:
                side[0, :, 128 * dy : 128 * dy + 128] = turned
            if dz == 2:
                side[1, :, 128 * dy : 128 * dy + 128] = turned
            for z in range(2):
                own = z + dz - 1
                if 0 <= own < 2:
                    at = (2 * dy + own) * 128
                    wide[128 * z : 128 * z + 128, at : at + 128] = turned

    def inner(y):
        acc[y] = dot(wide[...], slabs[pl.ds(y, 3), 1:3].reshape(6 * SLAB, NX))

    def inner_step(y, carry):
        inner(y)
        return carry

    lax.fori_loop(1, 7, inner_step, 0)

    loads[3].wait()
    loads[5].wait()

    def own_cells(y, carry):
        for z in range(2):
            for t in range(2):
                cells[y, z, :, 128 * t : 128 * t + 128] = cell_v[
                    pl.ds(y * 4 + 2 * t + z, 32, stride=32), :
                ]
        return carry

    lax.fori_loop(0, 8, own_cells, 0)

    for k in range(2):
        copies["edge", k, 0].wait_recv()
        copies["edge", k, 1].wait_recv()
        rows = vy_r[k].astype(F32)
        y = 9 - 9 * k
        vels[y, 1] = rows[0:8]
        vels[y, 2] = rows[8:16]
        fill(y, 1)
        fill(y, 2)
    inner(0)
    inner(7)

    def update(y, carry):
        for z in range(2):
            outer = slabs[pl.ds(y, 3), 3 * z].reshape(3 * SLAB, NX)
            gates = acc[y, 128 * z : 128 * z + 128, :] + dot(side[z], outer)
            turned = jnp.tanh(gates)
            new = 0.5 * (
                (turned[32:64] + 1.0) * cells[y, z] + (turned[0:32] + 1.0) * turned[64:96]
            )
            cells[y, z] = new
            hids[y, z] = (0.5 * (turned[96:128] + 1.0) * jnp.tanh(new)).astype(BF16)
        return carry

    def fill_outer(y, carry):
        fill(y, 0)
        fill(y, 3)
        return carry

    for z in range(2):
        copies["side", z].wait_recv()
        to = 3 - 3 * z
        rows = vz_r[z].astype(F32)
        for t in range(2):
            vel_t[t] = rows[:, 128 * t : 128 * t + 128]
            for y in range(8):
                vels[y + 1, to, 0:3, 128 * t : 128 * t + 128] = vel_t[t, pl.ds(y, 3, stride=8), :]
    for part, ys, rows in (
        (0, (0, 3), (0, 1)), (1, (3, 5), (1, 3)), (2, (5, 7), (3, 5)), (3, (7, 10), (5, 8))
    ):
        for z in range(2):
            copies["plane", z, part].wait_recv()
            if part in (0, 3):
                k = 1 - part // 3
                copies["corner", k, z, 0].wait_recv()
                copies["corner", k, z, 1].wait_recv()
                vels[9 - 9 * k, 3 - 3 * z] = vc_r[2 * k + z].astype(F32)[0:8]
        for y in range(*ys):
            fill_outer(y, 0)
        for y in range(*rows):
            update(y, 0)

    for y in range(8):
        for z in range(2):
            advanced = vels[y + 1, z + 1, 0:3, :] + dot(dec_ref[...], hids[y, z])
            for t in range(2):
                at = 16 * y + 8 * z
                moved[t, at : at + 3, :] = advanced[:, 128 * t : 128 * t + 128]
    for c in range(3):
        for z in range(2):
            for t in range(2):
                start = 16 * c + 8 * z
                u_ref[start : start + 8, 128 * t : 128 * t + 128] = moved[
                    t, pl.ds(8 * z + c, 8, stride=16), :
                ]

    def store_states():
        def turn(y, carry):
            for z in range(2):
                for t in range(2):
                    rows = pl.ds(y * 4 + 2 * t + z, 32, stride=32)
                    lanes = slice(128 * t, 128 * t + 128)
                    cell_v[rows, :] = cells[y, z, :, lanes]
                    hid_f[rows, :] = hids[y, z, :, lanes].astype(F32)
            return carry

        lax.fori_loop(0, 8, turn, 0)
        hid_in[...] = hid_f[...].astype(BF16)

    for load in loads[6:]:
        load.wait()
    project(u_ref, tables, vel_next, send, recv, tile_send_sem, tile_recv_sem, store_states)
    for copy in copies.values():
        copy.wait_send()


def hand_on_kernel(*refs):
    sources, results, sem = refs[:3], refs[3:6], refs[6]
    copies = [pltpu.make_async_copy(a, b, sem.at[i]) for i, (a, b) in enumerate(zip(sources, results))]
    for copy in copies:
        copy.start()
    for copy in copies:
        copy.wait()


def to_rows(array):
    c = array.shape[0]
    return array.reshape(c, 8, 2, 2, 128).transpose(0, 1, 3, 2, 4).reshape(c * 32, 128)


def from_rows(array):
    c = array.shape[0] // 32
    return array.reshape(c, 8, 2, 2, 128).transpose(0, 1, 3, 2, 4).reshape(c, 8, 2, 256)


def per_device(velocity, hidden, cell, gate_weight, gate_bias, decoder):
    anywhere = pl.BlockSpec(memory_space=pl.ANY)
    vmem = pl.BlockSpec(memory_space=pltpu.VMEM)
    tables = [halves(t) for t in (*x_tables(), *y_tables(), *z_tables())]
    results = (
        jax.ShapeDtypeStruct((1024, 128), BF16),
        jax.ShapeDtypeStruct((1024, 128), F32),
        jax.ShapeDtypeStruct((96, 128), F32),
    )
    outs = pl.pallas_call(
        step_kernel,
        out_shape=tuple(pltpu.VMEM(r.shape, r.dtype) for r in results),
        in_specs=[anywhere] * 12,
        out_specs=(vmem,) * 3,
        scratch_shapes=[
            *(pltpu.VMEM(t.shape, BF16) for t in tables),
            pltpu.VMEM((1, 128), F32),
            pltpu.VMEM((3, 32), BF16),
            pltpu.VMEM((48, 256), F32),
            pltpu.VMEM((1024, 128), F32),
            pltpu.VMEM((96, 128), F32),
            pltpu.VMEM((945, 128), BF16),
            pltpu.VMEM((952, 128), F32),
            pltpu.VMEM((128, 128), F32),
            pltpu.VMEM((256, 768), BF16),
            pltpu.VMEM((2, 128, 384), BF16),
            pltpu.VMEM((10, 4, SLAB, NX), BF16),
            pltpu.VMEM((10, 4, 8, NX), F32),
            pltpu.VMEM((2, 32, 128), F32),
            pltpu.VMEM((2, 32, NX), BF16),
            pltpu.VMEM((2, 32, NX), BF16),
            pltpu.VMEM((2, 16, NX), BF16),
            pltpu.VMEM((2, 16, NX), BF16),
            pltpu.VMEM((4, 16, NX), BF16),
            pltpu.VMEM((4, 16, NX), BF16),
            pltpu.VMEM((8, 256, 256), F32),
            pltpu.VMEM((8, 2, 32, NX), F32),
            pltpu.VMEM((8, 2, 32, NX), BF16),
            pltpu.VMEM((2, 128, 128), F32),
            pltpu.VMEM((4, RANKS, 8, 128), F32),
            pltpu.VMEM((4, RANKS, 8, 128), F32),
            pltpu.SemaphoreType.DMA((12,)),
            pltpu.SemaphoreType.DMA((8, 5)),
            pltpu.SemaphoreType.DMA((8, 5)),
            pltpu.SemaphoreType.DMA((4,)),
            pltpu.SemaphoreType.DMA((4,)),
        ],
        compiler_params=pltpu.CompilerParams(
            collective_id=0, has_side_effects=True, vmem_limit_bytes=58 * 1024 * 1024
        ),
    )(
        to_rows(velocity),
        to_rows(hidden),
        to_rows(cell),
        gate_weight.T,
        gate_bias.reshape(1, 128),
        decoder,
        *(jnp.asarray(t) for t in tables),
    )
    outs = pl.pallas_call(
        hand_on_kernel,
        out_shape=results,
        in_specs=[vmem] * 3,
        out_specs=(anywhere,) * 3,
        scratch_shapes=[pltpu.SemaphoreType.DMA((3,))],
        compiler_params=pltpu.CompilerParams(vmem_limit_bytes=1024 * 1024),
    )(*outs)
    return tuple(from_rows(out) for out in outs)


def solution(mesh):
    field = P(None, "gy", "gz", None)
    return jax.shard_map(
        per_device,
        mesh=mesh,
        in_specs=(field, field, field, P(), P(), P()),
        out_specs=(field, field, field),
        check_vma=False,
    )
```

```python
import functools

import jax
import jax.numpy as jnp
import numpy as np
from jax import lax
from jax.experimental import pallas as pl
from jax.experimental.pallas import tpu as pltpu
from jax.sharding import PartitionSpec as P

F32 = jnp.float32
BF16 = jnp.bfloat16
MESH = pl.DeviceIdType.MESH
NX, NY, NZ = 256, 128, 32
RANKS = 16
SLAB = 128
HALO = [(sy, sz) for sz in (-1, 1) for sy in (0, -1, 1)] + [(-1, 0), (1, 0)]


def halves(table):
    high = table.astype(np.float32).astype(jnp.bfloat16)
    low = (table - high.astype(np.float64)).astype(np.float32).astype(jnp.bfloat16)
    pair = np.stack([np.asarray(high), np.asarray(low)])
    if table.shape[1] == 256:
        pair = pair.reshape(2, -1, 2, 128).transpose(0, 2, 1, 3)
    return np.ascontiguousarray(pair)


def x_tables():
    mode = np.arange(128)
    n = np.arange(NX)
    angle = 2 * np.pi / NX * ((n[:, None] * mode[None, :]) % NX)
    sign = np.where(n % 2 == 0, 1.0, -1.0)
    imag = np.where(mode[None, :] == 0, sign[:, None], -np.sin(angle))
    forward = np.concatenate([np.cos(angle), imag], 1)
    weight = np.where(mode == 0, 1.0, 2.0) / NX
    inverse = forward.T * np.concatenate([weight, weight])[:, None]
    return forward, inverse


def real_waves(total):
    half = total // 2
    index = np.arange(total)
    return np.where(index < half, index, index - half).astype(np.float64)


def real_tables(total):
    half = total // 2
    cosines, sines = np.arange(half + 1), np.arange(1, half)
    place = np.arange(total)
    angle = 2 * np.pi / total * ((np.concatenate([cosines, sines])[:, None] * place[None, :]) % total)
    is_sine = np.arange(total)[:, None] > half
    analysis = np.where(is_sine, np.sin(angle), np.cos(angle))
    weight = np.full(total, 2.0 / total)
    weight[0] = weight[half] = 1.0 / total
    synthesis = analysis.T * weight[None, :]
    derivative = np.zeros((total, total))
    for k in range(1, half):
        derivative[k, half + k] = k
        derivative[half + k, k] = -k
    return analysis, synthesis, derivative


def y_tables():
    analysis, synthesis, derivative = real_tables(NY)
    forward = np.concatenate([analysis, derivative @ analysis], 0)
    inverse = np.concatenate([synthesis, -(synthesis @ derivative)], 0)
    return forward, inverse


def z_tables():
    analysis, synthesis, derivative = real_tables(NZ)
    lane = np.arange(NZ)
    z = (lane // 8 % 2) * 16 + (lane % 4) * 4 + (lane // 4 % 2) * 2 + lane // 16
    forward, inverse = np.zeros((128, 128)), np.zeros((128, 128))
    for c in range(3):
        lanes = slice(32 * c, 32 * c + 32)
        forward[lanes, :32] = (derivative @ analysis if c == 2 else analysis)[:, z].T
        inverse[:32, lanes] = (-(synthesis @ derivative) if c == 2 else synthesis)[z, :].T
    return forward, inverse


def split(value):
    high = value.astype(BF16)
    return high, (value - high.astype(F32)).astype(BF16)


def dot(a, b):
    return jnp.dot(a, b, preferred_element_type=F32)


def whole(table):
    if len(table.shape) == 3:
        return [table[0], table[1]]
    return [jnp.concatenate([table[part, 0], table[part, 1]], 1) for part in range(2)]


def data_by_table(value, table):
    table = whole(table)
    high, low = split(value)
    return dot(high, table[0]) + (dot(low, table[0]) + dot(high, table[1]))


def table_by_data(table, value):
    high, low = split(value)
    return dot(table[0], high) + (dot(table[0], low) + dot(table[1], high))


def roll_lanes(value, shift):
    return value if shift % 128 == 0 else pltpu.roll(value, shift % 128, 1)


def lane_mix(values, count, stride, base):
    digit = lax.broadcasted_iota(jnp.int32, (8, 128), 1) // stride % base
    masks = [digit == q for q in range(base)]
    rolled = [roll_lanes(v, r * stride) for r, v in enumerate(values)]
    outs = []
    for j in range(count):
        acc = rolled[0] if len(values) == base else jnp.zeros((8, 128), F32)
        for r, v in enumerate(rolled):
            if r or len(values) < base:
                acc = jnp.where(masks[(j + r) % base], v, acc)
        outs.append(roll_lanes(acc, -j * stride))
    return outs


def x_forward(rows, table):
    spectrum = data_by_table(rows, table)
    values = []
    for cz in range(6):
        part = [spectrum[8 * cz : 8 * cz + 8, 128 * p : 128 * p + 128] for p in range(2)]
        values += [-part[1], part[0]] if cz < 2 else part
    return lane_mix(values, RANKS, 8, 16)


def solve(tiles, yf_ref, yi_ref, zf_ref, zi_ref, wave_x):
    def swap(blocks, first_of, second_of):
        out = [None] * 16
        for low in range(4):
            mixed = lane_mix([blocks[first_of(low, i)] for i in range(4)], 4, 4, 4)
            for i in range(4):
                out[second_of(low, i)] = mixed[i]
        return out

    def by_source(low, i):
        return (i // 2) * 8 + low * 2 + i % 2

    def by_y(low, i):
        return i * 4 + low

    lane = lax.broadcasted_iota(jnp.int32, (NY, 128), 1)
    is_y = (lane >= 32) & (lane < 64)
    scale = jnp.where(lane < 32, wave_x, 1.0)
    rows = jnp.concatenate(swap(tiles, by_source, by_y), 0)
    out = table_by_data(yf_ref, rows)
    terms = jnp.where(is_y, out[NY:], out[:NY]) * scale
    divergence = data_by_table(terms, zf_ref)
    row = lax.broadcasted_iota(jnp.int32, (NY, 128), 0)
    wave_y = jnp.where(row < NY // 2, row, row - NY // 2).astype(F32)
    wave_z = jnp.where(lane < NZ // 2, lane, lane - NZ // 2).astype(F32)
    square = wave_x * wave_x + wave_y * wave_y + wave_z * wave_z
    potential = divergence / jnp.maximum(square, 1.0)
    out = table_by_data(yi_ref, data_by_table(potential, zi_ref))
    rows = jnp.where(is_y, out[NY:], out[:NY]) * scale
    return swap([rows[8 * i : 8 * i + 8] for i in range(16)], by_y, by_source)


def x_inverse(tiles, table):
    values = lane_mix(tiles, 12, 8, 16)
    rows = []
    for cz in range(6):
        pair = values[2 * cz : 2 * cz + 2]
        rows.append(jnp.concatenate([pair[1], -pair[0]] if cz < 2 else pair, 1))
    return data_by_table(jnp.concatenate(rows, 0), table)


def around(index, step):
    return lax.rem(index + step + RANKS, RANKS)


def ring(step, length):
    return min(step, length - step)


def positions():
    gy, gz = lax.axis_index("gy"), lax.axis_index("gz")
    y, z_low, z_high, x, core = gy // 4, gy % 4, gz // 8, gz // 2 % 4, gz % 2

    def first(index):
        return (index // 4 * 4 + z_low, z_high * 8 + index % 4 * 2 + core)

    def second(index):
        return (y * 4 + index // 2 % 4, index // 8 * 8 + x * 2 + index % 2)

    z = z_high * 4 + z_low
    first_others = [
        lax.rem(y + dy, 4) * 4 + lax.rem(x + dx, 4)
        for dy, dx in sorted(np.ndindex(4, 4), key=lambda d: -ring(d[0], 4) - ring(d[1], 4))[:-1]
    ]
    second_others = [
        lax.rem(z + dz, 8) * 2 + lax.rem(core + dc, 2)
        for dz, dc in sorted(np.ndindex(8, 2), key=lambda d: -ring(d[0], 8) - d[1])[:-1]
    ]
    return (y * 4 + x, first, first_others), (z * 2 + core, second, second_others)


def project(u_ref, tables, out_ref, send, recv, send_sem, recv_sem, meanwhile):
    xf_ref, xi_ref, yf_ref, yi_ref, zf_ref, zi_ref = tables
    group_1, group_2 = positions()

    def exchange(step, group, tiles, meanwhile=None):
        me, place, others = group
        for j in range(RANKS):
            send[step, j] = tiles[j]

        for to in others:
            pltpu.make_async_remote_copy(
                src_ref=send.at[step, to],
                dst_ref=recv.at[step, me],
                send_sem=send_sem.at[step],
                recv_sem=recv_sem.at[step],
                device_id=place(to),
                device_id_type=MESH,
            ).start()
        recv[step, pl.ds(me, 1)] = send[step, pl.ds(me, 1)]
        if meanwhile is not None:
            meanwhile()
        some = recv.at[step, pl.ds(0, RANKS - 1)]
        pltpu.make_async_copy(some, some, recv_sem.at[step]).wait()
        return [recv[step, j] for j in range(RANKS)]

    tiles = exchange(0, group_1, x_forward(u_ref[...], xf_ref), meanwhile)
    tiles = exchange(1, group_2, lane_mix(tiles, RANKS, 1, 16))
    wave_x = (group_1[0] * 8 + group_2[0] % 8).astype(F32)
    tiles = exchange(2, group_2, solve(tiles, yf_ref, yi_ref, zf_ref, zi_ref, wave_x))
    tiles = exchange(3, group_1, lane_mix(tiles, RANKS, 1, 16))
    gradient = x_inverse(tiles, xi_ref)
    result = u_ref[...] - gradient
    for c in range(3):
        for z in range(2):
            start = (2 * c + z) * 8
            for t in range(2):
                out_ref[pl.ds(c * 32 + 2 * t + z, 8, stride=4), :] = result[
                    start : start + 8, 128 * t : 128 * t + 128
                ]
    for step in range(4):
        some = send.at[step, pl.ds(0, RANKS - 1)]
        pltpu.make_async_copy(some, some, send_sem.at[step]).wait()


def step_kernel(
    vel_hbm, hid_hbm, cell_hbm, weight_hbm, bias_hbm, dec_hbm, *refs,
):
    tables_hbm, (hid_in, cell_v, vel_next) = refs[:6], refs[6:9]
    tables, refs = refs[9:15], refs[15:]
    (
        bias_ref, dec_ref, u_ref, hid_f, vel_f, weight_v, weight_f, block_f, wide, side, slabs, vels, vel_t,
        vz_s, vz_r, vy_s, vy_r, vc_s, vc_r, acc, cells, hids, moved, send, recv,
        load_sem, send_sem, recv_sem, tile_send_sem, tile_recv_sem,
    ) = refs
    gy, gz = lax.axis_index("gy"), lax.axis_index("gz")
    loads = [
        pltpu.make_async_copy(src, dst, load_sem.at[i])
        for i, (src, dst) in enumerate(
            [
                (hid_hbm, hid_in),
                (vel_hbm, vel_f.at[pl.ds(0, 96)]),
                (weight_hbm, weight_v),
                (cell_hbm, cell_v),
                (bias_hbm, bias_ref),
                (dec_hbm, dec_ref),
                *zip(tables_hbm, tables),
            ]
        )
    ]
    for load in loads[:2]:
        load.start()
    barrier = pltpu.get_barrier_semaphore()
    targets = [(around(gy, sy), around(gz, sz)) for sy, sz in HALO]
    for target in targets:
        pl.semaphore_signal(barrier, inc=1, device_id=target, device_id_type=MESH)

    for _, place, others in positions():
        for to in others:
            pl.semaphore_signal(barrier, inc=1, device_id=place(to), device_id_type=MESH)
    vels[...] = jnp.zeros_like(vels)

    loads[0].wait()
    hid_f[...] = hid_in[...].astype(F32)
    loads[1].wait()

    def centre(y, carry):
        for z in range(2):
            for t in range(2):
                lanes = slice(128 * t, 128 * t + 128)
                rows = hid_f[pl.ds(y * 4 + 2 * t + z, 32, stride=32), :]
                slabs[y + 1, z + 1, 32:64, lanes] = rows.astype(BF16)
                vels[y + 1, z + 1, 0:3, lanes] = vel_f[pl.ds(y * 4 + 2 * t + z, 3, stride=32), :]
        return carry

    lax.fori_loop(0, 8, centre, 0)
    for z in range(2):
        rows = [vel_f[pl.ds(2 * t + z, 24, stride=4), :] for t in range(2)]
        vz_s[z] = jnp.concatenate(rows, 0).astype(BF16)
    for k in range(2):
        y = 1 + 7 * k
        vy_s[k] = jnp.concatenate([vels[y, 1], vels[y, 2]], 0).astype(BF16)
        for z in range(2):
            v = vels[y, z + 1]
            vc_s[2 * k + z] = jnp.concatenate([v[:, :128], v[:, 128:]], 0).astype(BF16)

    pl.semaphore_wait(barrier, len(HALO) + 2 * (RANKS - 1))
    copies = {}

    def start_halo(name, i, n, src, dst):
        copies[name] = pltpu.make_async_remote_copy(
            src_ref=src,
            dst_ref=dst,
            send_sem=send_sem.at[i, n],
            recv_sem=recv_sem.at[i, n],
            device_id=targets[i],
            device_id_type=MESH,
        )
        copies[name].start()

    mids = pl.ds(32, 32)

    def send_plane(part):
        for i, (sy, sz) in enumerate(HALO):
            if sy == 0:
                z = (1 + sz) // 2
                ys = pl.ds(*((1, 2), (3, 2), (5, 3), (8, 1))[part])
                src, dst = slabs.at[ys, z + 1, mids], slabs.at[ys, 3 - 3 * z, mids]
                start_halo(("plane", z, part), i, part, src, dst)

    def send_edge(i):
        sy, sz = HALO[i]
        k, z = (1 + sy) // 2, (1 + sz) // 2
        if sz == 0:
            src, dst = slabs.at[1 + 7 * k, pl.ds(1, 2), mids], slabs.at[9 - 9 * k, pl.ds(1, 2), mids]
            start_halo(("edge", k, 0), i, 0, src, dst)
            start_halo(("edge", k, 1), i, 1, vy_s.at[k], vy_r.at[k])
        else:
            src, dst = slabs.at[1 + 7 * k, 1 + z, mids], slabs.at[9 - 9 * k, 3 - 3 * z, mids]
            start_halo(("corner", k, z, 0), i, 0, src, dst)
            start_halo(("corner", k, z, 1), i, 1, vc_s.at[2 * k + z], vc_r.at[2 * k + z])

    send_plane(0)
    for i, (sy, sz) in enumerate(HALO):
        if sy == 0:
            z = (1 + sz) // 2
            start_halo(("side", z), i, 4, vz_s.at[z], vz_r.at[z])
    for wanted in ((1, True),):
        for i, (sy, sz) in enumerate(HALO):
            if (sy, sz != 0) == wanted:
                send_edge(i)
    send_plane(1)
    send_edge(6)
    send_edge(7)
    send_plane(2)
    for i, (sy, sz) in enumerate(HALO):
        if sy == -1 and sz != 0:
            send_edge(i)
    send_plane(3)

    for load in loads[2:]:
        load.start()

    def fill(y, z):
        mid = slabs[y, z, 32:64, :]
        slabs[y, z, 0:32, :] = pltpu.roll(mid, 1, 1)
        slabs[y, z, 64:96, :] = pltpu.roll(mid, NX - 1, 1)
        v = vels[y, z]
        first = v + pltpu.roll(pltpu.roll(v, 1, 1), 3, 0)
        tile = jnp.concatenate([first, pltpu.roll(v, NX - 1, 1), jnp.ones((16, NX), F32)], 0)
        slabs[y, z, 96:128, :] = tile.astype(BF16)

    def fill_own(y, carry):
        fill(y, 1)
        fill(y, 2)
        return carry

    lax.fori_loop(1, 9, fill_own, 0)

    loads[2].wait()
    loads[4].wait()
    weight_f[0:945, :] = weight_v[...].astype(F32)
    block_f[96:128, :] = jnp.zeros((32, 128), F32)
    gate = lax.broadcasted_iota(jnp.int32, (128, 128), 0)
    gate_scale = jnp.where((gate >= 64) & (gate < 96), 1.0, 0.5)
    for dy in range(3):
        for dz in range(3):
            first = (9 * dy + 3 * dz) * 35
            for dx in range(3):
                at = first + 35 * dx
                block_f[32 * dx : 32 * dx + 32, :] = weight_f[at + 3 : at + 35, :]
                row = 96 + (3, 0, 8)[dx]
                block_f[row : row + 3, :] = weight_f[at : at + 3, :]
            if dy == 1 and dz == 1:
                rest = bias_ref[...]
                for part in range(3):
                    high = rest.astype(BF16).astype(F32)
                    block_f[112 + part : 113 + part, :] = high
                    rest = rest - high
            turned = (block_f[...].T * gate_scale).astype(BF16)
            if dy == 1 and dz == 1:
                block_f[112:120, :] = jnp.zeros((8, 128), F32)
            if dz == 0:
                side[0, :, 128 * dy : 128 * dy + 128] = turned
            if dz == 2:
                side[1, :, 128 * dy : 128 * dy + 128] = turned
            for z in range(2):
                own = z + dz - 1
                if 0 <= own < 2:
                    at = (2 * dy + own) * 128
                    wide[128 * z : 128 * z + 128, at : at + 128] = turned

    def inner(y):
        acc[y] = dot(wide[...], slabs[pl.ds(y, 3), 1:3].reshape(6 * SLAB, NX))

    def inner_step(y, carry):
        inner(y)
        return carry

    lax.fori_loop(1, 7, inner_step, 0)

    loads[3].wait()
    loads[5].wait()

    def own_cells(y, carry):
        for z in range(2):
            for t in range(2):
                cells[y, z, :, 128 * t : 128 * t + 128] = cell_v[
                    pl.ds(y * 4 + 2 * t + z, 32, stride=32), :
                ]
        return carry

    lax.fori_loop(0, 8, own_cells, 0)

    for k in range(2):
        copies["edge", k, 0].wait_recv()
        copies["edge", k, 1].wait_recv()
        rows = vy_r[k].astype(F32)
        y = 9 - 9 * k
        vels[y, 1] = rows[0:8]
        vels[y, 2] = rows[8:16]
        fill(y, 1)
        fill(y, 2)
    inner(0)
    inner(7)

    def update(y, carry):
        for z in range(2):
            outer = slabs[pl.ds(y, 3), 3 * z].reshape(3 * SLAB, NX)
            gates = acc[y, 128 * z : 128 * z + 128, :] + dot(side[z], outer)
            turned = jnp.tanh(gates)
            new = 0.5 * (
                (turned[32:64] + 1.0) * cells[y, z] + (turned[0:32] + 1.0) * turned[64:96]
            )
            cells[y, z] = new
            hids[y, z] = (0.5 * (turned[96:128] + 1.0) * jnp.tanh(new)).astype(BF16)
        return carry

    def fill_outer(y, carry):
        fill(y, 0)
        fill(y, 3)
        return carry

    for z in range(2):
        copies["side", z].wait_recv()
        to = 3 - 3 * z
        rows = vz_r[z].astype(F32)
        for t in range(2):
            vel_t[t, 0:24] = rows[24 * t : 24 * t + 24]
            for y in range(8):
                vels[y + 1, to, 0:3, 128 * t : 128 * t + 128] = vel_t[t, pl.ds(y, 3, stride=8), :]
    for part, ys, rows in (
        (0, (0, 3), (0, 1)), (1, (3, 5), (1, 3)), (2, (5, 8), (3, 6)), (3, (8, 10), (6, 8))
    ):
        for z in range(2):
            copies["plane", z, part].wait_recv()
            if part in (0, 3):
                k = 1 - part // 3
                copies["corner", k, z, 0].wait_recv()
                copies["corner", k, z, 1].wait_recv()
                rows_c = vc_r[2 * k + z].astype(F32)
                vels[9 - 9 * k, 3 - 3 * z] = jnp.concatenate([rows_c[0:8], rows_c[8:16]], 1)
        for y in range(*ys):
            fill_outer(y, 0)
        for y in range(*rows):
            update(y, 0)

    for y in range(8):
        for z in range(2):
            advanced = vels[y + 1, z + 1, 0:3, :] + dot(dec_ref[...], hids[y, z])
            for t in range(2):
                at = 16 * y + 8 * z
                moved[t, at : at + 3, :] = advanced[:, 128 * t : 128 * t + 128]
    for c in range(3):
        for z in range(2):
            for t in range(2):
                start = 16 * c + 8 * z
                u_ref[start : start + 8, 128 * t : 128 * t + 128] = moved[
                    t, pl.ds(8 * z + c, 8, stride=16), :
                ]

    def store_states():
        def turn(y, carry):
            for z in range(2):
                for t in range(2):
                    rows = pl.ds(y * 4 + 2 * t + z, 32, stride=32)
                    lanes = slice(128 * t, 128 * t + 128)
                    cell_v[rows, :] = cells[y, z, :, lanes]
                    hid_f[rows, :] = hids[y, z, :, lanes].astype(F32)
            return carry

        lax.fori_loop(0, 8, turn, 0)
        hid_in[...] = hid_f[...].astype(BF16)

    for load in loads[6:]:
        load.wait()
    project(u_ref, tables, vel_next, send, recv, tile_send_sem, tile_recv_sem, store_states)
    for copy in copies.values():
        copy.wait_send()


def hand_on_kernel(*refs):
    sources, results, sem = refs[:3], refs[3:6], refs[6]
    copies = [pltpu.make_async_copy(a, b, sem.at[i]) for i, (a, b) in enumerate(zip(sources, results))]
    for copy in copies:
        copy.start()
    for copy in copies:
        copy.wait()


def to_rows(array):
    c = array.shape[0]
    return array.reshape(c, 8, 2, 2, 128).transpose(0, 1, 3, 2, 4).reshape(c * 32, 128)


def from_rows(array):
    c = array.shape[0] // 32
    return array.reshape(c, 8, 2, 2, 128).transpose(0, 1, 3, 2, 4).reshape(c, 8, 2, 256)


def per_device(velocity, hidden, cell, gate_weight, gate_bias, decoder):
    anywhere = pl.BlockSpec(memory_space=pl.ANY)
    vmem = pl.BlockSpec(memory_space=pltpu.VMEM)
    tables = [halves(t) for t in (*x_tables(), *y_tables(), *z_tables())]
    results = (
        jax.ShapeDtypeStruct((1024, 128), BF16),
        jax.ShapeDtypeStruct((1024, 128), F32),
        jax.ShapeDtypeStruct((96, 128), F32),
    )
    outs = pl.pallas_call(
        step_kernel,
        out_shape=tuple(pltpu.VMEM(r.shape, r.dtype) for r in results),
        in_specs=[anywhere] * 12,
        out_specs=(vmem,) * 3,
        scratch_shapes=[
            *(pltpu.VMEM(t.shape, BF16) for t in tables),
            pltpu.VMEM((1, 128), F32),
            pltpu.VMEM((3, 32), BF16),
            pltpu.VMEM((48, 256), F32),
            pltpu.VMEM((1024, 128), F32),
            pltpu.VMEM((256, 128), F32),
            pltpu.VMEM((945, 128), BF16),
            pltpu.VMEM((952, 128), F32),
            pltpu.VMEM((128, 128), F32),
            pltpu.VMEM((256, 768), BF16),
            pltpu.VMEM((2, 128, 384), BF16),
            pltpu.VMEM((10, 4, SLAB, NX), BF16),
            pltpu.VMEM((10, 4, 8, NX), F32),
            pltpu.VMEM((2, 64, 128), F32),
            pltpu.VMEM((2, 48, 128), BF16),
            pltpu.VMEM((2, 48, 128), BF16),
            pltpu.VMEM((2, 16, NX), BF16),
            pltpu.VMEM((2, 16, NX), BF16),
            pltpu.VMEM((4, 16, 128), BF16),
            pltpu.VMEM((4, 16, 128), BF16),
            pltpu.VMEM((8, 256, 256), F32),
            pltpu.VMEM((8, 2, 32, NX), F32),
            pltpu.VMEM((8, 2, 32, NX), BF16),
            pltpu.VMEM((2, 128, 128), F32),
            pltpu.VMEM((4, RANKS, 8, 128), F32),
            pltpu.VMEM((4, RANKS, 8, 128), F32),
            pltpu.SemaphoreType.DMA((12,)),
            pltpu.SemaphoreType.DMA((8, 5)),
            pltpu.SemaphoreType.DMA((8, 5)),
            pltpu.SemaphoreType.DMA((4,)),
            pltpu.SemaphoreType.DMA((4,)),
        ],
        compiler_params=pltpu.CompilerParams(
            collective_id=0, has_side_effects=True, vmem_limit_bytes=58 * 1024 * 1024
        ),
    )(
        to_rows(velocity),
        to_rows(hidden),
        to_rows(cell),
        gate_weight.T,
        gate_bias.reshape(1, 128),
        decoder,
        *(jnp.asarray(t) for t in tables),
    )
    outs = pl.pallas_call(
        hand_on_kernel,
        out_shape=results,
        in_specs=[vmem] * 3,
        out_specs=(anywhere,) * 3,
        scratch_shapes=[pltpu.SemaphoreType.DMA((3,))],
        compiler_params=pltpu.CompilerParams(vmem_limit_bytes=1024 * 1024),
    )(*outs)
    return tuple(from_rows(out) for out in outs)


def solution(mesh):
    field = P(None, "gy", "gz", None)
    return jax.shard_map(
        per_device,
        mesh=mesh,
        in_specs=(field, field, field, P(), P(), P()),
        out_specs=(field, field, field),
        check_vma=False,
    )
```

```python
import functools

import jax
import jax.numpy as jnp
import numpy as np
from jax import lax
from jax.experimental import pallas as pl
from jax.experimental.pallas import tpu as pltpu
from jax.sharding import PartitionSpec as P

F32 = jnp.float32
BF16 = jnp.bfloat16
MESH = pl.DeviceIdType.MESH
NX, NY, NZ = 256, 128, 32
RANKS = 16
SLAB = 128
HALO = [(sy, sz) for sz in (-1, 1) for sy in (0, -1, 1)] + [(-1, 0), (1, 0)]


def halves(table):
    high = table.astype(np.float32).astype(jnp.bfloat16)
    low = (table - high.astype(np.float64)).astype(np.float32).astype(jnp.bfloat16)
    pair = np.stack([np.asarray(high), np.asarray(low)])
    if table.shape[1] == 256:
        pair = pair.reshape(2, -1, 2, 128).transpose(0, 2, 1, 3)
    return np.ascontiguousarray(pair)


def x_tables():
    mode = np.arange(128)
    n = np.arange(NX)
    angle = 2 * np.pi / NX * ((n[:, None] * mode[None, :]) % NX)
    sign = np.where(n % 2 == 0, 1.0, -1.0)
    imag = np.where(mode[None, :] == 0, sign[:, None], -np.sin(angle))
    forward = np.concatenate([np.cos(angle), imag], 1)
    weight = np.where(mode == 0, 1.0, 2.0) / NX
    inverse = forward.T * np.concatenate([weight, weight])[:, None]
    return forward, inverse


def real_waves(total):
    half = total // 2
    index = np.arange(total)
    return np.where(index < half, index, index - half).astype(np.float64)


def real_tables(total):
    half = total // 2
    cosines, sines = np.arange(half + 1), np.arange(1, half)
    place = np.arange(total)
    angle = 2 * np.pi / total * ((np.concatenate([cosines, sines])[:, None] * place[None, :]) % total)
    is_sine = np.arange(total)[:, None] > half
    analysis = np.where(is_sine, np.sin(angle), np.cos(angle))
    weight = np.full(total, 2.0 / total)
    weight[0] = weight[half] = 1.0 / total
    synthesis = analysis.T * weight[None, :]
    derivative = np.zeros((total, total))
    for k in range(1, half):
        derivative[k, half + k] = k
        derivative[half + k, k] = -k
    return analysis, synthesis, derivative


def y_tables():
    analysis, synthesis, derivative = real_tables(NY)
    forward = np.concatenate([analysis, derivative @ analysis], 0)
    inverse = np.concatenate([synthesis, -(synthesis @ derivative)], 0)
    return forward, inverse


def z_tables():
    analysis, synthesis, derivative = real_tables(NZ)
    lane = np.arange(NZ)
    z = (lane // 8 % 2) * 16 + (lane % 4) * 4 + (lane // 4 % 2) * 2 + lane // 16
    forward, inverse = np.zeros((128, 128)), np.zeros((128, 128))
    for c in range(3):
        lanes = slice(32 * c, 32 * c + 32)
        forward[lanes, :32] = (derivative @ analysis if c == 2 else analysis)[:, z].T
        inverse[:32, lanes] = (-(synthesis @ derivative) if c == 2 else synthesis)[z, :].T
    return forward, inverse


def split(value):
    high = value.astype(BF16)
    return high, (value - high.astype(F32)).astype(BF16)


def dot(a, b):
    return jnp.dot(a, b, preferred_element_type=F32)


def whole(table):
    if len(table.shape) == 3:
        return [table[0], table[1]]
    return [jnp.concatenate([table[part, 0], table[part, 1]], 1) for part in range(2)]


def data_by_table(value, table):
    table = whole(table)
    high, low = split(value)
    return dot(high, table[0]) + (dot(low, table[0]) + dot(high, table[1]))


def table_by_data(table, value):
    high, low = split(value)
    return dot(table[0], high) + (dot(table[0], low) + dot(table[1], high))


def roll_lanes(value, shift):
    return value if shift % 128 == 0 else pltpu.roll(value, shift % 128, 1)


def lane_mix(values, count, stride, base):
    digit = lax.broadcasted_iota(jnp.int32, (8, 128), 1) // stride % base
    masks = [digit == q for q in range(base)]
    rolled = [roll_lanes(v, r * stride) for r, v in enumerate(values)]
    outs = []
    for j in range(count):
        acc = rolled[0] if len(values) == base else jnp.zeros((8, 128), F32)
        for r, v in enumerate(rolled):
            if r or len(values) < base:
                acc = jnp.where(masks[(j + r) % base], v, acc)
        outs.append(roll_lanes(acc, -j * stride))
    return outs


def x_forward(rows, table):
    spectrum = data_by_table(rows, table)
    values = []
    for cz in range(6):
        part = [spectrum[8 * cz : 8 * cz + 8, 128 * p : 128 * p + 128] for p in range(2)]
        values += [-part[1], part[0]] if cz < 2 else part
    return lane_mix(values, RANKS, 8, 16)


def solve(tiles, yf_ref, yi_ref, zf_ref, zi_ref, wave_x):
    def swap(blocks, first_of, second_of):
        out = [None] * 16
        for low in range(4):
            mixed = lane_mix([blocks[first_of(low, i)] for i in range(4)], 4, 4, 4)
            for i in range(4):
                out[second_of(low, i)] = mixed[i]
        return out

    def by_source(low, i):
        return (i // 2) * 8 + low * 2 + i % 2

    def by_y(low, i):
        return i * 4 + low

    lane = lax.broadcasted_iota(jnp.int32, (NY, 128), 1)
    is_y = (lane >= 32) & (lane < 64)
    scale = jnp.where(lane < 32, wave_x, 1.0)
    rows = jnp.concatenate(swap(tiles, by_source, by_y), 0)
    out = table_by_data(yf_ref, rows)
    terms = jnp.where(is_y, out[NY:], out[:NY]) * scale
    divergence = data_by_table(terms, zf_ref)
    row = lax.broadcasted_iota(jnp.int32, (NY, 128), 0)
    wave_y = jnp.where(row < NY // 2, row, row - NY // 2).astype(F32)
    wave_z = jnp.where(lane < NZ // 2, lane, lane - NZ // 2).astype(F32)
    square = wave_x * wave_x + wave_y * wave_y + wave_z * wave_z
    potential = divergence / jnp.maximum(square, 1.0)
    out = table_by_data(yi_ref, data_by_table(potential, zi_ref))
    rows = jnp.where(is_y, out[NY:], out[:NY]) * scale
    return swap([rows[8 * i : 8 * i + 8] for i in range(16)], by_y, by_source)


def x_inverse(tiles, table):
    values = lane_mix(tiles, 12, 8, 16)
    rows = []
    for cz in range(6):
        pair = values[2 * cz : 2 * cz + 2]
        rows.append(jnp.concatenate([pair[1], -pair[0]] if cz < 2 else pair, 1))
    return data_by_table(jnp.concatenate(rows, 0), table)


def around(index, step):
    return lax.rem(index + step + RANKS, RANKS)


def ring(step, length):
    return min(step, length - step)


def positions():
    gy, gz = lax.axis_index("gy"), lax.axis_index("gz")
    y, z_low, z_high, x, core = gy // 4, gy % 4, gz // 8, gz // 2 % 4, gz % 2

    def first(index):
        return (index // 4 * 4 + z_low, z_high * 8 + index % 4 * 2 + core)

    def second(index):
        return (y * 4 + index // 2 % 4, index // 8 * 8 + x * 2 + index % 2)

    z = z_high * 4 + z_low
    first_others = [
        lax.rem(y + dy, 4) * 4 + lax.rem(x + dx, 4)
        for dy, dx in sorted(np.ndindex(4, 4), key=lambda d: -ring(d[0], 4) - ring(d[1], 4))[:-1]
    ]
    second_others = [
        lax.rem(z + dz, 8) * 2 + lax.rem(core + dc, 2)
        for dz, dc in sorted(np.ndindex(8, 2), key=lambda d: -ring(d[0], 8) - d[1])[:-1]
    ]
    return (y * 4 + x, first, first_others), (z * 2 + core, second, second_others)


def project(u_ref, tables, out_ref, send, recv, send_sem, recv_sem, meanwhile):
    xf_ref, xi_ref, yf_ref, yi_ref, zf_ref, zi_ref = tables
    group_1, group_2 = positions()

    def sent(step):
        some = send.at[step, pl.ds(0, RANKS - 1)]
        pltpu.make_async_copy(some, some, send_sem.at[step]).wait()

    def exchange(step, group, tiles, meanwhile=None):
        me, place, others = group
        for j in range(RANKS):
            send[step, j] = tiles[j]

        for to in others:
            pltpu.make_async_remote_copy(
                src_ref=send.at[step, to],
                dst_ref=recv.at[step, me],
                send_sem=send_sem.at[step],
                recv_sem=recv_sem.at[step],
                device_id=place(to),
                device_id_type=MESH,
            ).start()
        recv[step, pl.ds(me, 1)] = send[step, pl.ds(me, 1)]
        if meanwhile is not None:
            meanwhile()
        if step:
            sent(step - 1)
        some = recv.at[step, pl.ds(0, RANKS - 1)]
        pltpu.make_async_copy(some, some, recv_sem.at[step]).wait()
        return [recv[step, j] for j in range(RANKS)]

    tiles = exchange(0, group_1, x_forward(u_ref[...], xf_ref), meanwhile)
    tiles = exchange(1, group_2, lane_mix(tiles, RANKS, 1, 16))
    wave_x = (group_1[0] * 8 + group_2[0] % 8).astype(F32)
    tiles = exchange(2, group_2, solve(tiles, yf_ref, yi_ref, zf_ref, zi_ref, wave_x))
    tiles = exchange(3, group_1, lane_mix(tiles, RANKS, 1, 16))
    gradient = x_inverse(tiles, xi_ref)
    result = u_ref[...] - gradient
    for c in range(3):
        for z in range(2):
            start = (2 * c + z) * 8
            for t in range(2):
                out_ref[pl.ds(c * 32 + 2 * t + z, 8, stride=4), :] = result[
                    start : start + 8, 128 * t : 128 * t + 128
                ]
    sent(3)


def step_kernel(
    vel_hbm, hid_hbm, cell_hbm, weight_hbm, bias_hbm, dec_hbm, *refs,
):
    tables_hbm, (hid_in, cell_v, vel_next) = refs[:6], refs[6:9]
    tables, refs = refs[9:15], refs[15:]
    (
        bias_ref, dec_ref, u_ref, hid_f, vel_f, weight_v, weight_f, block_f, wide, side, slabs, vels, vel_t,
        vz_s, vz_r, vy_s, vy_r, vc_s, vc_r, acc, cells, hids, moved, send, recv,
        load_sem, send_sem, recv_sem, tile_send_sem, tile_recv_sem,
    ) = refs
    gy, gz = lax.axis_index("gy"), lax.axis_index("gz")
    loads = [
        pltpu.make_async_copy(src, dst, load_sem.at[i])
        for i, (src, dst) in enumerate(
            [
                (hid_hbm, hid_in),
                (vel_hbm, vel_f.at[pl.ds(0, 96)]),
                (weight_hbm, weight_v),
                (cell_hbm, cell_v),
                (bias_hbm, bias_ref),
                (dec_hbm, dec_ref),
                *zip(tables_hbm, tables),
            ]
        )
    ]
    for load in loads[:2]:
        load.start()
    barrier = pltpu.get_barrier_semaphore()
    targets = [(around(gy, sy), around(gz, sz)) for sy, sz in HALO]
    for target in targets:
        pl.semaphore_signal(barrier, inc=1, device_id=target, device_id_type=MESH)

    for _, place, others in positions():
        for to in others:
            pl.semaphore_signal(barrier, inc=1, device_id=place(to), device_id_type=MESH)
    vels[...] = jnp.zeros_like(vels)

    loads[0].wait()
    hid_f[...] = hid_in[...].astype(F32)
    loads[1].wait()

    def centre(y, carry):
        for z in range(2):
            for t in range(2):
                lanes = slice(128 * t, 128 * t + 128)
                rows = hid_f[pl.ds(y * 4 + 2 * t + z, 32, stride=32), :]
                slabs[y + 1, z + 1, 32:64, lanes] = rows.astype(BF16)
                vels[y + 1, z + 1, 0:3, lanes] = vel_f[pl.ds(y * 4 + 2 * t + z, 3, stride=32), :]
        return carry

    lax.fori_loop(0, 8, centre, 0)
    for z in range(2):
        rows = [vel_f[pl.ds(2 * t + z, 24, stride=4), :] for t in range(2)]
        vz_s[z] = jnp.concatenate(rows, 0).astype(BF16)
    for k in range(2):
        y = 1 + 7 * k
        vy_s[k] = jnp.concatenate([vels[y, 1], vels[y, 2]], 0).astype(BF16)
        for z in range(2):
            v = vels[y, z + 1]
            vc_s[2 * k + z] = jnp.concatenate([v[:, :128], v[:, 128:]], 0).astype(BF16)

    pl.semaphore_wait(barrier, len(HALO) + 2 * (RANKS - 1))
    copies = {}

    def start_halo(name, i, n, src, dst):
        copies[name] = pltpu.make_async_remote_copy(
            src_ref=src,
            dst_ref=dst,
            send_sem=send_sem.at[i, n],
            recv_sem=recv_sem.at[i, n],
            device_id=targets[i],
            device_id_type=MESH,
        )
        copies[name].start()

    mids = pl.ds(32, 32)

    def send_plane(part):
        for i, (sy, sz) in enumerate(HALO):
            if sy == 0:
                z = (1 + sz) // 2
                ys = pl.ds(*((1, 2), (3, 2), (5, 3), (8, 1))[part])
                src, dst = slabs.at[ys, z + 1, mids], slabs.at[ys, 3 - 3 * z, mids]
                start_halo(("plane", z, part), i, part, src, dst)

    def send_edge(i):
        sy, sz = HALO[i]
        k, z = (1 + sy) // 2, (1 + sz) // 2
        if sz == 0:
            src, dst = slabs.at[1 + 7 * k, pl.ds(1, 2), mids], slabs.at[9 - 9 * k, pl.ds(1, 2), mids]
            start_halo(("edge", k, 0), i, 0, src, dst)
            start_halo(("edge", k, 1), i, 1, vy_s.at[k], vy_r.at[k])
        else:
            src, dst = slabs.at[1 + 7 * k, 1 + z, mids], slabs.at[9 - 9 * k, 3 - 3 * z, mids]
            start_halo(("corner", k, z, 0), i, 0, src, dst)
            start_halo(("corner", k, z, 1), i, 1, vc_s.at[2 * k + z], vc_r.at[2 * k + z])

    send_plane(0)
    for i, (sy, sz) in enumerate(HALO):
        if sy == 0:
            z = (1 + sz) // 2
            start_halo(("side", z), i, 4, vz_s.at[z], vz_r.at[z])
    for wanted in ((1, True),):
        for i, (sy, sz) in enumerate(HALO):
            if (sy, sz != 0) == wanted:
                send_edge(i)
    send_plane(1)
    send_edge(6)
    send_edge(7)
    send_plane(2)
    for i, (sy, sz) in enumerate(HALO):
        if sy == -1 and sz != 0:
            send_edge(i)
    send_plane(3)

    for load in loads[2:]:
        load.start()

    def fill(y, z):
        mid = slabs[y, z, 32:64, :]
        slabs[y, z, 0:32, :] = pltpu.roll(mid, 1, 1)
        slabs[y, z, 64:96, :] = pltpu.roll(mid, NX - 1, 1)
        v = vels[y, z]
        first = v + pltpu.roll(pltpu.roll(v, 1, 1), 3, 0)
        tile = jnp.concatenate([first, pltpu.roll(v, NX - 1, 1), jnp.ones((16, NX), F32)], 0)
        slabs[y, z, 96:128, :] = tile.astype(BF16)

    def fill_own(y, carry):
        fill(y, 1)
        fill(y, 2)
        return carry

    lax.fori_loop(1, 9, fill_own, 0)

    loads[2].wait()
    loads[4].wait()
    weight_f[0:945, :] = weight_v[...].astype(F32)
    block_f[96:128, :] = jnp.zeros((32, 128), F32)
    gate = lax.broadcasted_iota(jnp.int32, (128, 128), 0)
    gate_scale = jnp.where((gate >= 64) & (gate < 96), 1.0, 0.5)
    for dy in range(3):
        for dz in range(3):
            first = (9 * dy + 3 * dz) * 35
            for dx in range(3):
                at = first + 35 * dx
                block_f[32 * dx : 32 * dx + 32, :] = weight_f[at + 3 : at + 35, :]
                row = 96 + (3, 0, 8)[dx]
                block_f[row : row + 3, :] = weight_f[at : at + 3, :]
            if dy == 1 and dz == 1:
                rest = bias_ref[...]
                for part in range(3):
                    high = rest.astype(BF16).astype(F32)
                    block_f[112 + part : 113 + part, :] = high
                    rest = rest - high
            turned = (block_f[...].T * gate_scale).astype(BF16)
            if dy == 1 and dz == 1:
                block_f[112:120, :] = jnp.zeros((8, 128), F32)
            if dz == 0:
                side[0, :, 128 * dy : 128 * dy + 128] = turned
            if dz == 2:
                side[1, :, 128 * dy : 128 * dy + 128] = turned
            for z in range(2):
                own = z + dz - 1
                if 0 <= own < 2:
                    at = (2 * dy + own) * 128
                    wide[128 * z : 128 * z + 128, at : at + 128] = turned

    def inner(y):
        acc[y] = dot(wide[...], slabs[pl.ds(y, 3), 1:3].reshape(6 * SLAB, NX))

    def inner_step(y, carry):
        inner(y)
        return carry

    lax.fori_loop(1, 7, inner_step, 0)

    loads[3].wait()
    loads[5].wait()

    def own_cells(y, carry):
        for z in range(2):
            for t in range(2):
                cells[y, z, :, 128 * t : 128 * t + 128] = cell_v[
                    pl.ds(y * 4 + 2 * t + z, 32, stride=32), :
                ]
        return carry

    lax.fori_loop(0, 8, own_cells, 0)

    for k in range(2):
        copies["edge", k, 0].wait_recv()
        copies["edge", k, 1].wait_recv()
        rows = vy_r[k].astype(F32)
        y = 9 - 9 * k
        vels[y, 1] = rows[0:8]
        vels[y, 2] = rows[8:16]
        fill(y, 1)
        fill(y, 2)
    inner(0)
    inner(7)

    def update(y, carry):
        for z in range(2):
            outer = slabs[pl.ds(y, 3), 3 * z].reshape(3 * SLAB, NX)
            gates = acc[y, 128 * z : 128 * z + 128, :] + dot(side[z], outer)
            turned = jnp.tanh(gates)
            new = 0.5 * (
                (turned[32:64] + 1.0) * cells[y, z] + (turned[0:32] + 1.0) * turned[64:96]
            )
            cells[y, z] = new
            hids[y, z] = (0.5 * (turned[96:128] + 1.0) * jnp.tanh(new)).astype(BF16)
        return carry

    def fill_outer(y, carry):
        fill(y, 0)
        fill(y, 3)
        return carry

    for z in range(2):
        copies["side", z].wait_recv()
        to = 3 - 3 * z
        rows = vz_r[z].astype(F32)
        for t in range(2):
            vel_t[t, 0:24] = rows[24 * t : 24 * t + 24]
            for y in range(8):
                vels[y + 1, to, 0:3, 128 * t : 128 * t + 128] = vel_t[t, pl.ds(y, 3, stride=8), :]
    for part, ys, rows in (
        (0, (0, 3), (0, 1)), (1, (3, 5), (1, 3)), (2, (5, 8), (3, 6)), (3, (8, 10), (6, 8))
    ):
        for z in range(2):
            copies["plane", z, part].wait_recv()
            if part in (0, 3):
                k = 1 - part // 3
                copies["corner", k, z, 0].wait_recv()
                copies["corner", k, z, 1].wait_recv()
                rows_c = vc_r[2 * k + z].astype(F32)
                vels[9 - 9 * k, 3 - 3 * z] = jnp.concatenate([rows_c[0:8], rows_c[8:16]], 1)
        for y in range(*ys):
            fill_outer(y, 0)
        for y in range(*rows):
            update(y, 0)

    for y in range(8):
        for z in range(2):
            advanced = vels[y + 1, z + 1, 0:3, :] + dot(dec_ref[...], hids[y, z])
            for t in range(2):
                at = 16 * y + 8 * z
                moved[t, at : at + 3, :] = advanced[:, 128 * t : 128 * t + 128]
    for c in range(3):
        for z in range(2):
            for t in range(2):
                start = 16 * c + 8 * z
                u_ref[start : start + 8, 128 * t : 128 * t + 128] = moved[
                    t, pl.ds(8 * z + c, 8, stride=16), :
                ]

    def store_states():
        def turn(y, carry):
            for z in range(2):
                for t in range(2):
                    rows = pl.ds(y * 4 + 2 * t + z, 32, stride=32)
                    lanes = slice(128 * t, 128 * t + 128)
                    cell_v[rows, :] = cells[y, z, :, lanes]
                    hid_f[rows, :] = hids[y, z, :, lanes].astype(F32)
            return carry

        lax.fori_loop(0, 8, turn, 0)
        hid_in[...] = hid_f[...].astype(BF16)
        for copy in copies.values():
            copy.wait_send()

    for load in loads[6:]:
        load.wait()
    project(u_ref, tables, vel_next, send, recv, tile_send_sem, tile_recv_sem, store_states)


def hand_on_kernel(*refs):
    sources, results, sem = refs[:3], refs[3:6], refs[6]
    copies = [pltpu.make_async_copy(a, b, sem.at[i]) for i, (a, b) in enumerate(zip(sources, results))]
    for copy in copies:
        copy.start()
    for copy in copies:
        copy.wait()


def to_rows(array):
    c = array.shape[0]
    return array.reshape(c, 8, 2, 2, 128).transpose(0, 1, 3, 2, 4).reshape(c * 32, 128)


def from_rows(array):
    c = array.shape[0] // 32
    return array.reshape(c, 8, 2, 2, 128).transpose(0, 1, 3, 2, 4).reshape(c, 8, 2, 256)


def per_device(velocity, hidden, cell, gate_weight, gate_bias, decoder):
    anywhere = pl.BlockSpec(memory_space=pl.ANY)
    vmem = pl.BlockSpec(memory_space=pltpu.VMEM)
    tables = [halves(t) for t in (*x_tables(), *y_tables(), *z_tables())]
    results = (
        jax.ShapeDtypeStruct((1024, 128), BF16),
        jax.ShapeDtypeStruct((1024, 128), F32),
        jax.ShapeDtypeStruct((96, 128), F32),
    )
    outs = pl.pallas_call(
        step_kernel,
        out_shape=tuple(pltpu.VMEM(r.shape, r.dtype) for r in results),
        in_specs=[anywhere] * 12,
        out_specs=(vmem,) * 3,
        scratch_shapes=[
            *(pltpu.VMEM(t.shape, BF16) for t in tables),
            pltpu.VMEM((1, 128), F32),
            pltpu.VMEM((3, 32), BF16),
            pltpu.VMEM((48, 256), F32),
            pltpu.VMEM((1024, 128), F32),
            pltpu.VMEM((256, 128), F32),
            pltpu.VMEM((945, 128), BF16),
            pltpu.VMEM((952, 128), F32),
            pltpu.VMEM((128, 128), F32),
            pltpu.VMEM((256, 768), BF16),
            pltpu.VMEM((2, 128, 384), BF16),
            pltpu.VMEM((10, 4, SLAB, NX), BF16),
            pltpu.VMEM((10, 4, 8, NX), F32),
            pltpu.VMEM((2, 64, 128), F32),
            pltpu.VMEM((2, 48, 128), BF16),
            pltpu.VMEM((2, 48, 128), BF16),
            pltpu.VMEM((2, 16, NX), BF16),
            pltpu.VMEM((2, 16, NX), BF16),
            pltpu.VMEM((4, 16, 128), BF16),
            pltpu.VMEM((4, 16, 128), BF16),
            pltpu.VMEM((8, 256, 256), F32),
            pltpu.VMEM((8, 2, 32, NX), F32),
            pltpu.VMEM((8, 2, 32, NX), BF16),
            pltpu.VMEM((2, 128, 128), F32),
            pltpu.VMEM((4, RANKS, 8, 128), F32),
            pltpu.VMEM((4, RANKS, 8, 128), F32),
            pltpu.SemaphoreType.DMA((12,)),
            pltpu.SemaphoreType.DMA((8, 5)),
            pltpu.SemaphoreType.DMA((8, 5)),
            pltpu.SemaphoreType.DMA((4,)),
            pltpu.SemaphoreType.DMA((4,)),
        ],
        compiler_params=pltpu.CompilerParams(
            collective_id=0, has_side_effects=True, vmem_limit_bytes=58 * 1024 * 1024
        ),
    )(
        to_rows(velocity),
        to_rows(hidden),
        to_rows(cell),
        gate_weight.T,
        gate_bias.reshape(1, 128),
        decoder,
        *(jnp.asarray(t) for t in tables),
    )
    outs = pl.pallas_call(
        hand_on_kernel,
        out_shape=results,
        in_specs=[vmem] * 3,
        out_specs=(anywhere,) * 3,
        scratch_shapes=[pltpu.SemaphoreType.DMA((3,))],
        compiler_params=pltpu.CompilerParams(vmem_limit_bytes=1024 * 1024),
    )(*outs)
    return tuple(from_rows(out) for out in outs)


def solution(mesh):
    field = P(None, "gy", "gz", None)
    return jax.shard_map(
        per_device,
        mesh=mesh,
        in_specs=(field, field, field, P(), P(), P()),
        out_specs=(field, field, field),
        check_vma=False,
    )
```
